32 devices in a mesh: dp: 4 (over y, x), zero: 8 (over z, core).
Axes of the slice: x: 2, y: 2, z: 4, core: 2. Of those that a mesh axis runs over, the one named last changes fastest.
Arguments:
- feats: bfloat16 [4096, 6144], P(('dp', 'zero')), may hold values from -6 to 6
- short_filter: bfloat16 [7, 6144], P(None, 'zero'), may hold values from -2 to 2
- medium_filter: float32 [128, 128], replicated, may hold values from -0.5 to 0.5
- doc_ids: int32 [32, 128], P(('dp', 'zero')), may hold values from 0 to 2, never falling along the last dimension, each value on 1 to 112 neighbouring positions
- counts: int32 [32], P(('dp', 'zero')), may hold values from 64 to 128
- plan: int32 [32], P(('dp', 'zero')), may hold values from 0 to 3, as said below
- cotangent: bfloat16 [4096, 2048], P(('dp', 'zero')), may hold values from -6 to 6
Outputs:
- mixed: bfloat16 [4096, 2048], P(('dp', 'zero'))
- feats_grad: bfloat16 [4096, 6144], P(('dp', 'zero'))
- short_grad: float32 [7, 6144], P(None, 'zero')
- medium_grad: float32 [128, 128], replicated
The draws below stay inside these ranges and needn't reach their ends.
Inputs may be any that keep to these rules, and one draw needn't show every extreme that they name: `plan`: every data rank is named by some tile.
All inputs are finite; a program needn't handle non-finite values.
Results may differ from the reference program's by a relative error of at most 0.0058.
Values may be sent and summed in bfloat16 or wider, within the bound.
A program may use at most 64 MiB of HBM per device.

```python
import math
import jax
import jax.numpy as jnp
import numpy as np
from jax import lax

GROUPS = 128
SHORT = 7
MED = 128
TILE = 128
CH = 2048
TILES = 32
TOKENS = 4096
RANKS = 4
N_DP = 4


def draw_plan(key, part):
    draw_one, draw_two = jax.random.split(key)
    first_pick = jax.random.randint(draw_one, (TILES,), 0, RANKS)
    second_pick = jax.random.randint(draw_two, (TILES,), 0, RANKS)
    chosen = jnp.minimum(first_pick, second_pick)
    return chosen.at[:RANKS].set(jnp.arange(RANKS, dtype=jnp.int32)).astype(jnp.int32)


def set_ends(array, stream_key, least, top_value):
    shape = array.shape
    index_at = [jax.random.randint(jax.random.fold_in(stream_key, axis), (), 0, shape[axis]) for axis in range(len(shape))]
    array = array.at[tuple(index_at)].set(least)
    longest = shape.index(max(shape))
    index_at[longest] = (index_at[longest] + 1) % shape[longest]
    return array.at[tuple(index_at)].set(top_value)


def shard_levels(rng, dims, shards, smallest, top_value):
    level, own = 1.0, jax.random.fold_in(rng, 6)
    for dim, parts in shards:
        steps = jnp.exp(jax.random.uniform(jax.random.fold_in(own, dim), (parts,), jnp.float32, smallest / len(shards), top_value / len(shards)))
        level = level * jnp.repeat(steps, dims[dim] // parts).reshape([-1 if axis == dim else 1 for axis in range(len(dims))])
    return level


def profile(amount, total, bound, lean):
    portions = [(1 << 20) // math.isqrt(standing ** lean) + 1 for standing in range(2, amount + 1)]
    spare, given = total - bound - (amount - 1), [1] * (amount - 1)
    while spare > 0:
        free = [i for i in range(amount - 1) if given[i] < bound]
        pool, budget = sum([portions[i] for i in free]), spare
        for i in free:
            addition = min(bound - given[i], max(1, budget * portions[i] // pool), spare)
            given[i] = given[i] + addition
            spare = spare - addition
    return np.array([bound] + given)


def ragged(rng, number_of, total, reach, lean):
    if number_of == 2:
        one = jax.random.randint(rng, (), max(1, total - reach), min(reach, total - 1) + 1)
        return jnp.stack([one, total - one])
    sizes = jnp.asarray(profile(number_of, total, reach, lean), jnp.int32)
    couples = (number_of - 1) // 2
    donor, taker = sizes[1:1 + 2 * couples:2], sizes[2:2 + 2 * couples:2]
    slack = jnp.minimum(donor - 1, reach - taker)
    passed = jax.random.randint(jax.random.fold_in(rng, 1), (couples,), 0, 1 << 20) % (slack + 1)
    sizes = sizes.at[1:1 + 2 * couples:2].set(donor - passed).at[2:2 + 2 * couples:2].set(taker + passed)
    return sizes[jax.random.permutation(jax.random.fold_in(rng, 2), number_of)]


def scatter_about(own_key, dims, spread, reach, shards=(), held_as=jnp.bfloat16):
    entries = spread * jax.random.normal(own_key, dims, jnp.float32)
    if shards:
        entries = entries * shard_levels(own_key, dims, shards, -0.22, 0.18)
    return jnp.clip(entries, -reach, reach).astype(held_as)


def setup_inputs(seed: int = 0) -> dict:
    arg_keys = jax.random.split(jax.random.key(seed), 8)
    feats = scatter_about(arg_keys[0], (TOKENS, 3 * CH), 1.0, 6.0, ((0, 32),))
    short_filter = scatter_about(arg_keys[1], (SHORT, 3 * CH), SHORT ** -0.5, 2.0, ((1, 8),))
    medium_filter = scatter_about(arg_keys[2], (MED, GROUPS), MED ** -0.5, 0.5, (), jnp.float32)
    doc_ids = jax.vmap(lambda own: jnp.searchsorted(jnp.cumsum(ragged(own, 3, TILE, TILE - TILE // 8, 0)), jnp.arange(TILE), side="right"))(jax.random.split(arg_keys[3], TILES)).reshape((TILES, TILE)).astype(jnp.int32)
    counts = set_ends(jax.random.randint(arg_keys[4], (TILES,), TILE // 2, TILE + 1), jax.random.fold_in(arg_keys[4], 1), TILE // 2, TILE).astype(jnp.int32)
    plan = draw_plan(jax.random.fold_in(arg_keys[7], 71), 0)
    cotangent = scatter_about(arg_keys[6], (TOKENS, CH), 1.0, 6.0, ((0, 32),))
    return dict(feats=feats, short_filter=short_filter, medium_filter=medium_filter, doc_ids=doc_ids, counts=counts, plan=plan, cotangent=cotangent)


def toeplitz_blocks(filters):
    groups, length = filters.shape
    padded = jnp.concatenate([filters[:, ::-1], jnp.zeros((groups, length), filters.dtype)], 1)
    repeated = jnp.broadcast_to(padded[:, None, :], (groups, length, 2 * length))
    flattened = repeated.reshape(groups, 2 * length * length)[:, : length * (2 * length - 1)]
    return flattened.reshape(groups, length, 2 * length - 1)[:, :, length - 1:]


def diagonal_sums(crossed):
    groups, length, _ = crossed.shape
    padded = jnp.concatenate([crossed[:, :, ::-1], jnp.zeros_like(crossed)], 2)
    flattened = padded.reshape(groups, 2 * length * length)[:, : length * (2 * length - 1)]
    skewed = flattened.reshape(groups, length, 2 * length - 1)[:, :, length - 1:]
    return jnp.sum(skewed, 1)


def shift_down(values, offset):
    return jnp.concatenate([jnp.zeros((offset, values.shape[1]), values.dtype), values[: values.shape[0] - offset]], 0)


def shift_up(values, offset):
    return jnp.concatenate([values[offset:], jnp.zeros((offset, values.shape[1]), values.dtype)], 0)


def short_masks(segment, length):
    masks = []
    for offset in range(SHORT):
        earlier = jnp.concatenate([jnp.full((offset,), -1, jnp.int32), segment[: length - offset]])
        masks.append((earlier == segment).astype(jnp.float32)[:, None])
    return masks


def tile_terms(inputs, blocks, filters, width):
    feats, segment, count, weighting, cotangent = inputs
    length = feats.shape[0]
    groups = blocks.shape[0]
    masks = short_masks(segment, length)
    position = jnp.arange(length)
    living = (position < count).astype(jnp.float32)[:, None]
    convolved = jnp.zeros(feats.shape, jnp.float32)
    for offset in range(SHORT):
        convolved = convolved + filters[offset] * shift_down(feats, offset).astype(jnp.float32) * masks[offset]
    query_part = convolved[:, :width]
    key_part = convolved[:, width:2 * width]
    value_part = convolved[:, 2 * width:]
    product = (key_part * value_part).astype(jnp.bfloat16)
    product_groups = product.reshape(length, groups, width // groups).astype(jnp.float32)
    same_doc = (segment[:, None] == segment[None, :]) & (position[:, None] >= position[None, :])
    toeplitz = jnp.where(same_doc[None], blocks, jnp.zeros_like(blocks)).astype(jnp.float32)
    long_conv = jnp.einsum("gts,sgc->tgc", toeplitz, product_groups).reshape(length, width)
    mixed = (living * query_part * long_conv).astype(jnp.bfloat16)
    grad_out = cotangent.astype(jnp.float32) * living * weighting
    grad_query = grad_out * long_conv
    grad_long = (grad_out * query_part).astype(jnp.bfloat16)
    grad_groups = grad_long.reshape(length, groups, width // groups).astype(jnp.float32)
    grad_product = jnp.einsum("gts,tgc->sgc", toeplitz, grad_groups).reshape(length, width)
    crossed = jnp.einsum("tgc,sgc->gts", grad_groups, product_groups)
    crossed = jnp.where(same_doc[None], crossed, jnp.zeros_like(crossed))
    medium_part = diagonal_sums(crossed)
    grad_short = jnp.concatenate([grad_query, grad_product * value_part, grad_product * key_part], 1)
    grad_feats = jnp.zeros(feats.shape, jnp.float32)
    short_rows = []
    for offset in range(SHORT):
        masked = grad_short * masks[offset]
        grad_feats = grad_feats + filters[offset] * shift_up(masked, offset)
        short_rows.append(jnp.sum(masked * shift_down(feats, offset).astype(jnp.float32), 0))
    return mixed, grad_feats.astype(jnp.bfloat16), jnp.stack(short_rows), medium_part


def reference(feats, short_filter, medium_filter, doc_ids, counts, plan, cotangent):
    tile_count = counts.shape[0]
    width = cotangent.shape[1]
    member = (plan[:, None] == jnp.arange(N_DP)[None, :]).astype(jnp.float32)
    totals = jnp.sum(member * counts.astype(jnp.float32)[:, None], 0)
    weighting = TILE * tile_count / (N_DP * jnp.sum(member * totals[None, :], 1))
    blocks = toeplitz_blocks(medium_filter.astype(jnp.bfloat16).T)
    filters = short_filter.astype(jnp.float32)

    def per_tile(inputs):
        return tile_terms(inputs, blocks, filters, width)

    results = lax.map(per_tile, (feats.reshape(tile_count, TILE, 3 * width), doc_ids, counts, weighting,
                                 cotangent.reshape(tile_count, TILE, width)))
    mixed = results[0].reshape(tile_count * TILE, width)
    feats_grad = results[1].reshape(tile_count * TILE, 3 * width)
    return mixed, feats_grad, jnp.sum(results[2], 0), jnp.sum(results[3], 0).T
```

```python
import functools

import jax
import jax.numpy as jnp
from jax import lax
from jax.experimental import pallas as pl
from jax.experimental.pallas import tpu as pltpu
from jax.sharding import PartitionSpec as P

F32 = jnp.float32
BF16 = jnp.bfloat16
MESH = pl.DeviceIdType.MESH
LANES = 128
WIDE = 256


def greet(replicas, zeros):
    barrier = pltpu.get_barrier_semaphore()
    mine, row = lax.axis_index("zero"), lax.axis_index("dp")
    for step in range(1, zeros):
        peer = lax.rem(mine + step, zeros)
        pl.semaphore_signal(barrier, inc=1, device_id={"zero": peer}, device_id_type=MESH)
    for step in range(1, replicas):
        peer = lax.rem(row + step, replicas)
        pl.semaphore_signal(barrier, inc=1, device_id={"dp": peer}, device_id_type=MESH)
    return barrier


def spread(axis, count, source, slots, send, recv):
    me = lax.axis_index(axis)
    copies = []
    for step in range(1, count):
        peer = lax.rem(me + step, count)
        copy = pltpu.make_async_remote_copy(
            src_ref=source(peer),
            dst_ref=slots.at[me],
            send_sem=send.at[step],
            recv_sem=recv.at[step],
            device_id={axis: peer},
            device_id_type=MESH,
        )
        copy.start()
        copies.append(copy)
    return copies


def gather_kernel(
    replicas, zeros, scale, short, filt, counts, plan, filters, weight,
    rows, stage, slots, tally, tallies, send, recv, tsend, trecv,
):
    barrier = greet(replicas, zeros)
    mine, row = lax.axis_index("zero"), lax.axis_index("dp")
    cw = filt.shape[1]
    half = cw // 2
    lane = lax.broadcasted_iota(jnp.int32, (1, cw), 1)
    rows[0:short, :] = filt[...].astype(F32)
    rows[short:8, :] = jnp.where(lane == plan[0], counts[0].astype(F32), 0.0)
    stage[...] = jnp.concatenate([rows[:, :half], rows[:, half:]], 0).astype(BF16)
    slots[mine] = stage[...]
    pl.semaphore_wait(barrier, zeros + replicas - 2)
    copies = spread("zero", zeros, lambda peer: stage, slots, send, recv)
    for copy in copies:
        copy.wait()
    total = slots[0].astype(F32)[short : short + 1, :LANES]
    for z in range(1, zeros):
        total = total + slots[z].astype(F32)[short : short + 1, :LANES]
    tally[...] = jnp.broadcast_to(total, (8, LANES))
    tallies[row] = tally[...]
    copies = spread("dp", replicas, lambda peer: tally, tallies, tsend, trecv)
    for z in range(zeros):
        block = slots[z].astype(F32)
        filters[:, z * cw : z * cw + half] = block[0:8]
        filters[:, z * cw + half : (z + 1) * cw] = block[8:16]
    for copy in copies:
        copy.wait()
    total = tallies[0]
    for r in range(1, replicas):
        total = total + tallies[r]
    lane8 = lax.broadcasted_iota(jnp.int32, (8, LANES), 1)
    own = jnp.sum(jnp.where(lane8 == plan[0], total, 0.0), 1, keepdims=True)
    weight[...] = jnp.broadcast_to(scale / own, (8, LANES))


def reduce_kernel(
    replicas, zeros, short, shorts, medium, short_out, medium_out,
    pack, slots, part, parts, share, shares, send, recv, psend, precv, msend, mrecv,
):
    barrier = greet(replicas, zeros)
    mine, row = lax.axis_index("zero"), lax.axis_index("dp")
    cw = shorts.shape[1] // zeros
    half = cw // 2
    depth = medium.shape[0] // zeros
    for z in range(zeros):
        one = shorts[:, z * cw : z * cw + half]
        two = shorts[:, z * cw + half : (z + 1) * cw]
        pack[z, :, :half] = jnp.concatenate([one, two], 0).astype(BF16)
        pack[z, :, half:] = medium[z * depth : (z + 1) * depth, :].astype(BF16)
    slots[mine] = pack[mine]
    pl.semaphore_wait(barrier, zeros + replicas - 2)
    copies = spread("zero", zeros, lambda peer: pack.at[peer], slots, send, recv)
    for copy in copies:
        copy.wait()
    total = slots[0].astype(F32)
    for z in range(1, zeros):
        total = total + slots[z].astype(F32)
    part[...] = total
    parts[row] = total
    copies = spread("dp", replicas, lambda peer: part, parts, psend, precv)
    for copy in copies:
        copy.wait()
    total = parts[0]
    for r in range(1, replicas):
        total = total + parts[r]
    share[...] = total[:, half:]
    shares[mine] = total[:, half:]
    copies = spread("zero", zeros, lambda peer: share, shares, msend, mrecv)
    short_out[:, :half] = total[0:short, :half]
    short_out[:, half:] = total[8 : 8 + short, :half]
    for copy in copies:
        copy.wait()
    for z in range(zeros):
        medium_out[z * depth : (z + 1) * depth, :] = shares[z]


def dot(a, b):
    return jnp.dot(a, b, preferred_element_type=F32)


def block_kernel(
    short, gsize, counts, doc, taps, weight, cot, fq, fk, fv, wq, wk, wv,
    mixed, grads, shorts, medium,
    down, up, causal, causal_t, causal_r, flip, tap_rows, tap_back, living, med,
):
    step = pl.program_id(0)
    length = cot.shape[0]
    width = grads.shape[1] // 3
    per = LANES // gsize
    square = (length, length)

    @pl.when(step == 0)
    def _():
        r = lax.broadcasted_iota(jnp.int32, square, 0)
        c = lax.broadcasted_iota(jnp.int32, square, 1)
        across = jnp.broadcast_to(doc[...].astype(F32), square)
        same = (across == across.T).astype(F32)
        for j in range(short):
            down[j] = jnp.where(r - c == j, same, 0.0).astype(BF16)
            up[j] = jnp.where(c - r == j, same, 0.0).astype(BF16)
        low = jnp.where(r >= c, same, 0.0)
        causal[...] = low
        causal_t[...] = jnp.where(c >= r, same, 0.0)
        turned = (r + c == length - 1).astype(BF16)
        flip[...] = turned
        causal_r[...] = dot(low.astype(BF16), turned)
        rounded = taps[...].astype(BF16).astype(F32).T
        tap_rows[...] = rounded
        back = (lax.rem(r + c, length) == 0).astype(BF16)
        tap_back[...] = dot(rounded.astype(BF16), back)
        living[...] = (r < counts[0]).astype(F32)

    def convolve(feats, filt):
        x = feats[...]
        total = filt[0:1, :] * x.astype(F32)
        for j in range(1, short):
            total = total + filt[j : j + 1, :] * dot(down[j], x)
        return total

    query, key, value = convolve(fq, wq), convolve(fk, wk), convolve(fv, wv)
    lane = lax.broadcasted_iota(jnp.int32, (1, LANES), 1)
    picks = [(lane // gsize == i).astype(BF16) for i in range(per)]
    weighting = weight[0:1, :]
    pieces = [[], [], []]
    for h in range(cot.shape[1] // LANES):
        cols = slice(h * LANES, (h + 1) * LANES)
        q, k, v = query[:, cols], key[:, cols], value[:, cols]
        product = (k * v).astype(BF16)
        first = step * (cot.shape[1] // gsize) + h * per
        forward, backward = [], []
        for i in range(per):
            row = jnp.broadcast_to(tap_back[pl.ds(first + i, 1), :], square)
            row = pltpu.roll(row, 0, 1, stride=1, stride_axis=0)
            forward.append((row * causal[...]).astype(BF16))
            row = jnp.broadcast_to(tap_rows[pl.ds(first + i, 1), :], square)
            row = pltpu.roll(row, 0, 1, stride=1, stride_axis=0)
            backward.append((row * causal_t[...]).astype(BF16))
        long_conv = dot(
            jnp.concatenate(forward, 1), jnp.concatenate([product * m for m in picks], 0)
        )
        alive = living[...]
        mixed[:, cols] = (alive * q * long_conv).astype(BF16)
        grad_out = cot[:, cols].astype(F32) * alive * weighting
        grad_long = (grad_out * q).astype(BF16)
        chosen = jnp.concatenate([grad_long * m for m in picks], 0)
        grad_product = dot(jnp.concatenate(backward, 1), chosen)
        turned = dot(flip[...], product).astype(BF16)
        crossed = lax.dot_general(
            chosen, turned, (((1,), (1,)), ((), ())), preferred_element_type=F32
        )
        for i in range(per):
            part = crossed[i * length : (i + 1) * length] * causal_r[...]
            part = pltpu.roll(part, 1, 1, stride=1, stride_axis=0)
            med[pl.ds(first + i, 1), :] = jnp.sum(part, 0, keepdims=True)
        pieces[0].append((grad_out * long_conv).astype(BF16))
        pieces[1].append((grad_product * v).astype(BF16))
        pieces[2].append((grad_product * k).astype(BF16))

    span = cot.shape[1]
    for n, (feats, filt) in enumerate(((fq, wq), (fk, wk), (fv, wv))):
        grad = jnp.concatenate(pieces[n], 1)
        x = feats[...].astype(F32)
        where = pl.ds(pl.multiple_of(n * width + step * span, LANES), span)
        total = None
        for j in range(short):
            moved = grad.astype(F32) if j == 0 else dot(up[j], grad)
            term = filt[j : j + 1, :] * moved
            total = term if total is None else total + term
            shorts[j : j + 1, where] = jnp.sum(moved * x, 0, keepdims=True)
        shorts[short:8, where] = jnp.zeros((8 - short, span), F32)
        grads[:, where] = total.astype(BF16)

    @pl.when(step == pl.num_programs(0) - 1)
    def _():
        medium[...] = med[...].T


def run_block(feats, filters, medium_filter, doc_ids, counts, weight, cotangent, short):
    length, width = cotangent.shape
    taps_count, groups = medium_filter.shape
    steps = width // WIDE
    square = (length, length)

    def part(n):
        return pl.BlockSpec((length, WIDE), lambda i, n=n: (0, n * steps + i))

    def part8(n):
        return pl.BlockSpec((8, WIDE), lambda i, n=n: (0, n * steps + i))

    def whole(shape):
        return pl.BlockSpec(shape, lambda i: (0, 0))

    return pl.pallas_call(
        functools.partial(block_kernel, short, width // groups),
        grid=(steps,),
        in_specs=[
            pl.BlockSpec(memory_space=pltpu.SMEM),
            whole((1, length)),
            whole((taps_count, groups)),
            whole((8, LANES)),
            part(0), part(0), part(1), part(2), part8(0), part8(1), part8(2),
        ],
        out_specs=[part(0), whole(feats.shape), whole((8, 3 * width)), whole((taps_count, groups))],
        out_shape=[
            jax.ShapeDtypeStruct((length, width), BF16),
            jax.ShapeDtypeStruct(feats.shape, BF16),
            jax.ShapeDtypeStruct((8, 3 * width), F32),
            jax.ShapeDtypeStruct((taps_count, groups), F32),
        ],
        scratch_shapes=[
            pltpu.VMEM((short, length, length), BF16),
            pltpu.VMEM((short, length, length), BF16),
            pltpu.VMEM(square, F32),
            pltpu.VMEM(square, F32),
            pltpu.VMEM(square, F32),
            pltpu.VMEM(square, BF16),
            pltpu.VMEM((groups, taps_count), F32),
            pltpu.VMEM((groups, taps_count), F32),
            pltpu.VMEM((length, LANES), F32),
            pltpu.VMEM((groups, taps_count), F32),
        ],
        compiler_params=pltpu.CompilerParams(vmem_limit_bytes=40 * 1024 * 1024),
        name="conv_block",
    )(counts, doc_ids, medium_filter, weight, cotangent, feats, feats, feats, filters, filters, filters)


def vmem(count):
    return [pl.BlockSpec(memory_space=pltpu.VMEM)] * count


def run_gather(short_filter, counts, plan, replicas, zeros, scale):
    short, cw = short_filter.shape
    half = cw // 2
    return pl.pallas_call(
        functools.partial(gather_kernel, replicas, zeros, scale, short),
        in_specs=vmem(1) + [pl.BlockSpec(memory_space=pltpu.SMEM)] * 2,
        out_specs=vmem(2),
        out_shape=[
            jax.ShapeDtypeStruct((8, cw * zeros), F32),
            jax.ShapeDtypeStruct((8, LANES), F32),
        ],
        scratch_shapes=[
            pltpu.VMEM((8, cw), F32),
            pltpu.VMEM((16, half), BF16),
            pltpu.VMEM((zeros, 16, half), BF16),
            pltpu.VMEM((8, LANES), F32),
            pltpu.VMEM((replicas, 8, LANES), F32),
            pltpu.SemaphoreType.DMA((zeros,)),
            pltpu.SemaphoreType.DMA((zeros,)),
            pltpu.SemaphoreType.DMA((replicas,)),
            pltpu.SemaphoreType.DMA((replicas,)),
        ],
        compiler_params=pltpu.CompilerParams(collective_id=0, has_side_effects=True),
        name="gather_filters",
    )(short_filter, counts, plan)


def run_reduce(shorts, medium, replicas, zeros, short):
    cw = shorts.shape[1] // zeros
    half = cw // 2
    taps_count, groups = medium.shape
    depth = taps_count // zeros
    return pl.pallas_call(
        functools.partial(reduce_kernel, replicas, zeros, short),
        in_specs=vmem(2),
        out_specs=vmem(2),
        out_shape=[
            jax.ShapeDtypeStruct((short, cw), F32),
            jax.ShapeDtypeStruct((taps_count, groups), F32),
        ],
        scratch_shapes=[
            pltpu.VMEM((zeros, 16, half + groups), BF16),
            pltpu.VMEM((zeros, 16, half + groups), BF16),
            pltpu.VMEM((16, half + groups), F32),
            pltpu.VMEM((replicas, 16, half + groups), F32),
            pltpu.VMEM((depth, groups), F32),
            pltpu.VMEM((zeros, depth, groups), F32),
            pltpu.SemaphoreType.DMA((zeros,)),
            pltpu.SemaphoreType.DMA((zeros,)),
            pltpu.SemaphoreType.DMA((replicas,)),
            pltpu.SemaphoreType.DMA((replicas,)),
            pltpu.SemaphoreType.DMA((zeros,)),
            pltpu.SemaphoreType.DMA((zeros,)),
        ],
        compiler_params=pltpu.CompilerParams(collective_id=1, has_side_effects=True),
        name="reduce_filters",
    )(shorts, medium)


def shards(feats, short_filter, medium_filter, doc_ids, counts, plan, cotangent):
    replicas = lax.axis_size("dp")
    zeros = lax.axis_size("zero")
    length = feats.shape[0]
    short, cw = short_filter.shape
    scale = float(length * replicas * zeros / replicas)
    packed = cw % WIDE == 0 and medium_filter.shape[0] == 16 * zeros
    if packed:
        filters, weight = run_gather(short_filter, counts, plan, replicas, zeros, scale)
    else:
        member = (plan[0] == jnp.arange(replicas)).astype(F32)
        totals = lax.psum(member * counts[0].astype(F32), ("dp", "zero"))
        weight = jnp.broadcast_to(scale / jnp.sum(member * totals), (8, LANES))
        filters = lax.all_gather(short_filter, "zero", axis=1, tiled=True).astype(F32)
        filters = jnp.pad(filters, ((0, 8 - short), (0, 0)))
    mixed, grads, shorts, medium = run_block(
        feats, filters, medium_filter, doc_ids, counts, weight, cotangent, short
    )
    if packed:
        short_grad, medium_grad = run_reduce(shorts, medium, replicas, zeros, short)
    else:
        own = lax.psum(shorts[:short], "dp")
        own = own.reshape(short, zeros, cw).transpose(1, 0, 2)
        short_grad = lax.psum_scatter(own, "zero", scatter_dimension=0, tiled=True)[0]
        medium_grad = lax.psum(medium, ("dp", "zero"))
    return mixed, grads, short_grad, medium_grad


def solution(mesh):
    in_specs = (
        P(("dp", "zero"), None),
        P(None, "zero"),
        P(),
        P(("dp", "zero"), None),
        P(("dp", "zero")),
        P(("dp", "zero")),
        P(("dp", "zero"), None),
    )
    out_specs = (P(("dp", "zero"), None), P(("dp", "zero"), None), P(None, "zero"), P())
    return jax.shard_map(shards, mesh=mesh, in_specs=in_specs, out_specs=out_specs, check_vma=False)
```

```python
import functools

import jax
import jax.numpy as jnp
from jax import lax
from jax.experimental import pallas as pl
from jax.experimental.pallas import tpu as pltpu
from jax.sharding import PartitionSpec as P

F32 = jnp.float32
BF16 = jnp.bfloat16
MESH = pl.DeviceIdType.MESH
LANES = 128
WIDE = 256


def greet(replicas, zeros):
    barrier = pltpu.get_barrier_semaphore()
    mine, row = lax.axis_index("zero"), lax.axis_index("dp")
    for step in range(1, zeros):
        peer = lax.rem(mine + step, zeros)
        pl.semaphore_signal(barrier, inc=1, device_id={"zero": peer}, device_id_type=MESH)
    for step in range(1, replicas):
        peer = lax.rem(row + step, replicas)
        pl.semaphore_signal(barrier, inc=1, device_id={"dp": peer}, device_id_type=MESH)
    return barrier


def spread(axis, count, source, slots, send, recv):
    me = lax.axis_index(axis)
    copies = []
    for step in range(1, count):
        peer = lax.rem(me + step, count)
        copy = pltpu.make_async_remote_copy(
            src_ref=source(peer),
            dst_ref=slots.at[me],
            send_sem=send.at[step],
            recv_sem=recv.at[step],
            device_id={axis: peer},
            device_id_type=MESH,
        )
        copy.start()
        copies.append(copy)
    return copies


def dot(a, b):
    return jnp.dot(a, b, preferred_element_type=F32)


def block_kernel(
    short, gsize, counts, doc, taps, weight, cot, fq, fk, fv, wq, wk, wv,
    mixed, grads, shorts, medium,
    down, up, causal, causal_t, causal_r, flip, tap_rows, tap_back, living, med,
):
    step = pl.program_id(0)
    length = cot.shape[0]
    width = grads.shape[1] // 3
    per = LANES // gsize
    square = (length, length)

    @pl.when(step == 0)
    def _():
        r = lax.broadcasted_iota(jnp.int32, square, 0)
        c = lax.broadcasted_iota(jnp.int32, square, 1)
        across = jnp.broadcast_to(doc[...].astype(F32), square)
        same = (across == across.T).astype(F32)
        for j in range(short):
            down[j] = jnp.where(r - c == j, same, 0.0).astype(BF16)
            up[j] = jnp.where(c - r == j, same, 0.0).astype(BF16)
        low = jnp.where(r >= c, same, 0.0)
        causal[...] = low
        causal_t[...] = jnp.where(c >= r, same, 0.0)
        turned = (r + c == length - 1).astype(BF16)
        flip[...] = turned
        causal_r[...] = dot(low.astype(BF16), turned)
        rounded = taps[...].astype(BF16).astype(F32).T
        tap_rows[...] = rounded
        back = (lax.rem(r + c, length) == 0).astype(BF16)
        tap_back[...] = dot(rounded.astype(BF16), back)
        living[...] = (r < counts[0]).astype(F32)

    def convolve(feats, filt):
        x = feats[...]
        total = filt[0:1, :] * x.astype(F32)
        for j in range(1, short):
            total = total + filt[j : j + 1, :] * dot(down[j], x)
        return total

    query, key, value = convolve(fq, wq), convolve(fk, wk), convolve(fv, wv)
    lane = lax.broadcasted_iota(jnp.int32, (1, LANES), 1)
    picks = [(lane // gsize == i).astype(BF16) for i in range(per)]
    weighting = weight[0:1, :]
    pieces = [[], [], []]
    for h in range(cot.shape[1] // LANES):
        cols = slice(h * LANES, (h + 1) * LANES)
        q, k, v = query[:, cols], key[:, cols], value[:, cols]
        product = (k * v).astype(BF16)
        first = step * (cot.shape[1] // gsize) + h * per
        forward, backward = [], []
        for i in range(per):
            row = jnp.broadcast_to(tap_back[pl.ds(first + i, 1), :], square)
            row = pltpu.roll(row, 0, 1, stride=1, stride_axis=0)
            forward.append((row * causal[...]).astype(BF16))
            row = jnp.broadcast_to(tap_rows[pl.ds(first + i, 1), :], square)
            row = pltpu.roll(row, 0, 1, stride=1, stride_axis=0)
            backward.append((row * causal_t[...]).astype(BF16))
        long_conv = dot(
            jnp.concatenate(forward, 1), jnp.concatenate([product * m for m in picks], 0)
        )
        alive = living[...]
        mixed[:, cols] = (alive * q * long_conv).astype(BF16)
        grad_out = cot[:, cols].astype(F32) * alive * weighting
        grad_long = (grad_out * q).astype(BF16)
        chosen = jnp.concatenate([grad_long * m for m in picks], 0)
        grad_product = dot(jnp.concatenate(backward, 1), chosen)
        turned = dot(flip[...], product).astype(BF16)
        crossed = lax.dot_general(
            chosen, turned, (((1,), (1,)), ((), ())), preferred_element_type=F32
        )
        for i in range(per):
            part = crossed[i * length : (i + 1) * length] * causal_r[...]
            part = pltpu.roll(part, 1, 1, stride=1, stride_axis=0)
            med[pl.ds(first + i, 1), :] = jnp.sum(part, 0, keepdims=True)
        pieces[0].append((grad_out * long_conv).astype(BF16))
        pieces[1].append((grad_product * v).astype(BF16))
        pieces[2].append((grad_product * k).astype(BF16))

    span = cot.shape[1]
    for n, (feats, filt) in enumerate(((fq, wq), (fk, wk), (fv, wv))):
        grad = jnp.concatenate(pieces[n], 1)
        x = feats[...].astype(F32)
        where = pl.ds(pl.multiple_of(n * width + step * span, LANES), span)
        total = None
        for j in range(short):
            moved = grad.astype(F32) if j == 0 else dot(up[j], grad)
            term = filt[j : j + 1, :] * moved
            total = term if total is None else total + term
            shorts[j : j + 1, where] = jnp.sum(moved * x, 0, keepdims=True)
        shorts[short:8, where] = jnp.zeros((8 - short, span), F32)
        grads[:, where] = total.astype(BF16)

    @pl.when(step == pl.num_programs(0) - 1)
    def _():
        medium[...] = med[...].T


def run_block(feats, filters, medium_filter, doc_ids, counts, weight, cotangent, short):
    length, width = cotangent.shape
    taps_count, groups = medium_filter.shape
    steps = width // WIDE
    square = (length, length)

    def part(n):
        return pl.BlockSpec((length, WIDE), lambda i, n=n: (0, n * steps + i))

    def part8(n):
        return pl.BlockSpec((8, WIDE), lambda i, n=n: (0, n * steps + i))

    def whole(shape):
        return pl.BlockSpec(shape, lambda i: (0, 0))

    return pl.pallas_call(
        functools.partial(block_kernel, short, width // groups),
        grid=(steps,),
        in_specs=[
            pl.BlockSpec(memory_space=pltpu.SMEM),
            whole((1, length)),
            whole((taps_count, groups)),
            whole((8, LANES)),
            part(0), part(0), part(1), part(2), part8(0), part8(1), part8(2),
        ],
        out_specs=[part(0), whole(feats.shape), whole((8, 3 * width)), whole((taps_count, groups))],
        out_shape=[
            jax.ShapeDtypeStruct((length, width), BF16),
            jax.ShapeDtypeStruct(feats.shape, BF16),
            jax.ShapeDtypeStruct((8, 3 * width), F32),
            jax.ShapeDtypeStruct((taps_count, groups), F32),
        ],
        scratch_shapes=[
            pltpu.VMEM((short, length, length), BF16),
            pltpu.VMEM((short, length, length), BF16),
            pltpu.VMEM(square, F32),
            pltpu.VMEM(square, F32),
            pltpu.VMEM(square, F32),
            pltpu.VMEM(square, BF16),
            pltpu.VMEM((groups, taps_count), F32),
            pltpu.VMEM((groups, taps_count), F32),
            pltpu.VMEM((length, LANES), F32),
            pltpu.VMEM((groups, taps_count), F32),
        ],
        compiler_params=pltpu.CompilerParams(vmem_limit_bytes=40 * 1024 * 1024),
        name="conv_block",
    )(counts, doc_ids, medium_filter, weight, cotangent, feats, feats, feats, filters, filters, filters)


def toeplitz(row, square):
    return pltpu.roll(jnp.broadcast_to(row, square), 0, 1, stride=1, stride_axis=0)


def whole_kernel(
    replicas, zeros, scale, short, gsize,
    counts, plan, doc, taps, filt, feats_hbm, cot_hbm,
    mixed, grads, short_out, medium_out,
    feats, cot, loaded, rows, stage, slots, tally, tallies, filters,
    down, up_cat, causal, causal_t, causal_r, flip, tap_rows, tap_back, living, med,
    forward, backward, grad_short,
    mpack, mslots, mpart, mparts, share, shares, spack, sslots, spart, sparts,
    send, recv, tsend, trecv, m1s, m1r, m2s, m2r, m3s, m3r, s1s, s1r, s2s, s2r,
):
    barrier = greet(replicas, zeros)
    mine, place = lax.axis_index("zero"), lax.axis_index("dp")
    length = cot.shape[0]
    width = cot.shape[1]
    cw = filt.shape[1]
    half = cw // 2
    per = LANES // gsize
    square = (length, length)
    load_feats = pltpu.make_async_copy(feats_hbm, feats, loaded.at[0])
    load_cot = pltpu.make_async_copy(cot_hbm, cot, loaded.at[1])
    load_feats.start()
    load_cot.start()

    lane = lax.broadcasted_iota(jnp.int32, (1, cw), 1)
    rows[0:short, :] = filt[...].astype(F32)
    rows[short:8, :] = jnp.where(lane == plan[0], counts[0].astype(F32), 0.0)
    staged = jnp.concatenate([rows[:, :half], rows[:, half:]], 0).astype(BF16)
    stage[...] = staged
    slots[mine] = staged
    pl.semaphore_wait(barrier, zeros + replicas - 2)
    gathering = spread("zero", zeros, lambda peer: stage, slots, send, recv)

    r = lax.broadcasted_iota(jnp.int32, square, 0)
    c = lax.broadcasted_iota(jnp.int32, square, 1)
    across = jnp.broadcast_to(doc[...].astype(F32), square)
    same = (across == across.T).astype(F32)
    for j in range(short):
        down[j] = jnp.where(r - c == j, same, 0.0).astype(BF16)
        up_cat[:, j * length : (j + 1) * length] = jnp.where(c - r == j, same, 0.0).astype(BF16)
    low = jnp.where(r >= c, same, 0.0)
    causal[...] = low
    causal_t[...] = jnp.where(c >= r, same, 0.0)
    turn = (r + c == length - 1).astype(BF16)
    flip[...] = turn
    causal_r[...] = dot(low.astype(BF16), turn)
    rounded = taps[...].astype(BF16).astype(F32).T
    tap_rows[...] = rounded
    back = (lax.rem(r + c, length) == 0).astype(BF16)
    tap_back[...] = dot(rounded.astype(BF16), back)
    living[...] = (r < counts[0]).astype(F32)

    def build(block, carry):
        back8 = tap_back[pl.ds(pl.multiple_of(block * per, per), per), :]
        rows8 = tap_rows[pl.ds(pl.multiple_of(block * per, per), per), :]
        for i in range(per):
            at = slice(i * length, (i + 1) * length)
            one = toeplitz(back8[i : i + 1], square)
            forward[block, :, at] = (one * causal[...]).astype(BF16)
            two = toeplitz(rows8[i : i + 1], square)
            backward[block, :, at] = (two * causal_t[...]).astype(BF16)
        return carry

    lax.fori_loop(0, width // LANES, build, 0)

    for copy in gathering:
        copy.wait()
    total = slots[0].astype(F32)[short : short + 1, :LANES]
    for z in range(1, zeros):
        total = total + slots[z].astype(F32)[short : short + 1, :LANES]
    tally[...] = jnp.broadcast_to(total, (8, LANES))
    tallies[place] = jnp.broadcast_to(total, (8, LANES))
    counting = spread("dp", replicas, lambda peer: tally, tallies, tsend, trecv)
    for z in range(zeros):
        block = slots[z].astype(F32)
        filters[:, z * cw : z * cw + half] = block[0:8]
        filters[:, z * cw + half : (z + 1) * cw] = block[8:16]
    load_feats.wait()
    load_cot.wait()

    group = lax.broadcasted_iota(jnp.int32, (1, LANES), 1) // gsize
    picks = [(group == i).astype(BF16) for i in range(per)]

    def blocks(step, carry):
        def convolve(n):
            where = pl.ds(pl.multiple_of(n * width + step * WIDE, LANES), WIDE)
            x = feats[:, where]
            taps7 = filters[:, where]
            total = taps7[0:1] * x.astype(F32)
            for j in range(1, short):
                total = total + taps7[j : j + 1] * dot(down[j], x)
            return total

        query, key, value = convolve(0), convolve(1), convolve(2)
        for h in range(WIDE // LANES):
            cols = slice(h * LANES, (h + 1) * LANES)
            q, k, v = query[:, cols], key[:, cols], value[:, cols]
            begin = pl.multiple_of(step * WIDE + h * LANES, LANES)
            here = pl.ds(begin, LANES)
            product = (k * v).astype(BF16)
            block = step * (WIDE // LANES) + h
            long_conv = dot(forward[block], jnp.concatenate([product * m for m in picks], 0))
            alive = living[...]
            mixed[:, here] = (alive * q * long_conv).astype(BF16)
            grad_out = cot[:, here].astype(F32) * alive
            grad_long = (grad_out * q).astype(BF16)
            chosen = jnp.concatenate([grad_long * m for m in picks], 0)
            grad_product = dot(backward[block], chosen)
            turned = dot(flip[...], product).astype(BF16)
            crossed = lax.dot_general(
                chosen, turned, (((1,), (1,)), ((), ())), preferred_element_type=F32
            )
            for i in range(per):
                part = crossed[i * length : (i + 1) * length] * causal_r[...]
                part = pltpu.roll(part, 1, 1, stride=1, stride_axis=0)
                med[pl.ds(block * per + i, 1), :] = jnp.sum(part, 0, keepdims=True)
            grad_short[:, here] = (grad_out * long_conv).astype(BF16)
            there = pl.ds(pl.multiple_of(begin + width, LANES), LANES)
            grad_short[:, there] = (grad_product * v).astype(BF16)
            there = pl.ds(pl.multiple_of(begin + 2 * width, LANES), LANES)
            grad_short[:, there] = (grad_product * k).astype(BF16)
        return carry

    lax.fori_loop(0, width // WIDE, blocks, 0)

    for copy in counting:
        copy.wait()
    total = tallies[0]
    for p in range(1, replicas):
        total = total + tallies[p]
    lane8 = lax.broadcasted_iota(jnp.int32, (8, LANES), 1)
    own = jnp.sum(jnp.where(lane8 == plan[0], total, 0.0), 1, keepdims=True)
    weight = (scale / own)[0:1]

    depth = taps.shape[0] // zeros
    medium = med[...].T * weight
    for z in range(zeros):
        mpack[z] = medium[z * depth : (z + 1) * depth].astype(BF16)
    mslots[mine] = mpack[mine]
    medium_one = spread("zero", zeros, lambda peer: mpack.at[peer], mslots, m1s, m1r)

    def short_chunk(owner):
        sums = []
        for s in range(cw // WIDE):
            where = pl.ds(pl.multiple_of(owner * cw + s * WIDE, LANES), WIDE)
            x = feats[:, where]
            grad = grad_short[:, where].astype(F32)
            lines = [jnp.sum(grad * x.astype(F32), 0, keepdims=True)]
            for j in range(1, short):
                lines.append(jnp.sum(grad * dot(down[j], x), 0, keepdims=True))
            lines.append(jnp.zeros((8 - short, WIDE), F32))
            sums.append(jnp.concatenate(lines, 0))
        both = jnp.concatenate(sums, 1) * weight
        return jnp.concatenate([both[:, :half], both[:, half:]], 0).astype(BF16)

    def short_copy(step):
        peer = lax.rem(mine + step, zeros)
        return pltpu.make_async_remote_copy(
            src_ref=spack.at[peer],
            dst_ref=sslots.at[mine],
            send_sem=s1s.at[step],
            recv_sem=s1r.at[step],
            device_id={"zero": peer},
            device_id_type=MESH,
        )

    def send_short(step, carry):
        peer = lax.rem(mine + step, zeros)
        spack[peer] = short_chunk(peer)
        short_copy(step).start()
        return carry

    lax.fori_loop(1, zeros, send_short, 0)
    sslots[mine] = short_chunk(mine)

    for copy in medium_one:
        copy.wait()
    total = mslots[0].astype(F32)
    for z in range(1, zeros):
        total = total + mslots[z].astype(F32)
    mpart[...] = total
    mparts[place] = total
    medium_two = spread("dp", replicas, lambda peer: mpart, mparts, m2s, m2r)

    def feats_chunk(index, carry):
        where = pl.ds(pl.multiple_of(index * WIDE, LANES), WIDE)
        grad = grad_short[:, where]
        taps7 = filters[:, where].astype(BF16)
        scaled = jnp.concatenate([grad * taps7[j : j + 1] for j in range(short)], 0)
        grads[:, where] = (dot(up_cat[...], scaled) * weight).astype(BF16)
        return carry

    pieces = 3 * width // WIDE
    lax.fori_loop(0, pieces // 2, feats_chunk, 0)

    for step in range(1, zeros):
        short_copy(step).wait()
    total = sslots[0].astype(F32)
    for z in range(1, zeros):
        total = total + sslots[z].astype(F32)
    spart[...] = total
    sparts[place] = total
    short_two = spread("dp", replicas, lambda peer: spart, sparts, s2s, s2r)
    for copy in medium_two:
        copy.wait()
    total = mparts[0]
    for p in range(1, replicas):
        total = total + mparts[p]
    share[...] = total
    shares[mine] = total
    medium_three = spread("zero", zeros, lambda peer: share, shares, m3s, m3r)

    lax.fori_loop(pieces // 2, pieces, feats_chunk, 0)

    for copy in short_two:
        copy.wait()
    total = sparts[0]
    for p in range(1, replicas):
        total = total + sparts[p]
    short_out[:, :half] = total[0:short]
    short_out[:, half:] = total[8 : 8 + short]
    for copy in medium_three:
        copy.wait()
    for z in range(zeros):
        medium_out[z * depth : (z + 1) * depth, :] = shares[z]


def run_whole(feats, short_filter, medium_filter, doc_ids, counts, plan, cotangent, replicas, zeros, scale):
    length, width = cotangent.shape
    short, cw = short_filter.shape
    half = cw // 2
    taps_count, groups = medium_filter.shape
    depth = taps_count // zeros
    square = (length, length)
    gsize = width // groups
    in_vmem = pl.BlockSpec(memory_space=pltpu.VMEM)
    in_smem = pl.BlockSpec(memory_space=pltpu.SMEM)
    anywhere = pl.BlockSpec(memory_space=pl.ANY)
    stacked = (width // LANES, length, LANES // gsize * length)
    along_zero, along_dp = pltpu.SemaphoreType.DMA((zeros,)), pltpu.SemaphoreType.DMA((replicas,))
    return pl.pallas_call(
        functools.partial(whole_kernel, replicas, zeros, scale, short, gsize),
        in_specs=[in_smem, in_smem, in_vmem, in_vmem, in_vmem, anywhere, anywhere],
        out_specs=[in_vmem] * 4,
        out_shape=[
            jax.ShapeDtypeStruct((length, width), BF16),
            jax.ShapeDtypeStruct(feats.shape, BF16),
            jax.ShapeDtypeStruct((short, cw), F32),
            jax.ShapeDtypeStruct((taps_count, groups), F32),
        ],
        scratch_shapes=[
            pltpu.VMEM(feats.shape, BF16),
            pltpu.VMEM((length, width), BF16),
            pltpu.SemaphoreType.DMA((2,)),
            pltpu.VMEM((8, cw), F32),
            pltpu.VMEM((16, half), BF16),
            pltpu.VMEM((zeros, 16, half), BF16),
            pltpu.VMEM((8, LANES), F32),
            pltpu.VMEM((replicas, 8, LANES), F32),
            pltpu.VMEM((8, 3 * width), F32),
            pltpu.VMEM((short, length, length), BF16),
            pltpu.VMEM((length, short * length), BF16),
            pltpu.VMEM(square, F32),
            pltpu.VMEM(square, F32),
            pltpu.VMEM(square, F32),
            pltpu.VMEM(square, BF16),
            pltpu.VMEM((groups, taps_count), F32),
            pltpu.VMEM((groups, taps_count), F32),
            pltpu.VMEM((length, LANES), F32),
            pltpu.VMEM((groups, taps_count), F32),
            pltpu.VMEM(stacked, BF16),
            pltpu.VMEM(stacked, BF16),
            pltpu.VMEM(feats.shape, BF16),
            pltpu.VMEM((zeros, depth, groups), BF16),
            pltpu.VMEM((zeros, depth, groups), BF16),
            pltpu.VMEM((depth, groups), F32),
            pltpu.VMEM((replicas, depth, groups), F32),
            pltpu.VMEM((depth, groups), F32),
            pltpu.VMEM((zeros, depth, groups), F32),
            pltpu.VMEM((zeros, 16, half), BF16),
            pltpu.VMEM((zeros, 16, half), BF16),
            pltpu.VMEM((16, half), F32),
            pltpu.VMEM((replicas, 16, half), F32),
            along_zero, along_zero, along_dp, along_dp,
            along_zero, along_zero, along_dp, along_dp, along_zero, along_zero,
            along_zero, along_zero, along_dp, along_dp,
        ],
        compiler_params=pltpu.CompilerParams(
            collective_id=0, has_side_effects=True, vmem_limit_bytes=56 * 1024 * 1024
        ),
        name="whole_block",
    )(counts, plan, doc_ids, medium_filter, short_filter, feats, cotangent)


def hand_kernel(count, *refs):
    sources, targets, done = refs[:count], refs[count : 2 * count], refs[2 * count]
    copies = []
    for n in range(count):
        rows = sources[n].shape[0]
        cuts = 4 if rows % 64 == 0 else 1
        for cut in range(cuts):
            part = pl.ds(cut * rows // cuts, rows // cuts)
            source, target = sources[n].at[part], targets[n].at[part]
            copies.append(pltpu.make_async_copy(source, target, done.at[len(copies)]))
    for copy in copies:
        copy.start()
    for copy in copies:
        copy.wait()


def hand_over(arrays):
    anywhere = pl.BlockSpec(memory_space=pl.ANY)
    return pl.pallas_call(
        functools.partial(hand_kernel, len(arrays)),
        in_specs=[anywhere] * len(arrays),
        out_specs=[anywhere] * len(arrays),
        out_shape=[jax.ShapeDtypeStruct(a.shape, a.dtype) for a in arrays],
        scratch_shapes=[pltpu.SemaphoreType.DMA((4 * len(arrays),))],
        compiler_params=pltpu.CompilerParams(vmem_limit_bytes=56 * 1024 * 1024),
        name="hand_over",
    )(*arrays)


def shards(feats, short_filter, medium_filter, doc_ids, counts, plan, cotangent):
    replicas = lax.axis_size("dp")
    zeros = lax.axis_size("zero")
    length = feats.shape[0]
    short, cw = short_filter.shape
    scale = float(length * replicas * zeros / replicas)
    packed = cw % WIDE == 0 and medium_filter.shape[0] == 16 * zeros
    if packed:
        return hand_over(run_whole(
            feats, short_filter, medium_filter, doc_ids, counts, plan, cotangent, replicas, zeros, scale
        ))
    member = (plan[0] == jnp.arange(replicas)).astype(F32)
    totals = lax.psum(member * counts[0].astype(F32), ("dp", "zero"))
    weight = jnp.broadcast_to(scale / jnp.sum(member * totals), (8, LANES))
    filters = lax.all_gather(short_filter, "zero", axis=1, tiled=True).astype(F32)
    filters = jnp.pad(filters, ((0, 8 - short), (0, 0)))
    mixed, grads, shorts, medium = run_block(
        feats, filters, medium_filter, doc_ids, counts, weight, cotangent, short
    )
    own = lax.psum(shorts[:short], "dp")
    own = own.reshape(short, zeros, cw).transpose(1, 0, 2)
    short_grad = lax.psum_scatter(own, "zero", scatter_dimension=0, tiled=True)[0]
    medium_grad = lax.psum(medium, ("dp", "zero"))
    return mixed, grads, short_grad, medium_grad


def solution(mesh):
    in_specs = (
        P(("dp", "zero"), None),
        P(None, "zero"),
        P(),
        P(("dp", "zero"), None),
        P(("dp", "zero")),
        P(("dp", "zero")),
        P(("dp", "zero"), None),
    )
    out_specs = (P(("dp", "zero"), None), P(("dp", "zero"), None), P(None, "zero"), P())
    return jax.shard_map(shards, mesh=mesh, in_specs=in_specs, out_specs=out_specs, check_vma=False)
```

```python
import functools

import jax
import jax.numpy as jnp
from jax import lax
from jax.experimental import pallas as pl
from jax.experimental.pallas import tpu as pltpu
from jax.sharding import PartitionSpec as P

F32 = jnp.float32
BF16 = jnp.bfloat16
MESH = pl.DeviceIdType.MESH
LANES = 128
WIDE = 256


def greet(replicas, zeros):
    barrier = pltpu.get_barrier_semaphore()
    mine, row = lax.axis_index("zero"), lax.axis_index("dp")
    for step in range(1, zeros):
        peer = lax.rem(mine + step, zeros)
        pl.semaphore_signal(barrier, inc=1, device_id={"zero": peer}, device_id_type=MESH)
    for step in range(1, replicas):
        peer = lax.rem(row + step, replicas)
        pl.semaphore_signal(barrier, inc=1, device_id={"dp": peer}, device_id_type=MESH)
    return barrier


def spread(axis, count, source, slots, send, recv):
    me = lax.axis_index(axis)
    copies = []
    for step in range(1, count):
        peer = lax.rem(me + step, count)
        copy = pltpu.make_async_remote_copy(
            src_ref=source(peer),
            dst_ref=slots.at[me],
            send_sem=send.at[step],
            recv_sem=recv.at[step],
            device_id={axis: peer},
            device_id_type=MESH,
        )
        copy.start()
        copies.append(copy)
    return copies


def dot(a, b):
    return jnp.dot(a, b, preferred_element_type=F32)


def block_kernel(
    short, gsize, counts, doc, taps, weight, cot, fq, fk, fv, wq, wk, wv,
    mixed, grads, shorts, medium,
    down, up, causal, causal_t, causal_r, flip, tap_rows, tap_back, living, med,
):
    step = pl.program_id(0)
    length = cot.shape[0]
    width = grads.shape[1] // 3
    per = LANES // gsize
    square = (length, length)

    @pl.when(step == 0)
    def _():
        r = lax.broadcasted_iota(jnp.int32, square, 0)
        c = lax.broadcasted_iota(jnp.int32, square, 1)
        across = jnp.broadcast_to(doc[...].astype(F32), square)
        same = (across == across.T).astype(F32)
        for j in range(short):
            down[j] = jnp.where(r - c == j, same, 0.0).astype(BF16)
            up[j] = jnp.where(c - r == j, same, 0.0).astype(BF16)
        low = jnp.where(r >= c, same, 0.0)
        causal[...] = low
        causal_t[...] = jnp.where(c >= r, same, 0.0)
        turned = (r + c == length - 1).astype(BF16)
        flip[...] = turned
        causal_r[...] = dot(low.astype(BF16), turned)
        rounded = taps[...].astype(BF16).astype(F32).T
        tap_rows[...] = rounded
        back = (lax.rem(r + c, length) == 0).astype(BF16)
        tap_back[...] = dot(rounded.astype(BF16), back)
        living[...] = (r < counts[0]).astype(F32)

    def convolve(feats, filt):
        x = feats[...]
        total = filt[0:1, :] * x.astype(F32)
        for j in range(1, short):
            total = total + filt[j : j + 1, :] * dot(down[j], x)
        return total

    query, key, value = convolve(fq, wq), convolve(fk, wk), convolve(fv, wv)
    lane = lax.broadcasted_iota(jnp.int32, (1, LANES), 1)
    picks = [(lane // gsize == i).astype(BF16) for i in range(per)]
    weighting = weight[0:1, :]
    pieces = [[], [], []]
    for h in range(cot.shape[1] // LANES):
        cols = slice(h * LANES, (h + 1) * LANES)
        q, k, v = query[:, cols], key[:, cols], value[:, cols]
        product = (k * v).astype(BF16)
        first = step * (cot.shape[1] // gsize) + h * per
        forward, backward = [], []
        for i in range(per):
            row = jnp.broadcast_to(tap_back[pl.ds(first + i, 1), :], square)
            row = pltpu.roll(row, 0, 1, stride=1, stride_axis=0)
            forward.append((row * causal[...]).astype(BF16))
            row = jnp.broadcast_to(tap_rows[pl.ds(first + i, 1), :], square)
            row = pltpu.roll(row, 0, 1, stride=1, stride_axis=0)
            backward.append((row * causal_t[...]).astype(BF16))
        long_conv = dot(
            jnp.concatenate(forward, 1), jnp.concatenate([product * m for m in picks], 0)
        )
        alive = living[...]
        mixed[:, cols] = (alive * q * long_conv).astype(BF16)
        grad_out = cot[:, cols].astype(F32) * alive * weighting
        grad_long = (grad_out * q).astype(BF16)
        chosen = jnp.concatenate([grad_long * m for m in picks], 0)
        grad_product = dot(jnp.concatenate(backward, 1), chosen)
        turned = dot(flip[...], product).astype(BF16)
        crossed = lax.dot_general(
            chosen, turned, (((1,), (1,)), ((), ())), preferred_element_type=F32
        )
        for i in range(per):
            part = crossed[i * length : (i + 1) * length] * causal_r[...]
            part = pltpu.roll(part, 1, 1, stride=1, stride_axis=0)
            med[pl.ds(first + i, 1), :] = jnp.sum(part, 0, keepdims=True)
        pieces[0].append((grad_out * long_conv).astype(BF16))
        pieces[1].append((grad_product * v).astype(BF16))
        pieces[2].append((grad_product * k).astype(BF16))

    span = cot.shape[1]
    for n, (feats, filt) in enumerate(((fq, wq), (fk, wk), (fv, wv))):
        grad = jnp.concatenate(pieces[n], 1)
        x = feats[...].astype(F32)
        where = pl.ds(pl.multiple_of(n * width + step * span, LANES), span)
        total = None
        for j in range(short):
            moved = grad.astype(F32) if j == 0 else dot(up[j], grad)
            term = filt[j : j + 1, :] * moved
            total = term if total is None else total + term
            shorts[j : j + 1, where] = jnp.sum(moved * x, 0, keepdims=True)
        shorts[short:8, where] = jnp.zeros((8 - short, span), F32)
        grads[:, where] = total.astype(BF16)

    @pl.when(step == pl.num_programs(0) - 1)
    def _():
        medium[...] = med[...].T


def run_block(feats, filters, medium_filter, doc_ids, counts, weight, cotangent, short):
    length, width = cotangent.shape
    taps_count, groups = medium_filter.shape
    steps = width // WIDE
    square = (length, length)

    def part(n):
        return pl.BlockSpec((length, WIDE), lambda i, n=n: (0, n * steps + i))

    def part8(n):
        return pl.BlockSpec((8, WIDE), lambda i, n=n: (0, n * steps + i))

    def whole(shape):
        return pl.BlockSpec(shape, lambda i: (0, 0))

    return pl.pallas_call(
        functools.partial(block_kernel, short, width // groups),
        grid=(steps,),
        in_specs=[
            pl.BlockSpec(memory_space=pltpu.SMEM),
            whole((1, length)),
            whole((taps_count, groups)),
            whole((8, LANES)),
            part(0), part(0), part(1), part(2), part8(0), part8(1), part8(2),
        ],
        out_specs=[part(0), whole(feats.shape), whole((8, 3 * width)), whole((taps_count, groups))],
        out_shape=[
            jax.ShapeDtypeStruct((length, width), BF16),
            jax.ShapeDtypeStruct(feats.shape, BF16),
            jax.ShapeDtypeStruct((8, 3 * width), F32),
            jax.ShapeDtypeStruct((taps_count, groups), F32),
        ],
        scratch_shapes=[
            pltpu.VMEM((short, length, length), BF16),
            pltpu.VMEM((short, length, length), BF16),
            pltpu.VMEM(square, F32),
            pltpu.VMEM(square, F32),
            pltpu.VMEM(square, F32),
            pltpu.VMEM(square, BF16),
            pltpu.VMEM((groups, taps_count), F32),
            pltpu.VMEM((groups, taps_count), F32),
            pltpu.VMEM((length, LANES), F32),
            pltpu.VMEM((groups, taps_count), F32),
        ],
        compiler_params=pltpu.CompilerParams(vmem_limit_bytes=40 * 1024 * 1024),
        name="conv_block",
    )(counts, doc_ids, medium_filter, weight, cotangent, feats, feats, feats, filters, filters, filters)


def toeplitz(tile, length):
    return jnp.concatenate([pltpu.roll(tile, at, 1) if at else tile for at in range(0, length, 8)], 0)


def whole_kernel(
    replicas, zeros, scale, short, gsize,
    counts, plan, doc, taps, filt, feats_hbm, cot_hbm,
    mixed_hbm, grads_hbm, short_out, medium_out,
    mixed, grads, feats, cot, loaded, rows, stage, slots, tally, tallies, filters,
    down, up_cat, causal, causal_t, causal_r, flip, base_rows, base_back, living, med,
    forward, backward, grad_short,
    mpack, mslots, mpart, mparts, share, shares, spack, sslots, spart, sparts,
    send, recv, tsend, trecv, m1s, m1r, m2s, m2r, m3s, m3r, s1s, s1r, s2s, s2r,
):
    barrier = greet(replicas, zeros)
    mine, place = lax.axis_index("zero"), lax.axis_index("dp")
    length = cot.shape[0]
    width = cot.shape[1]
    cw = filt.shape[1]
    half = cw // 2
    per = LANES // gsize
    square = (length, length)
    load_feats = pltpu.make_async_copy(feats_hbm, feats, loaded.at[0])
    load_cot = pltpu.make_async_copy(cot_hbm, cot, loaded.at[1])
    load_feats.start()
    load_cot.start()

    lane = lax.broadcasted_iota(jnp.int32, (1, cw), 1)
    rows[0:short, :] = filt[...].astype(F32)
    rows[short:8, :] = jnp.where(lane == plan[0], counts[0].astype(F32), 0.0)
    staged = jnp.concatenate([rows[:, :half], rows[:, half:]], 0).astype(BF16)
    stage[...] = staged
    slots[mine] = staged
    pl.semaphore_wait(barrier, zeros + replicas - 2)
    gathering = spread("zero", zeros, lambda peer: stage, slots, send, recv)

    r = lax.broadcasted_iota(jnp.int32, square, 0)
    c = lax.broadcasted_iota(jnp.int32, square, 1)
    across = jnp.broadcast_to(doc[...].astype(F32), square)
    same = (across == across.T).astype(F32)
    for j in range(short):
        down[j] = jnp.where(r - c == j, same, 0.0).astype(BF16)
        up_cat[:, j * length : (j + 1) * length] = jnp.where(c - r == j, same, 0.0).astype(BF16)
    low = jnp.where(r >= c, same, 0.0)
    causal[...] = low
    causal_t[...] = jnp.where(c >= r, same, 0.0)
    turn = (r + c == length - 1).astype(BF16)
    flip[...] = turn
    causal_r[...] = dot(low.astype(BF16), turn)
    rounded = taps[...].astype(BF16).astype(F32).T
    tap_rows = rounded
    back = (lax.rem(r + c, length) == 0).astype(BF16)
    tap_back = dot(rounded.astype(BF16), back)
    living[...] = (r < counts[0]).astype(F32)

    for a in range(8):
        lines = pl.ds(a, taps.shape[1], stride=8)
        base_back[lines, :] = pltpu.roll(tap_back, a, 1)
        base_rows[lines, :] = pltpu.roll(tap_rows, a, 1)

    def build(block, carry):
        for i in range(per):
            at = slice(i * length, (i + 1) * length)
            tile = pl.ds(pl.multiple_of((block * per + i) * 8, 8), 8)
            one = toeplitz(base_back[tile, :], length)
            forward[block, :, at] = (one * causal[...]).astype(BF16)
            two = toeplitz(base_rows[tile, :], length)
            backward[block, :, at] = (two * causal_t[...]).astype(BF16)
        return carry

    lax.fori_loop(0, width // LANES, build, 0)

    for copy in gathering:
        copy.wait()
    total = slots[0].astype(F32)[short : short + 1, :LANES]
    for z in range(1, zeros):
        total = total + slots[z].astype(F32)[short : short + 1, :LANES]
    tally[...] = jnp.broadcast_to(total, (8, LANES))
    tallies[place] = jnp.broadcast_to(total, (8, LANES))
    counting = spread("dp", replicas, lambda peer: tally, tallies, tsend, trecv)
    for z in range(zeros):
        block = slots[z].astype(F32)
        filters[:, z * cw : z * cw + half] = block[0:8]
        filters[:, z * cw + half : (z + 1) * cw] = block[8:16]
    load_feats.wait()
    load_cot.wait()

    group = lax.broadcasted_iota(jnp.int32, (1, LANES), 1) // gsize
    picks = [(group == i).astype(BF16) for i in range(per)]

    def blocks(step, carry):
        def convolve(n):
            where = pl.ds(pl.multiple_of(n * width + step * WIDE, LANES), WIDE)
            x = feats[:, where]
            taps7 = filters[:, where]
            total = taps7[0:1] * x.astype(F32)
            for j in range(1, short):
                total = total + taps7[j : j + 1] * dot(down[j], x)
            return total

        query, key, value = convolve(0), convolve(1), convolve(2)
        for h in range(WIDE // LANES):
            cols = slice(h * LANES, (h + 1) * LANES)
            q, k, v = query[:, cols], key[:, cols], value[:, cols]
            begin = pl.multiple_of(step * WIDE + h * LANES, LANES)
            here = pl.ds(begin, LANES)
            product = (k * v).astype(BF16)
            block = step * (WIDE // LANES) + h
            long_conv = dot(forward[block], jnp.concatenate([product * m for m in picks], 0))
            alive = living[...]
            mixed[:, here] = (alive * q * long_conv).astype(BF16)
            grad_out = cot[:, here].astype(F32) * alive
            grad_long = (grad_out * q).astype(BF16)
            chosen = jnp.concatenate([grad_long * m for m in picks], 0)
            grad_product = dot(backward[block], chosen)
            turned = dot(flip[...], product).astype(BF16)
            crossed = lax.dot_general(
                chosen, turned, (((1,), (1,)), ((), ())), preferred_element_type=F32
            )
            for i in range(per):
                part = crossed[i * length : (i + 1) * length] * causal_r[...]
                summed = part[0:8]
                for at in range(8, length, 8):
                    summed = summed + pltpu.roll(part[at : at + 8], at, 1)
                med[pl.ds(pl.multiple_of((block * per + i) * 8, 8), 8), :] = summed
            grad_short[:, here] = (grad_out * long_conv).astype(BF16)
            there = pl.ds(pl.multiple_of(begin + width, LANES), LANES)
            grad_short[:, there] = (grad_product * v).astype(BF16)
            there = pl.ds(pl.multiple_of(begin + 2 * width, LANES), LANES)
            grad_short[:, there] = (grad_product * k).astype(BF16)
        return carry

    lax.fori_loop(0, width // WIDE, blocks, 0)
    save_mixed = pltpu.make_async_copy(mixed, mixed_hbm, loaded.at[2])
    save_mixed.start()

    for copy in counting:
        copy.wait()
    total = tallies[0]
    for p in range(1, replicas):
        total = total + tallies[p]
    lane8 = lax.broadcasted_iota(jnp.int32, (8, LANES), 1)
    own = jnp.sum(jnp.where(lane8 == plan[0], total, 0.0), 1, keepdims=True)
    weight = (scale / own)[0:1]

    depth = taps.shape[0] // zeros
    total = None
    for a in range(8):
        part = pltpu.roll(med[pl.ds(a, taps.shape[1], stride=8), :], a + 1, 1)
        total = part if total is None else total + part
    medium = total.T * weight
    for z in range(zeros):
        mpack[z] = medium[z * depth : (z + 1) * depth].astype(BF16)
    mslots[mine] = mpack[mine]
    medium_one = spread("zero", zeros, lambda peer: mpack.at[peer], mslots, m1s, m1r)

    def short_chunk(owner):
        sums = []
        for s in range(cw // WIDE):
            where = pl.ds(pl.multiple_of(owner * cw + s * WIDE, LANES), WIDE)
            x = feats[:, where]
            grad = grad_short[:, where].astype(F32)
            lines = [jnp.sum(grad * x.astype(F32), 0, keepdims=True)]
            for j in range(1, short):
                lines.append(jnp.sum(grad * dot(down[j], x), 0, keepdims=True))
            lines.append(jnp.zeros((8 - short, WIDE), F32))
            sums.append(jnp.concatenate(lines, 0))
        both = jnp.concatenate(sums, 1) * weight
        return jnp.concatenate([both[:, :half], both[:, half:]], 0).astype(BF16)

    def short_copy(step):
        peer = lax.rem(mine + step, zeros)
        return pltpu.make_async_remote_copy(
            src_ref=spack.at[peer],
            dst_ref=sslots.at[mine],
            send_sem=s1s.at[step],
            recv_sem=s1r.at[step],
            device_id={"zero": peer},
            device_id_type=MESH,
        )

    def send_short(step, carry):
        peer = lax.rem(mine + step, zeros)
        spack[peer] = short_chunk(peer)
        short_copy(step).start()
        return carry

    lax.fori_loop(1, zeros, send_short, 0)
    sslots[mine] = short_chunk(mine)

    for copy in medium_one:
        copy.wait()
    total = mslots[0].astype(F32)
    for z in range(1, zeros):
        total = total + mslots[z].astype(F32)
    mpart[...] = total
    mparts[place] = total
    medium_two = spread("dp", replicas, lambda peer: mpart, mparts, m2s, m2r)

    def feats_chunk(index, carry):
        where = pl.ds(pl.multiple_of(index * WIDE, LANES), WIDE)
        grad = grad_short[:, where]
        taps7 = filters[:, where].astype(BF16)
        scaled = jnp.concatenate([grad * taps7[j : j + 1] for j in range(short)], 0)
        grads[:, where] = (dot(up_cat[...], scaled) * weight).astype(BF16)
        return carry

    pieces = 3 * width // WIDE
    middle = pieces // 2 * WIDE
    lax.fori_loop(0, pieces // 2, feats_chunk, 0)
    cols = slice(0, middle)
    save_one = pltpu.make_async_copy(grads.at[:, cols], grads_hbm.at[:, cols], loaded.at[3])
    save_one.start()

    for step in range(1, zeros):
        short_copy(step).wait()
    total = sslots[0].astype(F32)
    for z in range(1, zeros):
        total = total + sslots[z].astype(F32)
    spart[...] = total
    sparts[place] = total
    short_two = spread("dp", replicas, lambda peer: spart, sparts, s2s, s2r)
    for copy in medium_two:
        copy.wait()
    total = mparts[0]
    for p in range(1, replicas):
        total = total + mparts[p]
    share[...] = total
    shares[mine] = total
    medium_three = spread("zero", zeros, lambda peer: share, shares, m3s, m3r)

    lax.fori_loop(pieces // 2, pieces, feats_chunk, 0)
    cols = slice(middle, 3 * width)
    save_two = pltpu.make_async_copy(grads.at[:, cols], grads_hbm.at[:, cols], loaded.at[4])
    save_two.start()

    for copy in short_two:
        copy.wait()
    total = sparts[0]
    for p in range(1, replicas):
        total = total + sparts[p]
    short_out[:, :half] = total[0:short]
    short_out[:, half:] = total[8 : 8 + short]
    for copy in medium_three:
        copy.wait()
    for z in range(zeros):
        medium_out[z * depth : (z + 1) * depth, :] = shares[z]
    save_mixed.wait()
    save_one.wait()
    save_two.wait()


def run_whole(feats, short_filter, medium_filter, doc_ids, counts, plan, cotangent, replicas, zeros, scale):
    length, width = cotangent.shape
    short, cw = short_filter.shape
    half = cw // 2
    taps_count, groups = medium_filter.shape
    depth = taps_count // zeros
    square = (length, length)
    gsize = width // groups
    in_vmem = pl.BlockSpec(memory_space=pltpu.VMEM)
    in_smem = pl.BlockSpec(memory_space=pltpu.SMEM)
    anywhere = pl.BlockSpec(memory_space=pl.ANY)
    stacked = (width // LANES, length, LANES // gsize * length)
    along_zero, along_dp = pltpu.SemaphoreType.DMA((zeros,)), pltpu.SemaphoreType.DMA((replicas,))
    return pl.pallas_call(
        functools.partial(whole_kernel, replicas, zeros, scale, short, gsize),
        in_specs=[in_smem, in_smem, in_vmem, in_vmem, in_vmem, anywhere, anywhere],
        out_specs=[anywhere, anywhere, in_vmem, in_vmem],
        out_shape=[
            jax.ShapeDtypeStruct((length, width), BF16),
            jax.ShapeDtypeStruct(feats.shape, BF16),
            jax.ShapeDtypeStruct((short, cw), F32),
            jax.ShapeDtypeStruct((taps_count, groups), F32),
        ],
        scratch_shapes=[
            pltpu.VMEM((length, width), BF16),
            pltpu.VMEM(feats.shape, BF16),
            pltpu.VMEM(feats.shape, BF16),
            pltpu.VMEM((length, width), BF16),
            pltpu.SemaphoreType.DMA((5,)),
            pltpu.VMEM((8, cw), F32),
            pltpu.VMEM((16, half), BF16),
            pltpu.VMEM((zeros, 16, half), BF16),
            pltpu.VMEM((8, LANES), F32),
            pltpu.VMEM((replicas, 8, LANES), F32),
            pltpu.VMEM((8, 3 * width), F32),
            pltpu.VMEM((short, length, length), BF16),
            pltpu.VMEM((length, short * length), BF16),
            pltpu.VMEM(square, F32),
            pltpu.VMEM(square, F32),
            pltpu.VMEM(square, F32),
            pltpu.VMEM(square, BF16),
            pltpu.VMEM((8 * groups, taps_count), F32),
            pltpu.VMEM((8 * groups, taps_count), F32),
            pltpu.VMEM((length, LANES), F32),
            pltpu.VMEM((8 * groups, taps_count), F32),
            pltpu.VMEM(stacked, BF16),
            pltpu.VMEM(stacked, BF16),
            pltpu.VMEM(feats.shape, BF16),
            pltpu.VMEM((zeros, depth, groups), BF16),
            pltpu.VMEM((zeros, depth, groups), BF16),
            pltpu.VMEM((depth, groups), F32),
            pltpu.VMEM((replicas, depth, groups), F32),
            pltpu.VMEM((depth, groups), F32),
            pltpu.VMEM((zeros, depth, groups), F32),
            pltpu.VMEM((zeros, 16, half), BF16),
            pltpu.VMEM((zeros, 16, half), BF16),
            pltpu.VMEM((16, half), F32),
            pltpu.VMEM((replicas, 16, half), F32),
            along_zero, along_zero, along_dp, along_dp,
            along_zero, along_zero, along_dp, along_dp, along_zero, along_zero,
            along_zero, along_zero, along_dp, along_dp,
        ],
        compiler_params=pltpu.CompilerParams(
            collective_id=0, has_side_effects=True, vmem_limit_bytes=56 * 1024 * 1024
        ),
        name="whole_block",
    )(counts, plan, doc_ids, medium_filter, short_filter, feats, cotangent)


def hand_kernel(count, *refs):
    for source, target in zip(refs[:count], refs[count:]):
        target[...] = source[...]


def hand_over(arrays):
    length, parts = arrays[0].shape[0], 4
    specs = []
    for a in arrays[:2]:
        specs.append(pl.BlockSpec((length // parts, a.shape[1]), lambda i: (i, 0)))
    for a in arrays[2:]:
        specs.append(pl.BlockSpec(a.shape, lambda i: (0, 0)))
    return pl.pallas_call(
        functools.partial(hand_kernel, len(arrays)),
        grid=(parts,),
        in_specs=specs,
        out_specs=specs,
        out_shape=[jax.ShapeDtypeStruct(a.shape, a.dtype) for a in arrays],
        compiler_params=pltpu.CompilerParams(vmem_limit_bytes=56 * 1024 * 1024),
        name="hand_over",
    )(*arrays)


def shards(feats, short_filter, medium_filter, doc_ids, counts, plan, cotangent):
    replicas = lax.axis_size("dp")
    zeros = lax.axis_size("zero")
    length = feats.shape[0]
    short, cw = short_filter.shape
    scale = float(length * replicas * zeros / replicas)
    packed = cw % WIDE == 0 and medium_filter.shape[0] == 16 * zeros
    if packed:
        return hand_over(run_whole(
            feats, short_filter, medium_filter, doc_ids, counts, plan, cotangent, replicas, zeros, scale
        ))
    member = (plan[0] == jnp.arange(replicas)).astype(F32)
    totals = lax.psum(member * counts[0].astype(F32), ("dp", "zero"))
    weight = jnp.broadcast_to(scale / jnp.sum(member * totals), (8, LANES))
    filters = lax.all_gather(short_filter, "zero", axis=1, tiled=True).astype(F32)
    filters = jnp.pad(filters, ((0, 8 - short), (0, 0)))
    mixed, grads, shorts, medium = run_block(
        feats, filters, medium_filter, doc_ids, counts, weight, cotangent, short
    )
    own = lax.psum(shorts[:short], "dp")
    own = own.reshape(short, zeros, cw).transpose(1, 0, 2)
    short_grad = lax.psum_scatter(own, "zero", scatter_dimension=0, tiled=True)[0]
    medium_grad = lax.psum(medium, ("dp", "zero"))
    return mixed, grads, short_grad, medium_grad


def solution(mesh):
    in_specs = (
        P(("dp", "zero"), None),
        P(None, "zero"),
        P(),
        P(("dp", "zero"), None),
        P(("dp", "zero")),
        P(("dp", "zero")),
        P(("dp", "zero"), None),
    )
    out_specs = (P(("dp", "zero"), None), P(("dp", "zero"), None), P(None, "zero"), P())
    return jax.shard_map(shards, mesh=mesh, in_specs=in_specs, out_specs=out_specs, check_vma=False)
```

```python
import functools

import jax
import jax.numpy as jnp
from jax import lax
from jax.experimental import pallas as pl
from jax.experimental.pallas import tpu as pltpu
from jax.sharding import PartitionSpec as P

F32 = jnp.float32
BF16 = jnp.bfloat16
MESH = pl.DeviceIdType.MESH
LANES = 128
WIDE = 256


def greet(replicas, zeros):
    barrier = pltpu.get_barrier_semaphore()
    mine, row = lax.axis_index("zero"), lax.axis_index("dp")
    for step in range(1, zeros):
        peer = lax.rem(mine + step, zeros)
        pl.semaphore_signal(barrier, inc=1, device_id={"zero": peer}, device_id_type=MESH)
    for step in range(1, replicas):
        peer = lax.rem(row + step, replicas)
        pl.semaphore_signal(barrier, inc=1, device_id={"dp": peer}, device_id_type=MESH)
    return barrier


def spread(axis, count, source, slots, send, recv):
    me = lax.axis_index(axis)
    copies = []
    for step in range(1, count):
        peer = lax.rem(me + step, count)
        copy = pltpu.make_async_remote_copy(
            src_ref=source(peer),
            dst_ref=slots.at[me],
            send_sem=send.at[step],
            recv_sem=recv.at[step],
            device_id={axis: peer},
            device_id_type=MESH,
        )
        copy.start()
        copies.append(copy)
    return copies


def dot(a, b):
    return jnp.dot(a, b, preferred_element_type=F32)


def block_kernel(
    short, gsize, counts, doc, taps, weight, cot, fq, fk, fv, wq, wk, wv,
    mixed, grads, shorts, medium,
    down, up, causal, causal_t, causal_r, flip, tap_rows, tap_back, living, med,
):
    step = pl.program_id(0)
    length = cot.shape[0]
    width = grads.shape[1] // 3
    per = LANES // gsize
    square = (length, length)

    @pl.when(step == 0)
    def _():
        r = lax.broadcasted_iota(jnp.int32, square, 0)
        c = lax.broadcasted_iota(jnp.int32, square, 1)
        across = jnp.broadcast_to(doc[...].astype(F32), square)
        same = (across == across.T).astype(F32)
        for j in range(short):
            down[j] = jnp.where(r - c == j, same, 0.0).astype(BF16)
            up[j] = jnp.where(c - r == j, same, 0.0).astype(BF16)
        low = jnp.where(r >= c, same, 0.0)
        causal[...] = low
        causal_t[...] = jnp.where(c >= r, same, 0.0)
        turned = (r + c == length - 1).astype(BF16)
        flip[...] = turned
        causal_r[...] = dot(low.astype(BF16), turned)
        rounded = taps[...].astype(BF16).astype(F32).T
        tap_rows[...] = rounded
        back = (lax.rem(r + c, length) == 0).astype(BF16)
        tap_back[...] = dot(rounded.astype(BF16), back)
        living[...] = (r < counts[0]).astype(F32)

    def convolve(feats, filt):
        x = feats[...]
        total = filt[0:1, :] * x.astype(F32)
        for j in range(1, short):
            total = total + filt[j : j + 1, :] * dot(down[j], x)
        return total

    query, key, value = convolve(fq, wq), convolve(fk, wk), convolve(fv, wv)
    lane = lax.broadcasted_iota(jnp.int32, (1, LANES), 1)
    picks = [(lane // gsize == i).astype(BF16) for i in range(per)]
    weighting = weight[0:1, :]
    pieces = [[], [], []]
    for h in range(cot.shape[1] // LANES):
        cols = slice(h * LANES, (h + 1) * LANES)
        q, k, v = query[:, cols], key[:, cols], value[:, cols]
        product = (k * v).astype(BF16)
        first = step * (cot.shape[1] // gsize) + h * per
        forward, backward = [], []
        for i in range(per):
            row = jnp.broadcast_to(tap_back[pl.ds(first + i, 1), :], square)
            row = pltpu.roll(row, 0, 1, stride=1, stride_axis=0)
            forward.append((row * causal[...]).astype(BF16))
            row = jnp.broadcast_to(tap_rows[pl.ds(first + i, 1), :], square)
            row = pltpu.roll(row, 0, 1, stride=1, stride_axis=0)
            backward.append((row * causal_t[...]).astype(BF16))
        long_conv = dot(
            jnp.concatenate(forward, 1), jnp.concatenate([product * m for m in picks], 0)
        )
        alive = living[...]
        mixed[:, cols] = (alive * q * long_conv).astype(BF16)
        grad_out = cot[:, cols].astype(F32) * alive * weighting
        grad_long = (grad_out * q).astype(BF16)
        chosen = jnp.concatenate([grad_long * m for m in picks], 0)
        grad_product = dot(jnp.concatenate(backward, 1), chosen)
        turned = dot(flip[...], product).astype(BF16)
        crossed = lax.dot_general(
            chosen, turned, (((1,), (1,)), ((), ())), preferred_element_type=F32
        )
        for i in range(per):
            part = crossed[i * length : (i + 1) * length] * causal_r[...]
            part = pltpu.roll(part, 1, 1, stride=1, stride_axis=0)
            med[pl.ds(first + i, 1), :] = jnp.sum(part, 0, keepdims=True)
        pieces[0].append((grad_out * long_conv).astype(BF16))
        pieces[1].append((grad_product * v).astype(BF16))
        pieces[2].append((grad_product * k).astype(BF16))

    span = cot.shape[1]
    for n, (feats, filt) in enumerate(((fq, wq), (fk, wk), (fv, wv))):
        grad = jnp.concatenate(pieces[n], 1)
        x = feats[...].astype(F32)
        where = pl.ds(pl.multiple_of(n * width + step * span, LANES), span)
        total = None
        for j in range(short):
            moved = grad.astype(F32) if j == 0 else dot(up[j], grad)
            term = filt[j : j + 1, :] * moved
            total = term if total is None else total + term
            shorts[j : j + 1, where] = jnp.sum(moved * x, 0, keepdims=True)
        shorts[short:8, where] = jnp.zeros((8 - short, span), F32)
        grads[:, where] = total.astype(BF16)

    @pl.when(step == pl.num_programs(0) - 1)
    def _():
        medium[...] = med[...].T


def run_block(feats, filters, medium_filter, doc_ids, counts, weight, cotangent, short):
    length, width = cotangent.shape
    taps_count, groups = medium_filter.shape
    steps = width // WIDE
    square = (length, length)

    def part(n):
        return pl.BlockSpec((length, WIDE), lambda i, n=n: (0, n * steps + i))

    def part8(n):
        return pl.BlockSpec((8, WIDE), lambda i, n=n: (0, n * steps + i))

    def whole(shape):
        return pl.BlockSpec(shape, lambda i: (0, 0))

    return pl.pallas_call(
        functools.partial(block_kernel, short, width // groups),
        grid=(steps,),
        in_specs=[
            pl.BlockSpec(memory_space=pltpu.SMEM),
            whole((1, length)),
            whole((taps_count, groups)),
            whole((8, LANES)),
            part(0), part(0), part(1), part(2), part8(0), part8(1), part8(2),
        ],
        out_specs=[part(0), whole(feats.shape), whole((8, 3 * width)), whole((taps_count, groups))],
        out_shape=[
            jax.ShapeDtypeStruct((length, width), BF16),
            jax.ShapeDtypeStruct(feats.shape, BF16),
            jax.ShapeDtypeStruct((8, 3 * width), F32),
            jax.ShapeDtypeStruct((taps_count, groups), F32),
        ],
        scratch_shapes=[
            pltpu.VMEM((short, length, length), BF16),
            pltpu.VMEM((short, length, length), BF16),
            pltpu.VMEM(square, F32),
            pltpu.VMEM(square, F32),
            pltpu.VMEM(square, F32),
            pltpu.VMEM(square, BF16),
            pltpu.VMEM((groups, taps_count), F32),
            pltpu.VMEM((groups, taps_count), F32),
            pltpu.VMEM((length, LANES), F32),
            pltpu.VMEM((groups, taps_count), F32),
        ],
        compiler_params=pltpu.CompilerParams(vmem_limit_bytes=40 * 1024 * 1024),
        name="conv_block",
    )(counts, doc_ids, medium_filter, weight, cotangent, feats, feats, feats, filters, filters, filters)


def toeplitz(tile, length):
    return jnp.concatenate([pltpu.roll(tile, at, 1) if at else tile for at in range(0, length, 8)], 0)


def whole_kernel(
    replicas, zeros, scale, short, gsize,
    counts, plan, doc, taps, filt, feats_hbm, cot_hbm,
    mixed_hbm, grads_hbm, short_out, medium_out,
    mixed, grads, feats, cot, loaded, rows, stage, slots, tally, tallies, filters,
    down, up_cat, causal, causal_t, causal_r, flip, base_rows, base_back, living, med,
    forward, backward, grad_short, moved, crossing,
    mpack, mslots, mpart, mparts, share, shares, spack, sslots, spart, sparts,
    send, recv, tsend, trecv, m1s, m1r, m2s, m2r, m3s, m3r, s1s, s1r, s2s, s2r,
):
    barrier = greet(replicas, zeros)
    mine, place = lax.axis_index("zero"), lax.axis_index("dp")
    length = cot.shape[0]
    width = cot.shape[1]
    cw = filt.shape[1]
    half = cw // 2
    per = LANES // gsize
    square = (length, length)
    load_feats = pltpu.make_async_copy(feats_hbm, feats, loaded.at[0])
    load_cot = pltpu.make_async_copy(cot_hbm, cot, loaded.at[1])
    load_feats.start()
    load_cot.start()

    lane = lax.broadcasted_iota(jnp.int32, (1, cw), 1)
    rows[0:short, :] = filt[...].astype(F32)
    rows[short:8, :] = jnp.where(lane == plan[0], counts[0].astype(F32), 0.0)
    staged = jnp.concatenate([rows[:, :half], rows[:, half:]], 0).astype(BF16)
    stage[...] = staged
    slots[mine] = staged
    pl.semaphore_wait(barrier, zeros + replicas - 2)
    gathering = spread("zero", zeros, lambda peer: stage, slots, send, recv)

    r = lax.broadcasted_iota(jnp.int32, square, 0)
    c = lax.broadcasted_iota(jnp.int32, square, 1)
    across = jnp.broadcast_to(doc[...].astype(F32), square)
    same = (across == across.T).astype(F32)
    for j in range(short):
        if j:
            down[(j - 1) * length : j * length, :] = jnp.where(r - c == j, same, 0.0).astype(BF16)
        up_cat[:, j * length : (j + 1) * length] = jnp.where(c - r == j, same, 0.0).astype(BF16)
    low = jnp.where(r >= c, same, 0.0)
    causal[...] = low
    causal_t[...] = jnp.where(c >= r, same, 0.0)
    turn = (r + c == length - 1).astype(BF16)
    flip[...] = turn
    causal_r[...] = dot(low.astype(BF16), turn)
    rounded = taps[...].astype(BF16).astype(F32).T
    tap_rows = rounded
    back = (lax.rem(r + c, length) == 0).astype(BF16)
    tap_back = dot(rounded.astype(BF16), back)
    living[...] = (r < counts[0]).astype(F32)

    for a in range(8):
        lines = pl.ds(a, taps.shape[1], stride=8)
        base_back[lines, :] = pltpu.roll(tap_back, a, 1)
        base_rows[lines, :] = pltpu.roll(tap_rows, a, 1)

    def build(block, carry):
        for i in range(per):
            at = slice(i * length, (i + 1) * length)
            tile = pl.ds(pl.multiple_of((block * per + i) * 8, 8), 8)
            one = toeplitz(base_back[tile, :], length)
            forward[block, :, at] = (one * causal[...]).astype(BF16)
            two = toeplitz(base_rows[tile, :], length)
            backward[block, :, at] = (two * causal_t[...]).astype(BF16)
        return carry

    lax.fori_loop(0, width // LANES, build, 0)

    load_feats.wait()

    def shift(index, carry):
        where = pl.ds(pl.multiple_of(index * WIDE, LANES), WIDE)
        moved[:, where] = dot(down[...], feats[:, where]).astype(BF16)
        return carry

    lax.fori_loop(0, 3 * width // WIDE, shift, 0)
    crossing[...] = jnp.zeros_like(crossing)

    for copy in gathering:
        copy.wait()
    total = slots[0].astype(F32)[short : short + 1, :LANES]
    for z in range(1, zeros):
        total = total + slots[z].astype(F32)[short : short + 1, :LANES]
    tally[...] = jnp.broadcast_to(total, (8, LANES))
    tallies[place] = jnp.broadcast_to(total, (8, LANES))
    counting = spread("dp", replicas, lambda peer: tally, tallies, tsend, trecv)
    for z in range(zeros):
        block = slots[z].astype(F32)
        filters[:, z * cw : z * cw + half] = block[0:8]
        filters[:, z * cw + half : (z + 1) * cw] = block[8:16]
    load_cot.wait()

    group = lax.broadcasted_iota(jnp.int32, (1, LANES), 1) // gsize
    picks = [(group == i).astype(BF16) for i in range(per)]

    def blocks(step, carry):
        def convolve(n):
            where = pl.ds(pl.multiple_of(n * width + step * WIDE, LANES), WIDE)
            x = feats[:, where]
            taps7 = filters[:, where]
            total = taps7[0:1] * x.astype(F32)
            for j in range(1, short):
                at = slice((j - 1) * length, j * length)
                total = total + taps7[j : j + 1] * moved[at, where].astype(F32)
            return total

        query, key, value = convolve(0), convolve(1), convolve(2)
        for h in range(WIDE // LANES):
            cols = slice(h * LANES, (h + 1) * LANES)
            q, k, v = query[:, cols], key[:, cols], value[:, cols]
            begin = pl.multiple_of(step * WIDE + h * LANES, LANES)
            here = pl.ds(begin, LANES)
            product = (k * v).astype(BF16)
            block = step * (WIDE // LANES) + h
            long_conv = dot(forward[block], jnp.concatenate([product * m for m in picks], 0))
            alive = living[...]
            mixed[:, here] = (alive * q * long_conv).astype(BF16)
            grad_out = cot[:, here].astype(F32) * alive
            grad_long = (grad_out * q).astype(BF16)
            chosen = jnp.concatenate([grad_long * m for m in picks], 0)
            grad_product = dot(backward[block], chosen)
            turned = lax.dot_general(
                product, flip[...], (((0,), (0,)), ((), ())), preferred_element_type=F32
            ).astype(BF16)
            for i in range(per):
                at = slice(i * gsize, (i + 1) * gsize)
                crossing[h, at, i * length : (i + 1) * length] = turned[at]
            crossed = dot(grad_long, crossing[h])
            for i in range(per):
                part = crossed[:, i * length : (i + 1) * length] * causal_r[...]
                summed = part[0:8]
                for at in range(8, length, 8):
                    summed = summed + pltpu.roll(part[at : at + 8], at, 1)
                med[pl.ds(pl.multiple_of((block * per + i) * 8, 8), 8), :] = summed
            grad_short[:, here] = (grad_out * long_conv).astype(BF16)
            there = pl.ds(pl.multiple_of(begin + width, LANES), LANES)
            grad_short[:, there] = (grad_product * v).astype(BF16)
            there = pl.ds(pl.multiple_of(begin + 2 * width, LANES), LANES)
            grad_short[:, there] = (grad_product * k).astype(BF16)
        return carry

    lax.fori_loop(0, width // WIDE, blocks, 0)
    save_mixed = pltpu.make_async_copy(mixed, mixed_hbm, loaded.at[2])
    save_mixed.start()

    for copy in counting:
        copy.wait()
    total = tallies[0]
    for p in range(1, replicas):
        total = total + tallies[p]
    lane8 = lax.broadcasted_iota(jnp.int32, (8, LANES), 1)
    own = jnp.sum(jnp.where(lane8 == plan[0], total, 0.0), 1, keepdims=True)
    weight = (scale / own)[0:1]

    depth = taps.shape[0] // zeros
    total = None
    for a in range(8):
        part = pltpu.roll(med[pl.ds(a, taps.shape[1], stride=8), :], a + 1, 1)
        total = part if total is None else total + part
    medium = total.T * weight
    for z in range(zeros):
        mpack[z] = medium[z * depth : (z + 1) * depth].astype(BF16)
    mslots[mine] = mpack[mine]
    medium_one = spread("zero", zeros, lambda peer: mpack.at[peer], mslots, m1s, m1r)

    def short_chunk(owner):
        sums = []
        for s in range(cw // WIDE):
            where = pl.ds(pl.multiple_of(owner * cw + s * WIDE, LANES), WIDE)
            x = feats[:, where]
            grad = grad_short[:, where].astype(F32)
            lines = [jnp.sum(grad * x.astype(F32), 0, keepdims=True)]
            for j in range(1, short):
                at = slice((j - 1) * length, j * length)
                lines.append(jnp.sum(grad * moved[at, where].astype(F32), 0, keepdims=True))
            lines.append(jnp.zeros((8 - short, WIDE), F32))
            sums.append(jnp.concatenate(lines, 0))
        both = jnp.concatenate(sums, 1) * weight
        return jnp.concatenate([both[:, :half], both[:, half:]], 0).astype(BF16)

    def short_copy(step):
        peer = lax.rem(mine + step, zeros)
        return pltpu.make_async_remote_copy(
            src_ref=spack.at[peer],
            dst_ref=sslots.at[mine],
            send_sem=s1s.at[step],
            recv_sem=s1r.at[step],
            device_id={"zero": peer},
            device_id_type=MESH,
        )

    def send_short(step, carry):
        peer = lax.rem(mine + step, zeros)
        spack[peer] = short_chunk(peer)
        short_copy(step).start()
        return carry

    lax.fori_loop(1, zeros, send_short, 0)
    sslots[mine] = short_chunk(mine)

    for copy in medium_one:
        copy.wait()
    total = mslots[0].astype(F32)
    for z in range(1, zeros):
        total = total + mslots[z].astype(F32)
    mpart[...] = total
    mparts[place] = total
    medium_two = spread("dp", replicas, lambda peer: mpart, mparts, m2s, m2r)

    def feats_chunk(index, carry):
        where = pl.ds(pl.multiple_of(index * WIDE, LANES), WIDE)
        grad = grad_short[:, where]
        taps7 = filters[:, where].astype(BF16)
        scaled = jnp.concatenate([grad * taps7[j : j + 1] for j in range(short)], 0)
        grads[:, where] = (dot(up_cat[...], scaled) * weight).astype(BF16)
        return carry

    pieces = 3 * width // WIDE
    middle = pieces // 2 * WIDE
    lax.fori_loop(0, pieces // 2, feats_chunk, 0)
    cols = slice(0, middle)
    save_one = pltpu.make_async_copy(grads.at[:, cols], grads_hbm.at[:, cols], loaded.at[3])
    save_one.start()

    for step in range(1, zeros):
        short_copy(step).wait()
    total = sslots[0].astype(F32)
    for z in range(1, zeros):
        total = total + sslots[z].astype(F32)
    spart[...] = total
    sparts[place] = total
    short_two = spread("dp", replicas, lambda peer: spart, sparts, s2s, s2r)
    for copy in medium_two:
        copy.wait()
    total = mparts[0]
    for p in range(1, replicas):
        total = total + mparts[p]
    share[...] = total
    shares[mine] = total
    medium_three = spread("zero", zeros, lambda peer: share, shares, m3s, m3r)

    lax.fori_loop(pieces // 2, pieces, feats_chunk, 0)
    cols = slice(middle, 3 * width)
    save_two = pltpu.make_async_copy(grads.at[:, cols], grads_hbm.at[:, cols], loaded.at[4])
    save_two.start()

    for copy in short_two:
        copy.wait()
    total = sparts[0]
    for p in range(1, replicas):
        total = total + sparts[p]
    short_out[:, :half] = total[0:short]
    short_out[:, half:] = total[8 : 8 + short]
    for copy in medium_three:
        copy.wait()
    for z in range(zeros):
        medium_out[z * depth : (z + 1) * depth, :] = shares[z]
    save_mixed.wait()
    save_one.wait()
    save_two.wait()


def run_whole(feats, short_filter, medium_filter, doc_ids, counts, plan, cotangent, replicas, zeros, scale):
    length, width = cotangent.shape
    short, cw = short_filter.shape
    half = cw // 2
    taps_count, groups = medium_filter.shape
    depth = taps_count // zeros
    square = (length, length)
    gsize = width // groups
    in_vmem = pl.BlockSpec(memory_space=pltpu.VMEM)
    in_smem = pl.BlockSpec(memory_space=pltpu.SMEM)
    anywhere = pl.BlockSpec(memory_space=pl.ANY)
    stacked = (width // LANES, length, LANES // gsize * length)
    along_zero, along_dp = pltpu.SemaphoreType.DMA((zeros,)), pltpu.SemaphoreType.DMA((replicas,))
    return pl.pallas_call(
        functools.partial(whole_kernel, replicas, zeros, scale, short, gsize),
        in_specs=[in_smem, in_smem, in_vmem, in_vmem, in_vmem, anywhere, anywhere],
        out_specs=[anywhere, anywhere, in_vmem, in_vmem],
        out_shape=[
            jax.ShapeDtypeStruct((length, width), BF16),
            jax.ShapeDtypeStruct(feats.shape, BF16),
            jax.ShapeDtypeStruct((short, cw), F32),
            jax.ShapeDtypeStruct((taps_count, groups), F32),
        ],
        scratch_shapes=[
            pltpu.VMEM((length, width), BF16),
            pltpu.VMEM(feats.shape, BF16),
            pltpu.VMEM(feats.shape, BF16),
            pltpu.VMEM((length, width), BF16),
            pltpu.SemaphoreType.DMA((5,)),
            pltpu.VMEM((8, cw), F32),
            pltpu.VMEM((16, half), BF16),
            pltpu.VMEM((zeros, 16, half), BF16),
            pltpu.VMEM((8, LANES), F32),
            pltpu.VMEM((replicas, 8, LANES), F32),
            pltpu.VMEM((8, 3 * width), F32),
            pltpu.VMEM(((short - 1) * length, length), BF16),
            pltpu.VMEM((length, short * length), BF16),
            pltpu.VMEM(square, F32),
            pltpu.VMEM(square, F32),
            pltpu.VMEM(square, F32),
            pltpu.VMEM(square, BF16),
            pltpu.VMEM((8 * groups, taps_count), F32),
            pltpu.VMEM((8 * groups, taps_count), F32),
            pltpu.VMEM((length, LANES), F32),
            pltpu.VMEM((8 * groups, taps_count), F32),
            pltpu.VMEM(stacked, BF16),
            pltpu.VMEM(stacked, BF16),
            pltpu.VMEM(feats.shape, BF16),
            pltpu.VMEM(((short - 1) * length, 3 * width), BF16),
            pltpu.VMEM((WIDE // LANES, LANES, LANES // gsize * length), BF16),
            pltpu.VMEM((zeros, depth, groups), BF16),
            pltpu.VMEM((zeros, depth, groups), BF16),
            pltpu.VMEM((depth, groups), F32),
            pltpu.VMEM((replicas, depth, groups), F32),
            pltpu.VMEM((depth, groups), F32),
            pltpu.VMEM((zeros, depth, groups), F32),
            pltpu.VMEM((zeros, 16, half), BF16),
            pltpu.VMEM((zeros, 16, half), BF16),
            pltpu.VMEM((16, half), F32),
            pltpu.VMEM((replicas, 16, half), F32),
            along_zero, along_zero, along_dp, along_dp,
            along_zero, along_zero, along_dp, along_dp, along_zero, along_zero,
            along_zero, along_zero, along_dp, along_dp,
        ],
        compiler_params=pltpu.CompilerParams(
            collective_id=0, has_side_effects=True, vmem_limit_bytes=56 * 1024 * 1024
        ),
        name="whole_block",
    )(counts, plan, doc_ids, medium_filter, short_filter, feats, cotangent)


def hand_kernel(count, *refs):
    for source, target in zip(refs[:count], refs[count:]):
        target[...] = source[...]


def hand_over(arrays):
    length, parts = arrays[0].shape[0], 4
    specs = []
    for a in arrays[:2]:
        specs.append(pl.BlockSpec((length // parts, a.shape[1]), lambda i: (i, 0)))
    for a in arrays[2:]:
        specs.append(pl.BlockSpec(a.shape, lambda i: (0, 0)))
    return pl.pallas_call(
        functools.partial(hand_kernel, len(arrays)),
        grid=(parts,),
        in_specs=specs,
        out_specs=specs,
        out_shape=[jax.ShapeDtypeStruct(a.shape, a.dtype) for a in arrays],
        compiler_params=pltpu.CompilerParams(vmem_limit_bytes=56 * 1024 * 1024),
        name="hand_over",
    )(*arrays)


def shards(feats, short_filter, medium_filter, doc_ids, counts, plan, cotangent):
    replicas = lax.axis_size("dp")
    zeros = lax.axis_size("zero")
    length = feats.shape[0]
    short, cw = short_filter.shape
    scale = float(length * replicas * zeros / replicas)
    packed = cw % WIDE == 0 and medium_filter.shape[0] == 16 * zeros
    if packed:
        return hand_over(run_whole(
            feats, short_filter, medium_filter, doc_ids, counts, plan, cotangent, replicas, zeros, scale
        ))
    member = (plan[0] == jnp.arange(replicas)).astype(F32)
    totals = lax.psum(member * counts[0].astype(F32), ("dp", "zero"))
    weight = jnp.broadcast_to(scale / jnp.sum(member * totals), (8, LANES))
    filters = lax.all_gather(short_filter, "zero", axis=1, tiled=True).astype(F32)
    filters = jnp.pad(filters, ((0, 8 - short), (0, 0)))
    mixed, grads, shorts, medium = run_block(
        feats, filters, medium_filter, doc_ids, counts, weight, cotangent, short
    )
    own = lax.psum(shorts[:short], "dp")
    own = own.reshape(short, zeros, cw).transpose(1, 0, 2)
    short_grad = lax.psum_scatter(own, "zero", scatter_dimension=0, tiled=True)[0]
    medium_grad = lax.psum(medium, ("dp", "zero"))
    return mixed, grads, short_grad, medium_grad


def solution(mesh):
    in_specs = (
        P(("dp", "zero"), None),
        P(None, "zero"),
        P(),
        P(("dp", "zero"), None),
        P(("dp", "zero")),
        P(("dp", "zero")),
        P(("dp", "zero"), None),
    )
    out_specs = (P(("dp", "zero"), None), P(("dp", "zero"), None), P(None, "zero"), P())
    return jax.shard_map(shards, mesh=mesh, in_specs=in_specs, out_specs=out_specs, check_vma=False)
```

```python
import functools

import jax
import jax.numpy as jnp
from jax import lax
from jax.experimental import pallas as pl
from jax.experimental.pallas import tpu as pltpu
from jax.sharding import PartitionSpec as P

F32 = jnp.float32
BF16 = jnp.bfloat16
MESH = pl.DeviceIdType.MESH
LANES = 128
WIDE = 256


def greet(replicas, zeros):
    barrier = pltpu.get_barrier_semaphore()
    mine, row = lax.axis_index("zero"), lax.axis_index("dp")
    for step in range(1, zeros):
        peer = lax.rem(mine + step, zeros)
        pl.semaphore_signal(barrier, inc=1, device_id={"zero": peer}, device_id_type=MESH)
    for step in range(1, replicas):
        peer = lax.rem(row + step, replicas)
        pl.semaphore_signal(barrier, inc=1, device_id={"dp": peer}, device_id_type=MESH)
    return barrier


def spread(axis, count, source, slots, send, recv):
    me = lax.axis_index(axis)
    copies = []
    for step in range(1, count):
        peer = lax.rem(me + step, count)
        copy = pltpu.make_async_remote_copy(
            src_ref=source(peer),
            dst_ref=slots.at[me],
            send_sem=send.at[step],
            recv_sem=recv.at[step],
            device_id={axis: peer},
            device_id_type=MESH,
        )
        copy.start()
        copies.append(copy)
    return copies


def dot(a, b):
    return jnp.dot(a, b, preferred_element_type=F32)


def block_kernel(
    short, gsize, counts, doc, taps, weight, cot, fq, fk, fv, wq, wk, wv,
    mixed, grads, shorts, medium,
    down, up, causal, causal_t, causal_r, flip, tap_rows, tap_back, living, med,
):
    step = pl.program_id(0)
    length = cot.shape[0]
    width = grads.shape[1] // 3
    per = LANES // gsize
    square = (length, length)

    @pl.when(step == 0)
    def _():
        r = lax.broadcasted_iota(jnp.int32, square, 0)
        c = lax.broadcasted_iota(jnp.int32, square, 1)
        across = jnp.broadcast_to(doc[...].astype(F32), square)
        same = (across == across.T).astype(F32)
        for j in range(short):
            down[j] = jnp.where(r - c == j, same, 0.0).astype(BF16)
            up[j] = jnp.where(c - r == j, same, 0.0).astype(BF16)
        low = jnp.where(r >= c, same, 0.0)
        causal[...] = low
        causal_t[...] = jnp.where(c >= r, same, 0.0)
        turned = (r + c == length - 1).astype(BF16)
        flip[...] = turned
        causal_r[...] = dot(low.astype(BF16), turned)
        rounded = taps[...].astype(BF16).astype(F32).T
        tap_rows[...] = rounded
        back = (lax.rem(r + c, length) == 0).astype(BF16)
        tap_back[...] = dot(rounded.astype(BF16), back)
        living[...] = (r < counts[0]).astype(F32)

    def convolve(feats, filt):
        x = feats[...]
        total = filt[0:1, :] * x.astype(F32)
        for j in range(1, short):
            total = total + filt[j : j + 1, :] * dot(down[j], x)
        return total

    query, key, value = convolve(fq, wq), convolve(fk, wk), convolve(fv, wv)
    lane = lax.broadcasted_iota(jnp.int32, (1, LANES), 1)
    picks = [(lane // gsize == i).astype(BF16) for i in range(per)]
    weighting = weight[0:1, :]
    pieces = [[], [], []]
    for h in range(cot.shape[1] // LANES):
        cols = slice(h * LANES, (h + 1) * LANES)
        q, k, v = query[:, cols], key[:, cols], value[:, cols]
        product = (k * v).astype(BF16)
        first = step * (cot.shape[1] // gsize) + h * per
        forward, backward = [], []
        for i in range(per):
            row = jnp.broadcast_to(tap_back[pl.ds(first + i, 1), :], square)
            row = pltpu.roll(row, 0, 1, stride=1, stride_axis=0)
            forward.append((row * causal[...]).astype(BF16))
            row = jnp.broadcast_to(tap_rows[pl.ds(first + i, 1), :], square)
            row = pltpu.roll(row, 0, 1, stride=1, stride_axis=0)
            backward.append((row * causal_t[...]).astype(BF16))
        long_conv = dot(
            jnp.concatenate(forward, 1), jnp.concatenate([product * m for m in picks], 0)
        )
        alive = living[...]
        mixed[:, cols] = (alive * q * long_conv).astype(BF16)
        grad_out = cot[:, cols].astype(F32) * alive * weighting
        grad_long = (grad_out * q).astype(BF16)
        chosen = jnp.concatenate([grad_long * m for m in picks], 0)
        grad_product = dot(jnp.concatenate(backward, 1), chosen)
        turned = dot(flip[...], product).astype(BF16)
        crossed = lax.dot_general(
            chosen, turned, (((1,), (1,)), ((), ())), preferred_element_type=F32
        )
        for i in range(per):
            part = crossed[i * length : (i + 1) * length] * causal_r[...]
            part = pltpu.roll(part, 1, 1, stride=1, stride_axis=0)
            med[pl.ds(first + i, 1), :] = jnp.sum(part, 0, keepdims=True)
        pieces[0].append((grad_out * long_conv).astype(BF16))
        pieces[1].append((grad_product * v).astype(BF16))
        pieces[2].append((grad_product * k).astype(BF16))

    span = cot.shape[1]
    for n, (feats, filt) in enumerate(((fq, wq), (fk, wk), (fv, wv))):
        grad = jnp.concatenate(pieces[n], 1)
        x = feats[...].astype(F32)
        where = pl.ds(pl.multiple_of(n * width + step * span, LANES), span)
        total = None
        for j in range(short):
            moved = grad.astype(F32) if j == 0 else dot(up[j], grad)
            term = filt[j : j + 1, :] * moved
            total = term if total is None else total + term
            shorts[j : j + 1, where] = jnp.sum(moved * x, 0, keepdims=True)
        shorts[short:8, where] = jnp.zeros((8 - short, span), F32)
        grads[:, where] = total.astype(BF16)

    @pl.when(step == pl.num_programs(0) - 1)
    def _():
        medium[...] = med[...].T


def run_block(feats, filters, medium_filter, doc_ids, counts, weight, cotangent, short):
    length, width = cotangent.shape
    taps_count, groups = medium_filter.shape
    steps = width // WIDE
    square = (length, length)

    def part(n):
        return pl.BlockSpec((length, WIDE), lambda i, n=n: (0, n * steps + i))

    def part8(n):
        return pl.BlockSpec((8, WIDE), lambda i, n=n: (0, n * steps + i))

    def whole(shape):
        return pl.BlockSpec(shape, lambda i: (0, 0))

    return pl.pallas_call(
        functools.partial(block_kernel, short, width // groups),
        grid=(steps,),
        in_specs=[
            pl.BlockSpec(memory_space=pltpu.SMEM),
            whole((1, length)),
            whole((taps_count, groups)),
            whole((8, LANES)),
            part(0), part(0), part(1), part(2), part8(0), part8(1), part8(2),
        ],
        out_specs=[part(0), whole(feats.shape), whole((8, 3 * width)), whole((taps_count, groups))],
        out_shape=[
            jax.ShapeDtypeStruct((length, width), BF16),
            jax.ShapeDtypeStruct(feats.shape, BF16),
            jax.ShapeDtypeStruct((8, 3 * width), F32),
            jax.ShapeDtypeStruct((taps_count, groups), F32),
        ],
        scratch_shapes=[
            pltpu.VMEM((short, length, length), BF16),
            pltpu.VMEM((short, length, length), BF16),
            pltpu.VMEM(square, F32),
            pltpu.VMEM(square, F32),
            pltpu.VMEM(square, F32),
            pltpu.VMEM(square, BF16),
            pltpu.VMEM((groups, taps_count), F32),
            pltpu.VMEM((groups, taps_count), F32),
            pltpu.VMEM((length, LANES), F32),
            pltpu.VMEM((groups, taps_count), F32),
        ],
        compiler_params=pltpu.CompilerParams(vmem_limit_bytes=40 * 1024 * 1024),
        name="conv_block",
    )(counts, doc_ids, medium_filter, weight, cotangent, feats, feats, feats, filters, filters, filters)


def toeplitz(tile, length):
    return jnp.concatenate([pltpu.roll(tile, at, 1) if at else tile for at in range(0, length, 8)], 0)


def whole_kernel(
    replicas, zeros, scale, short, gsize,
    counts, plan, doc, taps, filt, feats_hbm, cot_hbm,
    mixed_hbm, grads_hbm, short_out, medium_out,
    mixed, grads, feats, cot, loaded, rows, stage, slots, tally, tallies, filters,
    down, down_cat, up_cat, causal, causal_t, causal_r, flip, base_rows, base_back, living, med,
    forward, backward, grad_short, crossing,
    mpack, mslots, mpart, mparts, share, shares, spack, sslots, spart, sparts,
    send, recv, tsend, trecv, m1s, m1r, m2s, m2r, m3s, m3r, s1s, s1r, s2s, s2r,
):
    barrier = greet(replicas, zeros)
    mine, place = lax.axis_index("zero"), lax.axis_index("dp")
    length = cot.shape[0]
    width = cot.shape[1]
    cw = filt.shape[1]
    half = cw // 2
    per = LANES // gsize
    square = (length, length)
    load_feats = pltpu.make_async_copy(feats_hbm, feats, loaded.at[0])
    load_cot = pltpu.make_async_copy(cot_hbm, cot, loaded.at[1])
    load_feats.start()
    load_cot.start()

    lane = lax.broadcasted_iota(jnp.int32, (1, cw), 1)
    rows[0:short, :] = filt[...].astype(F32)
    rows[short:8, :] = jnp.where(lane == plan[0], counts[0].astype(F32), 0.0)
    staged = jnp.concatenate([rows[:, :half], rows[:, half:]], 0).astype(BF16)
    stage[...] = staged
    slots[mine] = staged
    pl.semaphore_wait(barrier, zeros + replicas - 2)
    gathering = spread("zero", zeros, lambda peer: stage, slots, send, recv)

    r = lax.broadcasted_iota(jnp.int32, square, 0)
    c = lax.broadcasted_iota(jnp.int32, square, 1)
    across = jnp.broadcast_to(doc[...].astype(F32), square)
    same = (across == across.T).astype(F32)
    for j in range(short):
        down[j] = jnp.where(r - c == j, same, 0.0).astype(BF16)
        if j:
            at = slice((j - 1) * length, j * length)
            down_cat[:, at] = down[j]
            up_cat[:, at] = jnp.where(c - r == j, same, 0.0).astype(BF16)
    low = jnp.where(r >= c, same, 0.0)
    causal[...] = low.astype(BF16)
    causal_t[...] = jnp.where(c >= r, same, 0.0).astype(BF16)
    turn = (r + c == length - 1).astype(BF16)
    flip[...] = turn
    causal_r[...] = dot(low.astype(BF16), turn)
    rounded = taps[...].astype(BF16).astype(F32).T
    tap_rows = rounded
    back = (lax.rem(r + c, length) == 0).astype(BF16)
    tap_back = dot(rounded.astype(BF16), back)
    living[...] = (r < counts[0]).astype(F32)

    for a in range(8):
        lines = pl.ds(a, taps.shape[1], stride=8)
        base_back[lines, :] = pltpu.roll(tap_back, a, 1)
        base_rows[lines, :] = pltpu.roll(tap_rows, a, 1)

    def build(block, carry):
        for i in range(per):
            at = slice(i * length, (i + 1) * length)
            tile = pl.ds(pl.multiple_of((block * per + i) * 8, 8), 8)
            one = toeplitz(base_back[tile, :], length)
            forward[block, :, at] = one.astype(BF16) * causal[...]
            two = toeplitz(base_rows[tile, :], length)
            backward[block, :, at] = two.astype(BF16) * causal_t[...]
        return carry

    lax.fori_loop(0, width // LANES, build, 0)
    crossing[...] = jnp.zeros_like(crossing)

    for copy in gathering:
        copy.wait()
    total = slots[0].astype(F32)[short : short + 1, :LANES]
    for z in range(1, zeros):
        total = total + slots[z].astype(F32)[short : short + 1, :LANES]
    tally[...] = jnp.broadcast_to(total, (8, LANES))
    tallies[place] = jnp.broadcast_to(total, (8, LANES))
    counting = spread("dp", replicas, lambda peer: tally, tallies, tsend, trecv)
    for z in range(zeros):
        block = slots[z].astype(F32)
        filters[:, z * cw : z * cw + half] = block[0:8]
        filters[:, z * cw + half : (z + 1) * cw] = block[8:16]
    load_feats.wait()
    load_cot.wait()

    group = lax.broadcasted_iota(jnp.int32, (1, LANES), 1) // gsize
    picks = [(group == i).astype(BF16) for i in range(per)]

    def blocks(step, carry):
        def convolve(n):
            where = pl.ds(pl.multiple_of(n * width + step * WIDE, LANES), WIDE)
            x = feats[:, where]
            taps7 = filters[:, where]
            narrow = taps7.astype(BF16)
            scaled = jnp.concatenate([x * narrow[j : j + 1] for j in range(1, short)], 0)
            return taps7[0:1] * x.astype(F32) + dot(down_cat[...], scaled)

        query, key, value = convolve(0), convolve(1), convolve(2)
        for h in range(WIDE // LANES):
            cols = slice(h * LANES, (h + 1) * LANES)
            q, k, v = query[:, cols], key[:, cols], value[:, cols]
            begin = pl.multiple_of(step * WIDE + h * LANES, LANES)
            here = pl.ds(begin, LANES)
            product = (k * v).astype(BF16)
            block = step * (WIDE // LANES) + h
            long_conv = dot(forward[block], jnp.concatenate([product * m for m in picks], 0))
            alive = living[...]
            mixed[:, here] = (alive * q * long_conv).astype(BF16)
            grad_out = cot[:, here].astype(F32) * alive
            grad_long = (grad_out * q).astype(BF16)
            chosen = jnp.concatenate([grad_long * m for m in picks], 0)
            grad_product = dot(backward[block], chosen)
            turned = lax.dot_general(
                product, flip[...], (((0,), (0,)), ((), ())), preferred_element_type=F32
            ).astype(BF16)
            for i in range(per):
                at = slice(i * gsize, (i + 1) * gsize)
                crossing[h, at, i * length : (i + 1) * length] = turned[at]
            crossed = dot(grad_long, crossing[h])
            for i in range(per):
                part = crossed[:, i * length : (i + 1) * length] * causal_r[...]
                summed = part[0:8]
                for at in range(8, length, 8):
                    summed = summed + pltpu.roll(part[at : at + 8], at, 1)
                med[pl.ds(pl.multiple_of((block * per + i) * 8, 8), 8), :] = summed
            grad_short[:, here] = (grad_out * long_conv).astype(BF16)
            there = pl.ds(pl.multiple_of(begin + width, LANES), LANES)
            grad_short[:, there] = (grad_product * v).astype(BF16)
            there = pl.ds(pl.multiple_of(begin + 2 * width, LANES), LANES)
            grad_short[:, there] = (grad_product * k).astype(BF16)
        return carry

    lax.fori_loop(0, width // WIDE, blocks, 0)
    save_mixed = pltpu.make_async_copy(mixed, mixed_hbm, loaded.at[2])
    save_mixed.start()

    for copy in counting:
        copy.wait()
    total = tallies[0]
    for p in range(1, replicas):
        total = total + tallies[p]
    lane8 = lax.broadcasted_iota(jnp.int32, (8, LANES), 1)
    own = jnp.sum(jnp.where(lane8 == plan[0], total, 0.0), 1, keepdims=True)
    weight = (scale / own)[0:1]

    depth = taps.shape[0] // zeros
    total = None
    for a in range(8):
        part = pltpu.roll(med[pl.ds(a, taps.shape[1], stride=8), :], a + 1, 1)
        total = part if total is None else total + part
    medium = total.T * weight
    for z in range(zeros):
        mpack[z] = medium[z * depth : (z + 1) * depth].astype(BF16)
    mslots[mine] = mpack[mine]
    medium_one = spread("zero", zeros, lambda peer: mpack.at[peer], mslots, m1s, m1r)

    def short_chunk(owner):
        sums = []
        for s in range(cw // WIDE):
            where = pl.ds(pl.multiple_of(owner * cw + s * WIDE, LANES), WIDE)
            x = feats[:, where]
            grad = grad_short[:, where].astype(F32)
            lines = [jnp.sum(grad * x.astype(F32), 0, keepdims=True)]
            for j in range(1, short):
                lines.append(jnp.sum(grad * dot(down[j], x), 0, keepdims=True))
            lines.append(jnp.zeros((8 - short, WIDE), F32))
            sums.append(jnp.concatenate(lines, 0))
        both = jnp.concatenate(sums, 1) * weight
        return jnp.concatenate([both[:, :half], both[:, half:]], 0).astype(BF16)

    def short_copy(step):
        peer = lax.rem(mine + step, zeros)
        return pltpu.make_async_remote_copy(
            src_ref=spack.at[peer],
            dst_ref=sslots.at[mine],
            send_sem=s1s.at[step],
            recv_sem=s1r.at[step],
            device_id={"zero": peer},
            device_id_type=MESH,
        )

    def send_short(step, carry):
        peer = lax.rem(mine + step, zeros)
        spack[peer] = short_chunk(peer)
        short_copy(step).start()
        return carry

    lax.fori_loop(1, zeros, send_short, 0)
    sslots[mine] = short_chunk(mine)

    for copy in medium_one:
        copy.wait()
    total = mslots[0].astype(F32)
    for z in range(1, zeros):
        total = total + mslots[z].astype(F32)
    mpart[...] = total
    mparts[place] = total
    medium_two = spread("dp", replicas, lambda peer: mpart, mparts, m2s, m2r)

    def feats_chunk(index, carry):
        where = pl.ds(pl.multiple_of(index * WIDE, LANES), WIDE)
        grad = grad_short[:, where]
        taps7 = filters[:, where]
        narrow = taps7.astype(BF16)
        scaled = jnp.concatenate([grad * narrow[j : j + 1] for j in range(1, short)], 0)
        total = taps7[0:1] * grad.astype(F32) + dot(up_cat[...], scaled)
        grads[:, where] = (total * weight).astype(BF16)
        return carry

    pieces = 3 * width // WIDE
    middle = pieces // 2 * WIDE
    lax.fori_loop(0, pieces // 2, feats_chunk, 0)
    cols = slice(0, middle)
    save_one = pltpu.make_async_copy(grads.at[:, cols], grads_hbm.at[:, cols], loaded.at[3])
    save_one.start()

    for step in range(1, zeros):
        short_copy(step).wait()
    total = sslots[0].astype(F32)
    for z in range(1, zeros):
        total = total + sslots[z].astype(F32)
    spart[...] = total
    sparts[place] = total
    short_two = spread("dp", replicas, lambda peer: spart, sparts, s2s, s2r)
    for copy in medium_two:
        copy.wait()
    total = mparts[0]
    for p in range(1, replicas):
        total = total + mparts[p]
    share[...] = total
    shares[mine] = total
    medium_three = spread("zero", zeros, lambda peer: share, shares, m3s, m3r)

    lax.fori_loop(pieces // 2, pieces, feats_chunk, 0)
    cols = slice(middle, 3 * width)
    save_two = pltpu.make_async_copy(grads.at[:, cols], grads_hbm.at[:, cols], loaded.at[4])
    save_two.start()

    for copy in short_two:
        copy.wait()
    total = sparts[0]
    for p in range(1, replicas):
        total = total + sparts[p]
    short_out[:, :half] = total[0:short]
    short_out[:, half:] = total[8 : 8 + short]
    for copy in medium_three:
        copy.wait()
    for z in range(zeros):
        medium_out[z * depth : (z + 1) * depth, :] = shares[z]
    save_mixed.wait()
    save_one.wait()
    save_two.wait()


def run_whole(feats, short_filter, medium_filter, doc_ids, counts, plan, cotangent, replicas, zeros, scale):
    length, width = cotangent.shape
    short, cw = short_filter.shape
    half = cw // 2
    taps_count, groups = medium_filter.shape
    depth = taps_count // zeros
    square = (length, length)
    gsize = width // groups
    in_vmem = pl.BlockSpec(memory_space=pltpu.VMEM)
    in_smem = pl.BlockSpec(memory_space=pltpu.SMEM)
    anywhere = pl.BlockSpec(memory_space=pl.ANY)
    stacked = (width // LANES, length, LANES // gsize * length)
    along_zero, along_dp = pltpu.SemaphoreType.DMA((zeros,)), pltpu.SemaphoreType.DMA((replicas,))
    return pl.pallas_call(
        functools.partial(whole_kernel, replicas, zeros, scale, short, gsize),
        in_specs=[in_smem, in_smem, in_vmem, in_vmem, in_vmem, anywhere, anywhere],
        out_specs=[anywhere, anywhere, in_vmem, in_vmem],
        out_shape=[
            jax.ShapeDtypeStruct((length, width), BF16),
            jax.ShapeDtypeStruct(feats.shape, BF16),
            jax.ShapeDtypeStruct((short, cw), F32),
            jax.ShapeDtypeStruct((taps_count, groups), F32),
        ],
        scratch_shapes=[
            pltpu.VMEM((length, width), BF16),
            pltpu.VMEM(feats.shape, BF16),
            pltpu.VMEM(feats.shape, BF16),
            pltpu.VMEM((length, width), BF16),
            pltpu.SemaphoreType.DMA((5,)),
            pltpu.VMEM((8, cw), F32),
            pltpu.VMEM((16, half), BF16),
            pltpu.VMEM((zeros, 16, half), BF16),
            pltpu.VMEM((8, LANES), F32),
            pltpu.VMEM((replicas, 8, LANES), F32),
            pltpu.VMEM((8, 3 * width), F32),
            pltpu.VMEM((short, length, length), BF16),
            pltpu.VMEM((length, (short - 1) * length), BF16),
            pltpu.VMEM((length, (short - 1) * length), BF16),
            pltpu.VMEM(square, BF16),
            pltpu.VMEM(square, BF16),
            pltpu.VMEM(square, F32),
            pltpu.VMEM(square, BF16),
            pltpu.VMEM((8 * groups, taps_count), F32),
            pltpu.VMEM((8 * groups, taps_count), F32),
            pltpu.VMEM((length, LANES), F32),
            pltpu.VMEM((8 * groups, taps_count), F32),
            pltpu.VMEM(stacked, BF16),
            pltpu.VMEM(stacked, BF16),
            pltpu.VMEM(feats.shape, BF16),
            pltpu.VMEM((WIDE // LANES, LANES, LANES // gsize * length), BF16),
            pltpu.VMEM((zeros, depth, groups), BF16),
            pltpu.VMEM((zeros, depth, groups), BF16),
            pltpu.VMEM((depth, groups), F32),
            pltpu.VMEM((replicas, depth, groups), F32),
            pltpu.VMEM((depth, groups), F32),
            pltpu.VMEM((zeros, depth, groups), F32),
            pltpu.VMEM((zeros, 16, half), BF16),
            pltpu.VMEM((zeros, 16, half), BF16),
            pltpu.VMEM((16, half), F32),
            pltpu.VMEM((replicas, 16, half), F32),
            along_zero, along_zero, along_dp, along_dp,
            along_zero, along_zero, along_dp, along_dp, along_zero, along_zero,
            along_zero, along_zero, along_dp, along_dp,
        ],
        compiler_params=pltpu.CompilerParams(
            collective_id=0, has_side_effects=True, vmem_limit_bytes=56 * 1024 * 1024
        ),
        name="whole_block",
    )(counts, plan, doc_ids, medium_filter, short_filter, feats, cotangent)


def hand_kernel(count, *refs):
    sources, targets = refs[:count], refs[count : 2 * count]
    held, came, left = refs[2 * count : 3 * count], refs[3 * count], refs[3 * count + 1]
    arriving, leaving = [], []
    for n in range(count):
        rows = sources[n].shape[0]
        cuts = 4 if rows % 64 == 0 and n < 2 else 1
        for cut in range(cuts):
            part = pl.ds(cut * rows // cuts, rows // cuts)
            slot, at = held[n].at[part], len(arriving)
            arriving.append(pltpu.make_async_copy(sources[n].at[part], slot, came.at[at]))
            leaving.append(pltpu.make_async_copy(slot, targets[n].at[part], left.at[at]))
    for copy in arriving:
        copy.start()
    for copy, onward in zip(arriving, leaving):
        copy.wait()
        onward.start()
    for copy in leaving:
        copy.wait()


def hand_over(arrays):
    anywhere = pl.BlockSpec(memory_space=pl.ANY)
    return pl.pallas_call(
        functools.partial(hand_kernel, len(arrays)),
        in_specs=[anywhere] * len(arrays),
        out_specs=[anywhere] * len(arrays),
        out_shape=[jax.ShapeDtypeStruct(a.shape, a.dtype) for a in arrays],
        scratch_shapes=[pltpu.VMEM(a.shape, a.dtype) for a in arrays]
        + [pltpu.SemaphoreType.DMA((4 * len(arrays),))] * 2,
        compiler_params=pltpu.CompilerParams(vmem_limit_bytes=56 * 1024 * 1024),
        name="hand_over",
    )(*arrays)


def shards(feats, short_filter, medium_filter, doc_ids, counts, plan, cotangent):
    replicas = lax.axis_size("dp")
    zeros = lax.axis_size("zero")
    length = feats.shape[0]
    short, cw = short_filter.shape
    scale = float(length * replicas * zeros / replicas)
    packed = cw % WIDE == 0 and medium_filter.shape[0] == 16 * zeros
    if packed:
        return hand_over(run_whole(
            feats, short_filter, medium_filter, doc_ids, counts, plan, cotangent, replicas, zeros, scale
        ))
    member = (plan[0] == jnp.arange(replicas)).astype(F32)
    totals = lax.psum(member * counts[0].astype(F32), ("dp", "zero"))
    weight = jnp.broadcast_to(scale / jnp.sum(member * totals), (8, LANES))
    filters = lax.all_gather(short_filter, "zero", axis=1, tiled=True).astype(F32)
    filters = jnp.pad(filters, ((0, 8 - short), (0, 0)))
    mixed, grads, shorts, medium = run_block(
        feats, filters, medium_filter, doc_ids, counts, weight, cotangent, short
    )
    own = lax.psum(shorts[:short], "dp")
    own = own.reshape(short, zeros, cw).transpose(1, 0, 2)
    short_grad = lax.psum_scatter(own, "zero", scatter_dimension=0, tiled=True)[0]
    medium_grad = lax.psum(medium, ("dp", "zero"))
    return mixed, grads, short_grad, medium_grad


def solution(mesh):
    in_specs = (
        P(("dp", "zero"), None),
        P(None, "zero"),
        P(),
        P(("dp", "zero"), None),
        P(("dp", "zero")),
        P(("dp", "zero")),
        P(("dp", "zero"), None),
    )
    out_specs = (P(("dp", "zero"), None), P(("dp", "zero"), None), P(None, "zero"), P())
    return jax.shard_map(shards, mesh=mesh, in_specs=in_specs, out_specs=out_specs, check_vma=False)
```

```python
import functools

import jax
import jax.numpy as jnp
from jax import lax
from jax.experimental import pallas as pl
from jax.experimental.pallas import tpu as pltpu
from jax.sharding import PartitionSpec as P

F32 = jnp.float32
BF16 = jnp.bfloat16
MESH = pl.DeviceIdType.MESH
LANES = 128
WIDE = 256


def greet(replicas, zeros):
    barrier = pltpu.get_barrier_semaphore()
    mine, row = lax.axis_index("zero"), lax.axis_index("dp")
    for step in range(1, zeros):
        peer = lax.rem(mine + step, zeros)
        pl.semaphore_signal(barrier, inc=1, device_id={"zero": peer}, device_id_type=MESH)
    for step in range(1, replicas):
        peer = lax.rem(row + step, replicas)
        pl.semaphore_signal(barrier, inc=1, device_id={"dp": peer}, device_id_type=MESH)
    return barrier


def spread(axis, count, source, slots, send, recv):
    me = lax.axis_index(axis)
    copies = []
    for step in range(1, count):
        peer = lax.rem(me + step, count)
        copy = pltpu.make_async_remote_copy(
            src_ref=source(peer),
            dst_ref=slots.at[me],
            send_sem=send.at[step],
            recv_sem=recv.at[step],
            device_id={axis: peer},
            device_id_type=MESH,
        )
        copy.start()
        copies.append(copy)
    return copies


def dot(a, b):
    return jnp.dot(a, b, preferred_element_type=F32)


def block_kernel(
    short, gsize, counts, doc, taps, weight, cot, fq, fk, fv, wq, wk, wv,
    mixed, grads, shorts, medium,
    down, up, causal, causal_t, causal_r, flip, tap_rows, tap_back, living, med,
):
    step = pl.program_id(0)
    length = cot.shape[0]
    width = grads.shape[1] // 3
    per = LANES // gsize
    square = (length, length)

    @pl.when(step == 0)
    def _():
        r = lax.broadcasted_iota(jnp.int32, square, 0)
        c = lax.broadcasted_iota(jnp.int32, square, 1)
        across = jnp.broadcast_to(doc[...].astype(F32), square)
        same = (across == across.T).astype(F32)
        for j in range(short):
            down[j] = jnp.where(r - c == j, same, 0.0).astype(BF16)
            up[j] = jnp.where(c - r == j, same, 0.0).astype(BF16)
        low = jnp.where(r >= c, same, 0.0)
        causal[...] = low
        causal_t[...] = jnp.where(c >= r, same, 0.0)
        turned = (r + c == length - 1).astype(BF16)
        flip[...] = turned
        causal_r[...] = dot(low.astype(BF16), turned)
        rounded = taps[...].astype(BF16).astype(F32).T
        tap_rows[...] = rounded
        back = (lax.rem(r + c, length) == 0).astype(BF16)
        tap_back[...] = dot(rounded.astype(BF16), back)
        living[...] = (r < counts[0]).astype(F32)

    def convolve(feats, filt):
        x = feats[...]
        total = filt[0:1, :] * x.astype(F32)
        for j in range(1, short):
            total = total + filt[j : j + 1, :] * dot(down[j], x)
        return total

    query, key, value = convolve(fq, wq), convolve(fk, wk), convolve(fv, wv)
    lane = lax.broadcasted_iota(jnp.int32, (1, LANES), 1)
    picks = [(lane // gsize == i).astype(BF16) for i in range(per)]
    weighting = weight[0:1, :]
    pieces = [[], [], []]
    for h in range(cot.shape[1] // LANES):
        cols = slice(h * LANES, (h + 1) * LANES)
        q, k, v = query[:, cols], key[:, cols], value[:, cols]
        product = (k * v).astype(BF16)
        first = step * (cot.shape[1] // gsize) + h * per
        forward, backward = [], []
        for i in range(per):
            row = jnp.broadcast_to(tap_back[pl.ds(first + i, 1), :], square)
            row = pltpu.roll(row, 0, 1, stride=1, stride_axis=0)
            forward.append((row * causal[...]).astype(BF16))
            row = jnp.broadcast_to(tap_rows[pl.ds(first + i, 1), :], square)
            row = pltpu.roll(row, 0, 1, stride=1, stride_axis=0)
            backward.append((row * causal_t[...]).astype(BF16))
        long_conv = dot(
            jnp.concatenate(forward, 1), jnp.concatenate([product * m for m in picks], 0)
        )
        alive = living[...]
        mixed[:, cols] = (alive * q * long_conv).astype(BF16)
        grad_out = cot[:, cols].astype(F32) * alive * weighting
        grad_long = (grad_out * q).astype(BF16)
        chosen = jnp.concatenate([grad_long * m for m in picks], 0)
        grad_product = dot(jnp.concatenate(backward, 1), chosen)
        turned = dot(flip[...], product).astype(BF16)
        crossed = lax.dot_general(
            chosen, turned, (((1,), (1,)), ((), ())), preferred_element_type=F32
        )
        for i in range(per):
            part = crossed[i * length : (i + 1) * length] * causal_r[...]
            part = pltpu.roll(part, 1, 1, stride=1, stride_axis=0)
            med[pl.ds(first + i, 1), :] = jnp.sum(part, 0, keepdims=True)
        pieces[0].append((grad_out * long_conv).astype(BF16))
        pieces[1].append((grad_product * v).astype(BF16))
        pieces[2].append((grad_product * k).astype(BF16))

    span = cot.shape[1]
    for n, (feats, filt) in enumerate(((fq, wq), (fk, wk), (fv, wv))):
        grad = jnp.concatenate(pieces[n], 1)
        x = feats[...].astype(F32)
        where = pl.ds(pl.multiple_of(n * width + step * span, LANES), span)
        total = None
        for j in range(short):
            moved = grad.astype(F32) if j == 0 else dot(up[j], grad)
            term = filt[j : j + 1, :] * moved
            total = term if total is None else total + term
            shorts[j : j + 1, where] = jnp.sum(moved * x, 0, keepdims=True)
        shorts[short:8, where] = jnp.zeros((8 - short, span), F32)
        grads[:, where] = total.astype(BF16)

    @pl.when(step == pl.num_programs(0) - 1)
    def _():
        medium[...] = med[...].T


def run_block(feats, filters, medium_filter, doc_ids, counts, weight, cotangent, short):
    length, width = cotangent.shape
    taps_count, groups = medium_filter.shape
    steps = width // WIDE
    square = (length, length)

    def part(n):
        return pl.BlockSpec((length, WIDE), lambda i, n=n: (0, n * steps + i))

    def part8(n):
        return pl.BlockSpec((8, WIDE), lambda i, n=n: (0, n * steps + i))

    def whole(shape):
        return pl.BlockSpec(shape, lambda i: (0, 0))

    return pl.pallas_call(
        functools.partial(block_kernel, short, width // groups),
        grid=(steps,),
        in_specs=[
            pl.BlockSpec(memory_space=pltpu.SMEM),
            whole((1, length)),
            whole((taps_count, groups)),
            whole((8, LANES)),
            part(0), part(0), part(1), part(2), part8(0), part8(1), part8(2),
        ],
        out_specs=[part(0), whole(feats.shape), whole((8, 3 * width)), whole((taps_count, groups))],
        out_shape=[
            jax.ShapeDtypeStruct((length, width), BF16),
            jax.ShapeDtypeStruct(feats.shape, BF16),
            jax.ShapeDtypeStruct((8, 3 * width), F32),
            jax.ShapeDtypeStruct((taps_count, groups), F32),
        ],
        scratch_shapes=[
            pltpu.VMEM((short, length, length), BF16),
            pltpu.VMEM((short, length, length), BF16),
            pltpu.VMEM(square, F32),
            pltpu.VMEM(square, F32),
            pltpu.VMEM(square, F32),
            pltpu.VMEM(square, BF16),
            pltpu.VMEM((groups, taps_count), F32),
            pltpu.VMEM((groups, taps_count), F32),
            pltpu.VMEM((length, LANES), F32),
            pltpu.VMEM((groups, taps_count), F32),
        ],
        compiler_params=pltpu.CompilerParams(vmem_limit_bytes=40 * 1024 * 1024),
        name="conv_block",
    )(counts, doc_ids, medium_filter, weight, cotangent, feats, feats, feats, filters, filters, filters)


def toeplitz(tile, length):
    return jnp.concatenate([pltpu.roll(tile, at, 1) if at else tile for at in range(0, length, 8)], 0)


def whole_kernel(
    replicas, zeros, scale, short, gsize,
    counts, plan, doc, taps, filt, feats_hbm, cot_hbm,
    mixed_hbm, grads_hbm, short_out, medium_out,
    mixed, grads, feats, cot, loaded, rows, stage, slots, tally, tallies, filters,
    down, down_cat, up_cat, causal, causal_t, causal_r, flip, base_rows, base_back, living, med,
    forward, backward, grad_short, crossing,
    mpack, mslots, mpart, mparts, share, shares, spack, sslots, spart, sparts,
    send, recv, tsend, trecv, m1s, m1r, m2s, m2r, m3s, m3r, s1s, s1r, s2s, s2r,
):
    barrier = greet(replicas, zeros)
    mine, place = lax.axis_index("zero"), lax.axis_index("dp")
    length = cot.shape[0]
    width = cot.shape[1]
    cw = filt.shape[1]
    half = cw // 2
    per = LANES // gsize
    square = (length, length)
    load_feats = pltpu.make_async_copy(feats_hbm, feats, loaded.at[0])
    load_cot = pltpu.make_async_copy(cot_hbm, cot, loaded.at[1])
    load_feats.start()
    load_cot.start()

    lane = lax.broadcasted_iota(jnp.int32, (1, cw), 1)
    rows[0:short, :] = filt[...].astype(F32)
    rows[short:8, :] = jnp.where(lane == plan[0], counts[0].astype(F32), 0.0)
    staged = jnp.concatenate([rows[:, :half], rows[:, half:]], 0).astype(BF16)
    stage[...] = staged
    slots[mine] = staged
    pl.semaphore_wait(barrier, zeros + replicas - 2)
    gathering = spread("zero", zeros, lambda peer: stage, slots, send, recv)

    r = lax.broadcasted_iota(jnp.int32, square, 0)
    c = lax.broadcasted_iota(jnp.int32, square, 1)
    across = jnp.broadcast_to(doc[...].astype(F32), square)
    same = (across == across.T).astype(F32)
    for j in range(short):
        down[j] = jnp.where(r - c == j, same, 0.0).astype(BF16)
        if j:
            at = slice((j - 1) * length, j * length)
            down_cat[:, at] = down[j]
            up_cat[:, at] = jnp.where(c - r == j, same, 0.0).astype(BF16)
    low = jnp.where(r >= c, same, 0.0)
    causal[...] = low.astype(BF16)
    causal_t[...] = jnp.where(c >= r, same, 0.0).astype(BF16)
    turn = (r + c == length - 1).astype(BF16)
    flip[...] = turn
    causal_r[...] = dot(low.astype(BF16), turn)
    rounded = taps[...].astype(BF16).astype(F32).T
    tap_rows = rounded
    back = (lax.rem(r + c, length) == 0).astype(BF16)
    tap_back = dot(rounded.astype(BF16), back)
    living[...] = (r < counts[0]).astype(F32)

    for a in range(8):
        lines = pl.ds(a, taps.shape[1], stride=8)
        base_back[lines, :] = pltpu.roll(tap_back, a, 1)
        base_rows[lines, :] = pltpu.roll(tap_rows, a, 1)

    def build(pair, carry):
        for n in range(2 * per):
            block, i = pair * 2 + n // per, n % per
            at = slice(i * length, (i + 1) * length)
            tile = pl.ds(pl.multiple_of((pair * 2 * per + n) * 8, 8), 8)
            one = toeplitz(base_back[tile, :], length)
            forward[block, :, at] = one.astype(BF16) * causal[...]
            two = toeplitz(base_rows[tile, :], length)
            backward[block, :, at] = two.astype(BF16) * causal_t[...]
        return carry

    lax.fori_loop(0, width // (2 * LANES), build, 0)
    crossing[...] = jnp.zeros_like(crossing)

    for copy in gathering:
        copy.wait()
    total = slots[0].astype(F32)[short : short + 1, :LANES]
    for z in range(1, zeros):
        total = total + slots[z].astype(F32)[short : short + 1, :LANES]
    tally[...] = jnp.broadcast_to(total, (8, LANES))
    tallies[place] = jnp.broadcast_to(total, (8, LANES))
    counting = spread("dp", replicas, lambda peer: tally, tallies, tsend, trecv)
    for z in range(zeros):
        block = slots[z].astype(F32)
        filters[:, z * cw : z * cw + half] = block[0:8]
        filters[:, z * cw + half : (z + 1) * cw] = block[8:16]
    load_feats.wait()
    load_cot.wait()

    group = lax.broadcasted_iota(jnp.int32, (1, LANES), 1) // gsize
    picks = [(group == i).astype(BF16) for i in range(per)]

    def convolve(n, begin):
        where = pl.ds(pl.multiple_of(n * width + begin, LANES), WIDE)
        x = feats[:, where]
        taps7 = filters[:, where]
        narrow = taps7.astype(BF16)
        scaled = jnp.concatenate([x * narrow[j : j + 1] for j in range(1, short)], 0)
        return taps7[0:1] * x.astype(F32) + dot(down_cat[...], scaled)

    span = crossing.shape[0] * LANES

    def blocks(step, carry):
        halves = []
        for sub in range(span // WIDE):
            begin = step * span + sub * WIDE
            parts = [convolve(n, begin) for n in range(3)]
            for h in range(WIDE // LANES):
                halves.append([p[:, h * LANES : (h + 1) * LANES] for p in parts])
        products, longs, chosens = [], [], []
        for h, (q, k, v) in enumerate(halves):
            product = (k * v).astype(BF16)
            products.append(product)
            block = step * (span // LANES) + h
            longs.append(dot(forward[block], jnp.concatenate([product * m for m in picks], 0)))
        for h, (q, k, v) in enumerate(halves):
            grad_out = cot[:, here(step, h, 0)].astype(F32) * living[...]
            grad_long = (grad_out * q).astype(BF16)
            chosens.append(grad_long)
            turned = lax.dot_general(
                products[h], flip[...], (((0,), (0,)), ((), ())), preferred_element_type=F32
            ).astype(BF16)
            for i in range(per):
                at = slice(i * gsize, (i + 1) * gsize)
                crossing[h, at, i * length : (i + 1) * length] = turned[at]
        for h, (q, k, v) in enumerate(halves):
            block = step * (span // LANES) + h
            grad_product = dot(
                backward[block], jnp.concatenate([chosens[h] * m for m in picks], 0)
            )
            grad_short[:, here(step, h, 1)] = (grad_product * v).astype(BF16)
            grad_short[:, here(step, h, 2)] = (grad_product * k).astype(BF16)
        for h, (q, k, v) in enumerate(halves):
            alive = living[...]
            mixed[:, here(step, h, 0)] = (alive * q * longs[h]).astype(BF16)
            grad_out = cot[:, here(step, h, 0)].astype(F32) * alive
            grad_short[:, here(step, h, 0)] = (grad_out * longs[h]).astype(BF16)
        for h in range(len(halves)):
            block = step * (span // LANES) + h
            crossed = dot(chosens[h], crossing[h])
            for i in range(per):
                part = crossed[:, i * length : (i + 1) * length] * causal_r[...]
                summed = part[0:8]
                for at in range(8, length, 8):
                    summed = summed + pltpu.roll(part[at : at + 8], at, 1)
                med[pl.ds(pl.multiple_of((block * per + i) * 8, 8), 8), :] = summed
        return carry

    def here(step, h, n):
        return pl.ds(pl.multiple_of(n * width + step * span + h * LANES, LANES), LANES)

    lax.fori_loop(0, width // span, blocks, 0)
    save_mixed = pltpu.make_async_copy(mixed, mixed_hbm, loaded.at[2])
    save_mixed.start()

    for copy in counting:
        copy.wait()
    total = tallies[0]
    for p in range(1, replicas):
        total = total + tallies[p]
    lane8 = lax.broadcasted_iota(jnp.int32, (8, LANES), 1)
    own = jnp.sum(jnp.where(lane8 == plan[0], total, 0.0), 1, keepdims=True)
    weight = (scale / own)[0:1]

    depth = taps.shape[0] // zeros
    total = None
    for a in range(8):
        part = pltpu.roll(med[pl.ds(a, taps.shape[1], stride=8), :], a + 1, 1)
        total = part if total is None else total + part
    medium = total.T * weight
    for z in range(zeros):
        mpack[z] = medium[z * depth : (z + 1) * depth].astype(BF16)
    mslots[mine] = mpack[mine]
    medium_one = spread("zero", zeros, lambda peer: mpack.at[peer], mslots, m1s, m1r)

    def short_chunk(owner):
        sums = []
        for s in range(cw // WIDE):
            where = pl.ds(pl.multiple_of(owner * cw + s * WIDE, LANES), WIDE)
            x = feats[:, where]
            grad = grad_short[:, where].astype(F32)
            lines = [jnp.sum(grad * x.astype(F32), 0, keepdims=True)]
            for j in range(1, short):
                lines.append(jnp.sum(grad * dot(down[j], x), 0, keepdims=True))
            lines.append(jnp.zeros((8 - short, WIDE), F32))
            sums.append(jnp.concatenate(lines, 0))
        both = jnp.concatenate(sums, 1) * weight
        return jnp.concatenate([both[:, :half], both[:, half:]], 0).astype(BF16)

    def short_copy(step):
        peer = lax.rem(mine + step, zeros)
        return pltpu.make_async_remote_copy(
            src_ref=spack.at[peer],
            dst_ref=sslots.at[mine],
            send_sem=s1s.at[step],
            recv_sem=s1r.at[step],
            device_id={"zero": peer},
            device_id_type=MESH,
        )

    def send_short(step, carry):
        peer = lax.rem(mine + step, zeros)
        spack[peer] = short_chunk(peer)
        short_copy(step).start()
        return carry

    lax.fori_loop(1, zeros, send_short, 0)
    sslots[mine] = short_chunk(mine)

    for copy in medium_one:
        copy.wait()
    total = mslots[0].astype(F32)
    for z in range(1, zeros):
        total = total + mslots[z].astype(F32)
    mpart[...] = total
    mparts[place] = total
    medium_two = spread("dp", replicas, lambda peer: mpart, mparts, m2s, m2r)

    bundle = 6

    def feats_chunk(index, carry):
        for sub in range(bundle):
            where = pl.ds(pl.multiple_of((index * bundle + sub) * WIDE, LANES), WIDE)
            grad = grad_short[:, where]
            taps7 = filters[:, where]
            narrow = taps7.astype(BF16)
            scaled = jnp.concatenate([grad * narrow[j : j + 1] for j in range(1, short)], 0)
            total = taps7[0:1] * grad.astype(F32) + dot(up_cat[...], scaled)
            grads[:, where] = (total * weight).astype(BF16)
        return carry

    pieces = 3 * width // WIDE // bundle
    middle = pieces // 2 * bundle * WIDE
    lax.fori_loop(0, pieces // 2, feats_chunk, 0)
    cols = slice(0, middle)
    save_one = pltpu.make_async_copy(grads.at[:, cols], grads_hbm.at[:, cols], loaded.at[3])
    save_one.start()

    for step in range(1, zeros):
        short_copy(step).wait()
    total = sslots[0].astype(F32)
    for z in range(1, zeros):
        total = total + sslots[z].astype(F32)
    spart[...] = total
    sparts[place] = total
    short_two = spread("dp", replicas, lambda peer: spart, sparts, s2s, s2r)
    for copy in medium_two:
        copy.wait()
    total = mparts[0]
    for p in range(1, replicas):
        total = total + mparts[p]
    share[...] = total
    shares[mine] = total
    medium_three = spread("zero", zeros, lambda peer: share, shares, m3s, m3r)

    lax.fori_loop(pieces // 2, pieces, feats_chunk, 0)
    cols = slice(middle, 3 * width)
    save_two = pltpu.make_async_copy(grads.at[:, cols], grads_hbm.at[:, cols], loaded.at[4])
    save_two.start()

    for copy in short_two:
        copy.wait()
    total = sparts[0]
    for p in range(1, replicas):
        total = total + sparts[p]
    short_out[:, :half] = total[0:short]
    short_out[:, half:] = total[8 : 8 + short]
    for copy in medium_three:
        copy.wait()
    for z in range(zeros):
        medium_out[z * depth : (z + 1) * depth, :] = shares[z]
    save_mixed.wait()
    save_one.wait()
    save_two.wait()


def run_whole(feats, short_filter, medium_filter, doc_ids, counts, plan, cotangent, replicas, zeros, scale):
    length, width = cotangent.shape
    short, cw = short_filter.shape
    half = cw // 2
    taps_count, groups = medium_filter.shape
    depth = taps_count // zeros
    square = (length, length)
    gsize = width // groups
    in_vmem = pl.BlockSpec(memory_space=pltpu.VMEM)
    in_smem = pl.BlockSpec(memory_space=pltpu.SMEM)
    anywhere = pl.BlockSpec(memory_space=pl.ANY)
    stacked = (width // LANES, length, LANES // gsize * length)
    along_zero, along_dp = pltpu.SemaphoreType.DMA((zeros,)), pltpu.SemaphoreType.DMA((replicas,))
    return pl.pallas_call(
        functools.partial(whole_kernel, replicas, zeros, scale, short, gsize),
        in_specs=[in_smem, in_smem, in_vmem, in_vmem, in_vmem, anywhere, anywhere],
        out_specs=[anywhere, anywhere, in_vmem, in_vmem],
        out_shape=[
            jax.ShapeDtypeStruct((length, width), BF16),
            jax.ShapeDtypeStruct(feats.shape, BF16),
            jax.ShapeDtypeStruct((short, cw), F32),
            jax.ShapeDtypeStruct((taps_count, groups), F32),
        ],
        scratch_shapes=[
            pltpu.VMEM((length, width), BF16),
            pltpu.VMEM(feats.shape, BF16),
            pltpu.VMEM(feats.shape, BF16),
            pltpu.VMEM((length, width), BF16),
            pltpu.SemaphoreType.DMA((5,)),
            pltpu.VMEM((8, cw), F32),
            pltpu.VMEM((16, half), BF16),
            pltpu.VMEM((zeros, 16, half), BF16),
            pltpu.VMEM((8, LANES), F32),
            pltpu.VMEM((replicas, 8, LANES), F32),
            pltpu.VMEM((8, 3 * width), F32),
            pltpu.VMEM((short, length, length), BF16),
            pltpu.VMEM((length, (short - 1) * length), BF16),
            pltpu.VMEM((length, (short - 1) * length), BF16),
            pltpu.VMEM(square, BF16),
            pltpu.VMEM(square, BF16),
            pltpu.VMEM(square, F32),
            pltpu.VMEM(square, BF16),
            pltpu.VMEM((8 * groups, taps_count), F32),
            pltpu.VMEM((8 * groups, taps_count), F32),
            pltpu.VMEM((length, LANES), F32),
            pltpu.VMEM((8 * groups, taps_count), F32),
            pltpu.VMEM(stacked, BF16),
            pltpu.VMEM(stacked, BF16),
            pltpu.VMEM(feats.shape, BF16),
            pltpu.VMEM((2 * WIDE // LANES, LANES, LANES // gsize * length), BF16),
            pltpu.VMEM((zeros, depth, groups), BF16),
            pltpu.VMEM((zeros, depth, groups), BF16),
            pltpu.VMEM((depth, groups), F32),
            pltpu.VMEM((replicas, depth, groups), F32),
            pltpu.VMEM((depth, groups), F32),
            pltpu.VMEM((zeros, depth, groups), F32),
            pltpu.VMEM((zeros, 16, half), BF16),
            pltpu.VMEM((zeros, 16, half), BF16),
            pltpu.VMEM((16, half), F32),
            pltpu.VMEM((replicas, 16, half), F32),
            along_zero, along_zero, along_dp, along_dp,
            along_zero, along_zero, along_dp, along_dp, along_zero, along_zero,
            along_zero, along_zero, along_dp, along_dp,
        ],
        compiler_params=pltpu.CompilerParams(
            collective_id=0, has_side_effects=True, vmem_limit_bytes=56 * 1024 * 1024
        ),
        name="whole_block",
    )(counts, plan, doc_ids, medium_filter, short_filter, feats, cotangent)


def hand_kernel(count, *refs):
    sources, targets = refs[:count], refs[count : 2 * count]
    held, came, left = refs[2 * count : 3 * count], refs[3 * count], refs[3 * count + 1]
    arriving, leaving = [], []
    for n in range(count):
        rows = sources[n].shape[0]
        cuts = 4 if rows % 64 == 0 and n < 2 else 1
        for cut in range(cuts):
            part = pl.ds(cut * rows // cuts, rows // cuts)
            slot, at = held[n].at[part], len(arriving)
            arriving.append(pltpu.make_async_copy(sources[n].at[part], slot, came.at[at]))
            leaving.append(pltpu.make_async_copy(slot, targets[n].at[part], left.at[at]))
    for copy in arriving:
        copy.start()
    for copy, onward in zip(arriving, leaving):
        copy.wait()
        onward.start()
    for copy in leaving:
        copy.wait()


def hand_over(arrays):
    anywhere = pl.BlockSpec(memory_space=pl.ANY)
    return pl.pallas_call(
        functools.partial(hand_kernel, len(arrays)),
        in_specs=[anywhere] * len(arrays),
        out_specs=[anywhere] * len(arrays),
        out_shape=[jax.ShapeDtypeStruct(a.shape, a.dtype) for a in arrays],
        scratch_shapes=[pltpu.VMEM(a.shape, a.dtype) for a in arrays]
        + [pltpu.SemaphoreType.DMA((4 * len(arrays),))] * 2,
        compiler_params=pltpu.CompilerParams(vmem_limit_bytes=56 * 1024 * 1024),
        name="hand_over",
    )(*arrays)


def shards(feats, short_filter, medium_filter, doc_ids, counts, plan, cotangent):
    replicas = lax.axis_size("dp")
    zeros = lax.axis_size("zero")
    length = feats.shape[0]
    short, cw = short_filter.shape
    scale = float(length * replicas * zeros / replicas)
    packed = cw % WIDE == 0 and medium_filter.shape[0] == 16 * zeros
    if packed:
        return hand_over(run_whole(
            feats, short_filter, medium_filter, doc_ids, counts, plan, cotangent, replicas, zeros, scale
        ))
    member = (plan[0] == jnp.arange(replicas)).astype(F32)
    totals = lax.psum(member * counts[0].astype(F32), ("dp", "zero"))
    weight = jnp.broadcast_to(scale / jnp.sum(member * totals), (8, LANES))
    filters = lax.all_gather(short_filter, "zero", axis=1, tiled=True).astype(F32)
    filters = jnp.pad(filters, ((0, 8 - short), (0, 0)))
    mixed, grads, shorts, medium = run_block(
        feats, filters, medium_filter, doc_ids, counts, weight, cotangent, short
    )
    own = lax.psum(shorts[:short], "dp")
    own = own.reshape(short, zeros, cw).transpose(1, 0, 2)
    short_grad = lax.psum_scatter(own, "zero", scatter_dimension=0, tiled=True)[0]
    medium_grad = lax.psum(medium, ("dp", "zero"))
    return mixed, grads, short_grad, medium_grad


def solution(mesh):
    in_specs = (
        P(("dp", "zero"), None),
        P(None, "zero"),
        P(),
        P(("dp", "zero"), None),
        P(("dp", "zero")),
        P(("dp", "zero")),
        P(("dp", "zero"), None),
    )
    out_specs = (P(("dp", "zero"), None), P(("dp", "zero"), None), P(None, "zero"), P())
    return jax.shard_map(shards, mesh=mesh, in_specs=in_specs, out_specs=out_specs, check_vma=False)
```

```python
import functools

import jax
import jax.numpy as jnp
from jax import lax
from jax.experimental import pallas as pl
from jax.experimental.pallas import tpu as pltpu
from jax.sharding import PartitionSpec as P

F32 = jnp.float32
BF16 = jnp.bfloat16
MESH = pl.DeviceIdType.MESH
LANES = 128
WIDE = 256


def greet(replicas, zeros):
    barrier = pltpu.get_barrier_semaphore()
    mine, row = lax.axis_index("zero"), lax.axis_index("dp")
    for step in range(1, zeros):
        peer = lax.rem(mine + step, zeros)
        pl.semaphore_signal(barrier, inc=1, device_id={"zero": peer}, device_id_type=MESH)
    for step in range(1, replicas):
        peer = lax.rem(row + step, replicas)
        pl.semaphore_signal(barrier, inc=1, device_id={"dp": peer}, device_id_type=MESH)
    return barrier


def spread(axis, count, source, slots, send, recv):
    me = lax.axis_index(axis)
    copies = []
    for step in range(1, count):
        peer = lax.rem(me + step, count)
        copy = pltpu.make_async_remote_copy(
            src_ref=source(peer),
            dst_ref=slots.at[me],
            send_sem=send.at[step],
            recv_sem=recv.at[step],
            device_id={axis: peer},
            device_id_type=MESH,
        )
        copy.start()
        copies.append(copy)
    return copies


def dot(a, b):
    return jnp.dot(a, b, preferred_element_type=F32)


def block_kernel(
    short, gsize, counts, doc, taps, weight, cot, fq, fk, fv, wq, wk, wv,
    mixed, grads, shorts, medium,
    down, up, causal, causal_t, causal_r, flip, tap_rows, tap_back, living, med,
):
    step = pl.program_id(0)
    length = cot.shape[0]
    width = grads.shape[1] // 3
    per = LANES // gsize
    square = (length, length)

    @pl.when(step == 0)
    def _():
        r = lax.broadcasted_iota(jnp.int32, square, 0)
        c = lax.broadcasted_iota(jnp.int32, square, 1)
        across = jnp.broadcast_to(doc[...].astype(F32), square)
        same = (across == across.T).astype(F32)
        for j in range(short):
            down[j] = jnp.where(r - c == j, same, 0.0).astype(BF16)
            up[j] = jnp.where(c - r == j, same, 0.0).astype(BF16)
        low = jnp.where(r >= c, same, 0.0)
        causal[...] = low
        causal_t[...] = jnp.where(c >= r, same, 0.0)
        turned = (r + c == length - 1).astype(BF16)
        flip[...] = turned
        causal_r[...] = dot(low.astype(BF16), turned)
        rounded = taps[...].astype(BF16).astype(F32).T
        tap_rows[...] = rounded
        back = (lax.rem(r + c, length) == 0).astype(BF16)
        tap_back[...] = dot(rounded.astype(BF16), back)
        living[...] = (r < counts[0]).astype(F32)

    def convolve(feats, filt):
        x = feats[...]
        total = filt[0:1, :] * x.astype(F32)
        for j in range(1, short):
            total = total + filt[j : j + 1, :] * dot(down[j], x)
        return total

    query, key, value = convolve(fq, wq), convolve(fk, wk), convolve(fv, wv)
    lane = lax.broadcasted_iota(jnp.int32, (1, LANES), 1)
    picks = [(lane // gsize == i).astype(BF16) for i in range(per)]
    weighting = weight[0:1, :]
    pieces = [[], [], []]
    for h in range(cot.shape[1] // LANES):
        cols = slice(h * LANES, (h + 1) * LANES)
        q, k, v = query[:, cols], key[:, cols], value[:, cols]
        product = (k * v).astype(BF16)
        first = step * (cot.shape[1] // gsize) + h * per
        forward, backward = [], []
        for i in range(per):
            row = jnp.broadcast_to(tap_back[pl.ds(first + i, 1), :], square)
            row = pltpu.roll(row, 0, 1, stride=1, stride_axis=0)
            forward.append((row * causal[...]).astype(BF16))
            row = jnp.broadcast_to(tap_rows[pl.ds(first + i, 1), :], square)
            row = pltpu.roll(row, 0, 1, stride=1, stride_axis=0)
            backward.append((row * causal_t[...]).astype(BF16))
        long_conv = dot(
            jnp.concatenate(forward, 1), jnp.concatenate([product * m for m in picks], 0)
        )
        alive = living[...]
        mixed[:, cols] = (alive * q * long_conv).astype(BF16)
        grad_out = cot[:, cols].astype(F32) * alive * weighting
        grad_long = (grad_out * q).astype(BF16)
        chosen = jnp.concatenate([grad_long * m for m in picks], 0)
        grad_product = dot(jnp.concatenate(backward, 1), chosen)
        turned = dot(flip[...], product).astype(BF16)
        crossed = lax.dot_general(
            chosen, turned, (((1,), (1,)), ((), ())), preferred_element_type=F32
        )
        for i in range(per):
            part = crossed[i * length : (i + 1) * length] * causal_r[...]
            part = pltpu.roll(part, 1, 1, stride=1, stride_axis=0)
            med[pl.ds(first + i, 1), :] = jnp.sum(part, 0, keepdims=True)
        pieces[0].append((grad_out * long_conv).astype(BF16))
        pieces[1].append((grad_product * v).astype(BF16))
        pieces[2].append((grad_product * k).astype(BF16))

    span = cot.shape[1]
    for n, (feats, filt) in enumerate(((fq, wq), (fk, wk), (fv, wv))):
        grad = jnp.concatenate(pieces[n], 1)
        x = feats[...].astype(F32)
        where = pl.ds(pl.multiple_of(n * width + step * span, LANES), span)
        total = None
        for j in range(short):
            moved = grad.astype(F32) if j == 0 else dot(up[j], grad)
            term = filt[j : j + 1, :] * moved
            total = term if total is None else total + term
            shorts[j : j + 1, where] = jnp.sum(moved * x, 0, keepdims=True)
        shorts[short:8, where] = jnp.zeros((8 - short, span), F32)
        grads[:, where] = total.astype(BF16)

    @pl.when(step == pl.num_programs(0) - 1)
    def _():
        medium[...] = med[...].T


def run_block(feats, filters, medium_filter, doc_ids, counts, weight, cotangent, short):
    length, width = cotangent.shape
    taps_count, groups = medium_filter.shape
    steps = width // WIDE
    square = (length, length)

    def part(n):
        return pl.BlockSpec((length, WIDE), lambda i, n=n: (0, n * steps + i))

    def part8(n):
        return pl.BlockSpec((8, WIDE), lambda i, n=n: (0, n * steps + i))

    def whole(shape):
        return pl.BlockSpec(shape, lambda i: (0, 0))

    return pl.pallas_call(
        functools.partial(block_kernel, short, width // groups),
        grid=(steps,),
        in_specs=[
            pl.BlockSpec(memory_space=pltpu.SMEM),
            whole((1, length)),
            whole((taps_count, groups)),
            whole((8, LANES)),
            part(0), part(0), part(1), part(2), part8(0), part8(1), part8(2),
        ],
        out_specs=[part(0), whole(feats.shape), whole((8, 3 * width)), whole((taps_count, groups))],
        out_shape=[
            jax.ShapeDtypeStruct((length, width), BF16),
            jax.ShapeDtypeStruct(feats.shape, BF16),
            jax.ShapeDtypeStruct((8, 3 * width), F32),
            jax.ShapeDtypeStruct((taps_count, groups), F32),
        ],
        scratch_shapes=[
            pltpu.VMEM((short, length, length), BF16),
            pltpu.VMEM((short, length, length), BF16),
            pltpu.VMEM(square, F32),
            pltpu.VMEM(square, F32),
            pltpu.VMEM(square, F32),
            pltpu.VMEM(square, BF16),
            pltpu.VMEM((groups, taps_count), F32),
            pltpu.VMEM((groups, taps_count), F32),
            pltpu.VMEM((length, LANES), F32),
            pltpu.VMEM((groups, taps_count), F32),
        ],
        compiler_params=pltpu.CompilerParams(vmem_limit_bytes=40 * 1024 * 1024),
        name="conv_block",
    )(counts, doc_ids, medium_filter, weight, cotangent, feats, feats, feats, filters, filters, filters)


def toeplitz(tile, length):
    return jnp.concatenate([pltpu.roll(tile, at, 1) if at else tile for at in range(0, length, 8)], 0)


def whole_kernel(
    replicas, zeros, scale, short, gsize,
    counts, plan, doc, taps, filt, feats_hbm, cot_hbm,
    mixed_hbm, grads_hbm, short_out, medium_out,
    mixed, grads, feats, cot, loaded, rows, stage, slots, tally, tallies, filters,
    down, down_cat, up_cat, causal, causal_t, causal_r, flip, base_rows, base_back, living, med,
    forward, backward, grad_short, crossing,
    mpack, mslots, mpart, mparts, share, shares, spack, sslots, spart, sparts,
    send, recv, tsend, trecv, m1s, m1r, m2s, m2r, m3s, m3r, s1s, s1r, s2s, s2r,
):
    barrier = greet(replicas, zeros)
    mine, place = lax.axis_index("zero"), lax.axis_index("dp")
    length = cot.shape[0]
    width = cot.shape[1]
    cw = filt.shape[1]
    half = cw // 2
    per = LANES // gsize
    square = (length, length)
    load_feats = pltpu.make_async_copy(feats_hbm, feats, loaded.at[0])
    load_cot = pltpu.make_async_copy(cot_hbm, cot, loaded.at[1])
    load_feats.start()
    load_cot.start()

    lane = lax.broadcasted_iota(jnp.int32, (1, cw), 1)
    rows[0:short, :] = filt[...].astype(F32)
    rows[short:8, :] = jnp.where(lane == plan[0], counts[0].astype(F32), 0.0)
    staged = jnp.concatenate([rows[:, :half], rows[:, half:]], 0).astype(BF16)
    stage[...] = staged
    slots[mine] = staged
    pl.semaphore_wait(barrier, zeros + replicas - 2)
    gathering = spread("zero", zeros, lambda peer: stage, slots, send, recv)

    r = lax.broadcasted_iota(jnp.int32, square, 0)
    c = lax.broadcasted_iota(jnp.int32, square, 1)
    across = jnp.broadcast_to(doc[...].astype(F32), square)
    same = (across == across.T).astype(F32)
    for j in range(short):
        down[j] = jnp.where(r - c == j, same, 0.0).astype(BF16)
        if j:
            at = slice((j - 1) * length, j * length)
            down_cat[:, at] = down[j]
            up_cat[:, at] = jnp.where(c - r == j, same, 0.0).astype(BF16)
    low = jnp.where(r >= c, same, 0.0)
    causal[...] = low.astype(BF16)
    causal_t[...] = jnp.where(c >= r, same, 0.0).astype(BF16)
    turn = (r + c == length - 1).astype(BF16)
    flip[...] = turn
    causal_r[...] = dot(low.astype(BF16), turn)
    rounded = taps[...].astype(BF16).astype(F32).T
    tap_rows = rounded
    back = (lax.rem(r + c, length) == 0).astype(BF16)
    tap_back = dot(rounded.astype(BF16), back)
    living[...] = (r < counts[0]).astype(F32)

    for a in range(8):
        lines = pl.ds(a, taps.shape[1], stride=8)
        base_back[lines, :] = pltpu.roll(tap_back, a, 1)
        base_rows[lines, :] = pltpu.roll(tap_rows, a, 1)

    def build(pair, carry):
        for n in range(2 * per):
            block, i = pair * 2 + n // per, n % per
            at = slice(i * length, (i + 1) * length)
            tile = pl.ds(pl.multiple_of((pair * 2 * per + n) * 8, 8), 8)
            one = toeplitz(base_back[tile, :], length)
            forward[block, :, at] = one.astype(BF16) * causal[...]
            two = toeplitz(base_rows[tile, :], length)
            backward[block, :, at] = two.astype(BF16) * causal_t[...]
        return carry

    lax.fori_loop(0, width // (2 * LANES), build, 0)
    crossing[...] = jnp.zeros_like(crossing)

    for copy in gathering:
        copy.wait()
    total = slots[0].astype(F32)[short : short + 1, :LANES]
    for z in range(1, zeros):
        total = total + slots[z].astype(F32)[short : short + 1, :LANES]
    tally[...] = jnp.broadcast_to(total, (8, LANES))
    tallies[place] = jnp.broadcast_to(total, (8, LANES))
    counting = spread("dp", replicas, lambda peer: tally, tallies, tsend, trecv)
    for z in range(zeros):
        block = slots[z].astype(F32)
        filters[:, z * cw : z * cw + half] = block[0:8]
        filters[:, z * cw + half : (z + 1) * cw] = block[8:16]
    load_feats.wait()
    load_cot.wait()

    group = lax.broadcasted_iota(jnp.int32, (1, LANES), 1) // gsize
    picks = [(group == i).astype(BF16) for i in range(per)]

    def convolve(n, begin):
        where = pl.ds(pl.multiple_of(n * width + begin, LANES), WIDE)
        x = feats[:, where]
        taps7 = filters[:, where]
        narrow = taps7.astype(BF16)
        scaled = jnp.concatenate([x * narrow[j : j + 1] for j in range(1, short)], 0)
        return taps7[0:1] * x.astype(F32) + dot(down_cat[...], scaled)

    span = crossing.shape[0] * LANES

    def blocks(step, carry):
        halves = []
        for sub in range(span // WIDE):
            begin = step * span + sub * WIDE
            parts = [convolve(n, begin) for n in range(3)]
            for h in range(WIDE // LANES):
                halves.append([p[:, h * LANES : (h + 1) * LANES] for p in parts])
        products, longs, chosens = [], [], []
        for h, (q, k, v) in enumerate(halves):
            product = (k * v).astype(BF16)
            products.append(product)
            block = step * (span // LANES) + h
            longs.append(dot(forward[block], jnp.concatenate([product * m for m in picks], 0)))
        for h, (q, k, v) in enumerate(halves):
            grad_out = cot[:, here(step, h, 0)].astype(F32) * living[...]
            grad_long = (grad_out * q).astype(BF16)
            chosens.append(grad_long)
            turned = lax.dot_general(
                products[h], flip[...], (((0,), (0,)), ((), ())), preferred_element_type=F32
            ).astype(BF16)
            for i in range(per):
                at = slice(i * gsize, (i + 1) * gsize)
                crossing[h, at, i * length : (i + 1) * length] = turned[at]
        for h, (q, k, v) in enumerate(halves):
            block = step * (span // LANES) + h
            grad_product = dot(
                backward[block], jnp.concatenate([chosens[h] * m for m in picks], 0)
            )
            grad_short[:, here(step, h, 1)] = (grad_product * v).astype(BF16)
            grad_short[:, here(step, h, 2)] = (grad_product * k).astype(BF16)
        for h, (q, k, v) in enumerate(halves):
            alive = living[...]
            mixed[:, here(step, h, 0)] = (alive * q * longs[h]).astype(BF16)
            grad_out = cot[:, here(step, h, 0)].astype(F32) * alive
            grad_short[:, here(step, h, 0)] = (grad_out * longs[h]).astype(BF16)
        for h in range(len(halves)):
            block = step * (span // LANES) + h
            crossed = dot(chosens[h], crossing[h])
            for i in range(per):
                part = crossed[:, i * length : (i + 1) * length] * causal_r[...]
                summed = part[0:8]
                for at in range(8, length, 8):
                    summed = summed + pltpu.roll(part[at : at + 8], at, 1)
                med[pl.ds(pl.multiple_of((block * per + i) * 8, 8), 8), :] = summed
        return carry

    def here(step, h, n):
        return pl.ds(pl.multiple_of(n * width + step * span + h * LANES, LANES), LANES)

    lax.fori_loop(0, width // span, blocks, 0)
    save_mixed = pltpu.make_async_copy(mixed, mixed_hbm, loaded.at[2])
    save_mixed.start()

    for copy in counting:
        copy.wait()
    total = tallies[0]
    for p in range(1, replicas):
        total = total + tallies[p]
    lane8 = lax.broadcasted_iota(jnp.int32, (8, LANES), 1)
    own = jnp.sum(jnp.where(lane8 == plan[0], total, 0.0), 1, keepdims=True)
    weight = (scale / own)[0:1]

    depth = taps.shape[0] // zeros
    total = None
    for a in range(8):
        part = pltpu.roll(med[pl.ds(a, taps.shape[1], stride=8), :], a + 1, 1)
        total = part if total is None else total + part
    medium = total.T * weight
    for z in range(zeros):
        mpack[z] = medium[z * depth : (z + 1) * depth].astype(BF16)
    mslots[mine] = mpack[mine]
    medium_one = spread("zero", zeros, lambda peer: mpack.at[peer], mslots, m1s, m1r)

    def short_chunk(owner):
        sums = []
        for s in range(cw // WIDE):
            where = pl.ds(pl.multiple_of(owner * cw + s * WIDE, LANES), WIDE)
            x = feats[:, where]
            grad = grad_short[:, where].astype(F32)
            lines = [jnp.sum(grad * x.astype(F32), 0, keepdims=True)]
            for j in range(1, short):
                lines.append(jnp.sum(grad * dot(down[j], x), 0, keepdims=True))
            lines.append(jnp.zeros((8 - short, WIDE), F32))
            sums.append(jnp.concatenate(lines, 0))
        both = jnp.concatenate(sums, 1) * weight
        return jnp.concatenate([both[:, :half], both[:, half:]], 0).astype(BF16)

    def short_copy(step):
        peer = lax.rem(mine + step, zeros)
        return pltpu.make_async_remote_copy(
            src_ref=spack.at[peer],
            dst_ref=sslots.at[mine],
            send_sem=s1s.at[step],
            recv_sem=s1r.at[step],
            device_id={"zero": peer},
            device_id_type=MESH,
        )

    def send_short(step, carry):
        peer = lax.rem(mine + step, zeros)
        spack[peer] = short_chunk(peer)
        short_copy(step).start()
        return carry

    lax.fori_loop(1, zeros // 2 + 1, send_short, 0)
    for copy in medium_one:
        copy.wait()
    total = mslots[0].astype(F32)
    for z in range(1, zeros):
        total = total + mslots[z].astype(F32)
    mpart[...] = total
    mparts[place] = total
    medium_two = spread("dp", replicas, lambda peer: mpart, mparts, m2s, m2r)
    lax.fori_loop(zeros // 2 + 1, zeros, send_short, 0)
    sslots[mine] = short_chunk(mine)
    for copy in medium_two:
        copy.wait()
    total = mparts[0]
    for p in range(1, replicas):
        total = total + mparts[p]
    share[...] = total
    shares[mine] = total
    medium_three = spread("zero", zeros, lambda peer: share, shares, m3s, m3r)

    bundle = 12

    def feats_chunk(index, carry):
        for sub in range(bundle):
            where = pl.ds(pl.multiple_of((index * bundle + sub) * WIDE, LANES), WIDE)
            grad = grad_short[:, where]
            taps7 = filters[:, where]
            narrow = taps7.astype(BF16)
            scaled = jnp.concatenate([grad * narrow[j : j + 1] for j in range(1, short)], 0)
            total = taps7[0:1] * grad.astype(F32) + dot(up_cat[...], scaled)
            grads[:, where] = (total * weight).astype(BF16)
        return carry

    pieces = 3 * width // WIDE // bundle
    middle = pieces // 2 * bundle * WIDE
    lax.fori_loop(0, pieces // 2, feats_chunk, 0)
    cols = slice(0, middle)
    save_one = pltpu.make_async_copy(grads.at[:, cols], grads_hbm.at[:, cols], loaded.at[3])
    save_one.start()

    for step in range(1, zeros):
        short_copy(step).wait()
    total = sslots[0].astype(F32)
    for z in range(1, zeros):
        total = total + sslots[z].astype(F32)
    spart[...] = total
    sparts[place] = total
    short_two = spread("dp", replicas, lambda peer: spart, sparts, s2s, s2r)

    lax.fori_loop(pieces // 2, pieces, feats_chunk, 0)
    cols = slice(middle, 3 * width)
    save_two = pltpu.make_async_copy(grads.at[:, cols], grads_hbm.at[:, cols], loaded.at[4])
    save_two.start()

    for copy in short_two:
        copy.wait()
    total = sparts[0]
    for p in range(1, replicas):
        total = total + sparts[p]
    short_out[:, :half] = total[0:short]
    short_out[:, half:] = total[8 : 8 + short]
    for copy in medium_three:
        copy.wait()
    for z in range(zeros):
        medium_out[z * depth : (z + 1) * depth, :] = shares[z]
    save_mixed.wait()
    save_one.wait()
    save_two.wait()


def run_whole(feats, short_filter, medium_filter, doc_ids, counts, plan, cotangent, replicas, zeros, scale):
    length, width = cotangent.shape
    short, cw = short_filter.shape
    half = cw // 2
    taps_count, groups = medium_filter.shape
    depth = taps_count // zeros
    square = (length, length)
    gsize = width // groups
    in_vmem = pl.BlockSpec(memory_space=pltpu.VMEM)
    in_smem = pl.BlockSpec(memory_space=pltpu.SMEM)
    anywhere = pl.BlockSpec(memory_space=pl.ANY)
    stacked = (width // LANES, length, LANES // gsize * length)
    along_zero, along_dp = pltpu.SemaphoreType.DMA((zeros,)), pltpu.SemaphoreType.DMA((replicas,))
    return pl.pallas_call(
        functools.partial(whole_kernel, replicas, zeros, scale, short, gsize),
        in_specs=[in_smem, in_smem, in_vmem, in_vmem, in_vmem, anywhere, anywhere],
        out_specs=[anywhere, anywhere, in_vmem, in_vmem],
        out_shape=[
            jax.ShapeDtypeStruct((length, width), BF16),
            jax.ShapeDtypeStruct(feats.shape, BF16),
            jax.ShapeDtypeStruct((short, cw), F32),
            jax.ShapeDtypeStruct((taps_count, groups), F32),
        ],
        scratch_shapes=[
            pltpu.VMEM((length, width), BF16),
            pltpu.VMEM(feats.shape, BF16),
            pltpu.VMEM(feats.shape, BF16),
            pltpu.VMEM((length, width), BF16),
            pltpu.SemaphoreType.DMA((5,)),
            pltpu.VMEM((8, cw), F32),
            pltpu.VMEM((16, half), BF16),
            pltpu.VMEM((zeros, 16, half), BF16),
            pltpu.VMEM((8, LANES), F32),
            pltpu.VMEM((replicas, 8, LANES), F32),
            pltpu.VMEM((8, 3 * width), F32),
            pltpu.VMEM((short, length, length), BF16),
            pltpu.VMEM((length, (short - 1) * length), BF16),
            pltpu.VMEM((length, (short - 1) * length), BF16),
            pltpu.VMEM(square, BF16),
            pltpu.VMEM(square, BF16),
            pltpu.VMEM(square, F32),
            pltpu.VMEM(square, BF16),
            pltpu.VMEM((8 * groups, taps_count), F32),
            pltpu.VMEM((8 * groups, taps_count), F32),
            pltpu.VMEM((length, LANES), F32),
            pltpu.VMEM((8 * groups, taps_count), F32),
            pltpu.VMEM(stacked, BF16),
            pltpu.VMEM(stacked, BF16),
            pltpu.VMEM(feats.shape, BF16),
            pltpu.VMEM((2 * WIDE // LANES, LANES, LANES // gsize * length), BF16),
            pltpu.VMEM((zeros, depth, groups), BF16),
            pltpu.VMEM((zeros, depth, groups), BF16),
            pltpu.VMEM((depth, groups), F32),
            pltpu.VMEM((replicas, depth, groups), F32),
            pltpu.VMEM((depth, groups), F32),
            pltpu.VMEM((zeros, depth, groups), F32),
            pltpu.VMEM((zeros, 16, half), BF16),
            pltpu.VMEM((zeros, 16, half), BF16),
            pltpu.VMEM((16, half), F32),
            pltpu.VMEM((replicas, 16, half), F32),
            along_zero, along_zero, along_dp, along_dp,
            along_zero, along_zero, along_dp, along_dp, along_zero, along_zero,
            along_zero, along_zero, along_dp, along_dp,
        ],
        compiler_params=pltpu.CompilerParams(
            collective_id=0, has_side_effects=True, vmem_limit_bytes=56 * 1024 * 1024
        ),
        name="whole_block",
    )(counts, plan, doc_ids, medium_filter, short_filter, feats, cotangent)


def hand_kernel(count, *refs):
    sources, targets = refs[:count], refs[count : 2 * count]
    held, came, left = refs[2 * count : 3 * count], refs[3 * count], refs[3 * count + 1]
    arriving, leaving = [], []
    for n in range(count):
        rows = sources[n].shape[0]
        cuts = 4 if rows % 64 == 0 and n < 2 else 1
        for cut in range(cuts):
            part = pl.ds(cut * rows // cuts, rows // cuts)
            slot, at = held[n].at[part], len(arriving)
            arriving.append(pltpu.make_async_copy(sources[n].at[part], slot, came.at[at]))
            leaving.append(pltpu.make_async_copy(slot, targets[n].at[part], left.at[at]))
    for copy in arriving:
        copy.start()
    for copy, onward in zip(arriving, leaving):
        copy.wait()
        onward.start()
    for copy in leaving:
        copy.wait()


def hand_over(arrays):
    anywhere = pl.BlockSpec(memory_space=pl.ANY)
    return pl.pallas_call(
        functools.partial(hand_kernel, len(arrays)),
        in_specs=[anywhere] * len(arrays),
        out_specs=[anywhere] * len(arrays),
        out_shape=[jax.ShapeDtypeStruct(a.shape, a.dtype) for a in arrays],
        scratch_shapes=[pltpu.VMEM(a.shape, a.dtype) for a in arrays]
        + [pltpu.SemaphoreType.DMA((4 * len(arrays),))] * 2,
        compiler_params=pltpu.CompilerParams(vmem_limit_bytes=56 * 1024 * 1024),
        name="hand_over",
    )(*arrays)


def shards(feats, short_filter, medium_filter, doc_ids, counts, plan, cotangent):
    replicas = lax.axis_size("dp")
    zeros = lax.axis_size("zero")
    length = feats.shape[0]
    short, cw = short_filter.shape
    scale = float(length * replicas * zeros / replicas)
    packed = cw % WIDE == 0 and medium_filter.shape[0] == 16 * zeros
    if packed:
        return hand_over(run_whole(
            feats, short_filter, medium_filter, doc_ids, counts, plan, cotangent, replicas, zeros, scale
        ))
    member = (plan[0] == jnp.arange(replicas)).astype(F32)
    totals = lax.psum(member * counts[0].astype(F32), ("dp", "zero"))
    weight = jnp.broadcast_to(scale / jnp.sum(member * totals), (8, LANES))
    filters = lax.all_gather(short_filter, "zero", axis=1, tiled=True).astype(F32)
    filters = jnp.pad(filters, ((0, 8 - short), (0, 0)))
    mixed, grads, shorts, medium = run_block(
        feats, filters, medium_filter, doc_ids, counts, weight, cotangent, short
    )
    own = lax.psum(shorts[:short], "dp")
    own = own.reshape(short, zeros, cw).transpose(1, 0, 2)
    short_grad = lax.psum_scatter(own, "zero", scatter_dimension=0, tiled=True)[0]
    medium_grad = lax.psum(medium, ("dp", "zero"))
    return mixed, grads, short_grad, medium_grad


def solution(mesh):
    in_specs = (
        P(("dp", "zero"), None),
        P(None, "zero"),
        P(),
        P(("dp", "zero"), None),
        P(("dp", "zero")),
        P(("dp", "zero")),
        P(("dp", "zero"), None),
    )
    out_specs = (P(("dp", "zero"), None), P(("dp", "zero"), None), P(None, "zero"), P())
    return jax.shard_map(shards, mesh=mesh, in_specs=in_specs, out_specs=out_specs, check_vma=False)
```

```python
import functools

import jax
import jax.numpy as jnp
from jax import lax
from jax.experimental import pallas as pl
from jax.experimental.pallas import tpu as pltpu
from jax.sharding import PartitionSpec as P

F32 = jnp.float32
BF16 = jnp.bfloat16
MESH = pl.DeviceIdType.MESH
LANES = 128
WIDE = 256


def greet(replicas, zeros):
    barrier = pltpu.get_barrier_semaphore()
    mine, row = lax.axis_index("zero"), lax.axis_index("dp")
    for step in range(1, zeros):
        peer = lax.rem(mine + step, zeros)
        pl.semaphore_signal(barrier, inc=1, device_id={"zero": peer}, device_id_type=MESH)
    for step in range(1, replicas):
        peer = lax.rem(row + step, replicas)
        pl.semaphore_signal(barrier, inc=1, device_id={"dp": peer}, device_id_type=MESH)
    return barrier


def spread(axis, count, source, slots, send, recv):
    me = lax.axis_index(axis)
    copies = []
    for step in range(1, count):
        peer = lax.rem(me + step, count)
        copy = pltpu.make_async_remote_copy(
            src_ref=source(peer),
            dst_ref=slots.at[me],
            send_sem=send.at[step],
            recv_sem=recv.at[step],
            device_id={axis: peer},
            device_id_type=MESH,
        )
        copy.start()
        copies.append(copy)
    return copies


def dot(a, b):
    return jnp.dot(a, b, preferred_element_type=F32)


def block_kernel(
    short, gsize, counts, doc, taps, weight, cot, fq, fk, fv, wq, wk, wv,
    mixed, grads, shorts, medium,
    down, up, causal, causal_t, causal_r, flip, tap_rows, tap_back, living, med,
):
    step = pl.program_id(0)
    length = cot.shape[0]
    width = grads.shape[1] // 3
    per = LANES // gsize
    square = (length, length)

    @pl.when(step == 0)
    def _():
        r = lax.broadcasted_iota(jnp.int32, square, 0)
        c = lax.broadcasted_iota(jnp.int32, square, 1)
        across = jnp.broadcast_to(doc[...].astype(F32), square)
        same = (across == across.T).astype(F32)
        for j in range(short):
            down[j] = jnp.where(r - c == j, same, 0.0).astype(BF16)
            up[j] = jnp.where(c - r == j, same, 0.0).astype(BF16)
        low = jnp.where(r >= c, same, 0.0)
        causal[...] = low
        causal_t[...] = jnp.where(c >= r, same, 0.0)
        turned = (r + c == length - 1).astype(BF16)
        flip[...] = turned
        causal_r[...] = dot(low.astype(BF16), turned)
        rounded = taps[...].astype(BF16).astype(F32).T
        tap_rows[...] = rounded
        back = (lax.rem(r + c, length) == 0).astype(BF16)
        tap_back[...] = dot(rounded.astype(BF16), back)
        living[...] = (r < counts[0]).astype(F32)

    def convolve(feats, filt):
        x = feats[...]
        total = filt[0:1, :] * x.astype(F32)
        for j in range(1, short):
            total = total + filt[j : j + 1, :] * dot(down[j], x)
        return total

    query, key, value = convolve(fq, wq), convolve(fk, wk), convolve(fv, wv)
    lane = lax.broadcasted_iota(jnp.int32, (1, LANES), 1)
    picks = [(lane // gsize == i).astype(BF16) for i in range(per)]
    weighting = weight[0:1, :]
    pieces = [[], [], []]
    for h in range(cot.shape[1] // LANES):
        cols = slice(h * LANES, (h + 1) * LANES)
        q, k, v = query[:, cols], key[:, cols], value[:, cols]
        product = (k * v).astype(BF16)
        first = step * (cot.shape[1] // gsize) + h * per
        forward, backward = [], []
        for i in range(per):
            row = jnp.broadcast_to(tap_back[pl.ds(first + i, 1), :], square)
            row = pltpu.roll(row, 0, 1, stride=1, stride_axis=0)
            forward.append((row * causal[...]).astype(BF16))
            row = jnp.broadcast_to(tap_rows[pl.ds(first + i, 1), :], square)
            row = pltpu.roll(row, 0, 1, stride=1, stride_axis=0)
            backward.append((row * causal_t[...]).astype(BF16))
        long_conv = dot(
            jnp.concatenate(forward, 1), jnp.concatenate([product * m for m in picks], 0)
        )
        alive = living[...]
        mixed[:, cols] = (alive * q * long_conv).astype(BF16)
        grad_out = cot[:, cols].astype(F32) * alive * weighting
        grad_long = (grad_out * q).astype(BF16)
        chosen = jnp.concatenate([grad_long * m for m in picks], 0)
        grad_product = dot(jnp.concatenate(backward, 1), chosen)
        turned = dot(flip[...], product).astype(BF16)
        crossed = lax.dot_general(
            chosen, turned, (((1,), (1,)), ((), ())), preferred_element_type=F32
        )
        for i in range(per):
            part = crossed[i * length : (i + 1) * length] * causal_r[...]
            part = pltpu.roll(part, 1, 1, stride=1, stride_axis=0)
            med[pl.ds(first + i, 1), :] = jnp.sum(part, 0, keepdims=True)
        pieces[0].append((grad_out * long_conv).astype(BF16))
        pieces[1].append((grad_product * v).astype(BF16))
        pieces[2].append((grad_product * k).astype(BF16))

    span = cot.shape[1]
    for n, (feats, filt) in enumerate(((fq, wq), (fk, wk), (fv, wv))):
        grad = jnp.concatenate(pieces[n], 1)
        x = feats[...].astype(F32)
        where = pl.ds(pl.multiple_of(n * width + step * span, LANES), span)
        total = None
        for j in range(short):
            moved = grad.astype(F32) if j == 0 else dot(up[j], grad)
            term = filt[j : j + 1, :] * moved
            total = term if total is None else total + term
            shorts[j : j + 1, where] = jnp.sum(moved * x, 0, keepdims=True)
        shorts[short:8, where] = jnp.zeros((8 - short, span), F32)
        grads[:, where] = total.astype(BF16)

    @pl.when(step == pl.num_programs(0) - 1)
    def _():
        medium[...] = med[...].T


def run_block(feats, filters, medium_filter, doc_ids, counts, weight, cotangent, short):
    length, width = cotangent.shape
    taps_count, groups = medium_filter.shape
    steps = width // WIDE
    square = (length, length)

    def part(n):
        return pl.BlockSpec((length, WIDE), lambda i, n=n: (0, n * steps + i))

    def part8(n):
        return pl.BlockSpec((8, WIDE), lambda i, n=n: (0, n * steps + i))

    def whole(shape):
        return pl.BlockSpec(shape, lambda i: (0, 0))

    return pl.pallas_call(
        functools.partial(block_kernel, short, width // groups),
        grid=(steps,),
        in_specs=[
            pl.BlockSpec(memory_space=pltpu.SMEM),
            whole((1, length)),
            whole((taps_count, groups)),
            whole((8, LANES)),
            part(0), part(0), part(1), part(2), part8(0), part8(1), part8(2),
        ],
        out_specs=[part(0), whole(feats.shape), whole((8, 3 * width)), whole((taps_count, groups))],
        out_shape=[
            jax.ShapeDtypeStruct((length, width), BF16),
            jax.ShapeDtypeStruct(feats.shape, BF16),
            jax.ShapeDtypeStruct((8, 3 * width), F32),
            jax.ShapeDtypeStruct((taps_count, groups), F32),
        ],
        scratch_shapes=[
            pltpu.VMEM((short, length, length), BF16),
            pltpu.VMEM((short, length, length), BF16),
            pltpu.VMEM(square, F32),
            pltpu.VMEM(square, F32),
            pltpu.VMEM(square, F32),
            pltpu.VMEM(square, BF16),
            pltpu.VMEM((groups, taps_count), F32),
            pltpu.VMEM((groups, taps_count), F32),
            pltpu.VMEM((length, LANES), F32),
            pltpu.VMEM((groups, taps_count), F32),
        ],
        compiler_params=pltpu.CompilerParams(vmem_limit_bytes=40 * 1024 * 1024),
        name="conv_block",
    )(counts, doc_ids, medium_filter, weight, cotangent, feats, feats, feats, filters, filters, filters)


def toeplitz(tile, length):
    return jnp.concatenate([pltpu.roll(tile, at, 1) if at else tile for at in range(0, length, 8)], 0)


def whole_kernel(
    replicas, zeros, scale, short, gsize,
    counts, plan, doc, taps, filt, feats_hbm, cot_hbm,
    mixed_hbm, grads_hbm, short_out, medium_out,
    mixed, grads, feats, cot, loaded, rows, stage, slots, tally, tallies, filters,
    down, down_cat, up_cat, causal, causal_t, causal_r, flip, base_rows, base_back, living, med,
    forward, backward, grad_short, crossing,
    mpack, mslots, mpart, mparts, share, shares, spack, sslots, spart, sparts,
    send, recv, tsend, trecv, m1s, m1r, m2s, m2r, m3s, m3r, s1s, s1r, s2s, s2r,
):
    barrier = greet(replicas, zeros)
    mine, place = lax.axis_index("zero"), lax.axis_index("dp")
    length = cot.shape[0]
    width = cot.shape[1]
    cw = filt.shape[1]
    half = cw // 2
    per = LANES // gsize
    square = (length, length)
    load_feats = pltpu.make_async_copy(feats_hbm, feats, loaded.at[0])
    load_cot = pltpu.make_async_copy(cot_hbm, cot, loaded.at[1])
    load_feats.start()
    load_cot.start()

    lane = lax.broadcasted_iota(jnp.int32, (1, cw), 1)
    rows[0:short, :] = filt[...].astype(F32)
    rows[short:8, :] = jnp.where(lane == plan[0], counts[0].astype(F32), 0.0)
    staged = jnp.concatenate([rows[:, :half], rows[:, half:]], 0).astype(BF16)
    stage[...] = staged
    slots[mine] = staged
    pl.semaphore_wait(barrier, zeros + replicas - 2)
    gathering = spread("zero", zeros, lambda peer: stage, slots, send, recv)

    r = lax.broadcasted_iota(jnp.int32, square, 0)
    c = lax.broadcasted_iota(jnp.int32, square, 1)
    across = jnp.broadcast_to(doc[...].astype(F32), square)
    same = (across == across.T).astype(F32)
    for j in range(short):
        down[j] = jnp.where(r - c == j, same, 0.0).astype(BF16)
        if j:
            at = slice((j - 1) * length, j * length)
            down_cat[:, at] = down[j]
            up_cat[:, at] = jnp.where(c - r == j, same, 0.0).astype(BF16)
    low = jnp.where(r >= c, same, 0.0)
    causal[...] = low.astype(BF16)
    causal_t[...] = jnp.where(c >= r, same, 0.0).astype(BF16)
    turn = (r + c == length - 1).astype(BF16)
    flip[...] = turn
    causal_r[...] = dot(low.astype(BF16), turn)
    rounded = taps[...].astype(BF16).astype(F32).T
    tap_rows = rounded
    back = (lax.rem(r + c, length) == 0).astype(BF16)
    tap_back = dot(rounded.astype(BF16), back)
    living[...] = (r < counts[0]).astype(F32)

    for a in range(8):
        lines = pl.ds(a, taps.shape[1], stride=8)
        base_back[lines, :] = pltpu.roll(tap_back, a, 1)
        base_rows[lines, :] = pltpu.roll(tap_rows, a, 1)

    def build(pair, carry):
        for n in range(2 * per):
            block, i = pair * 2 + n // per, n % per
            at = slice(i * length, (i + 1) * length)
            tile = pl.ds(pl.multiple_of((pair * 2 * per + n) * 8, 8), 8)
            one = toeplitz(base_back[tile, :], length)
            forward[block, :, at] = one.astype(BF16) * causal[...]
            two = toeplitz(base_rows[tile, :], length)
            backward[block, :, at] = two.astype(BF16) * causal_t[...]
        return carry

    lax.fori_loop(0, width // (2 * LANES), build, 0)
    crossing[...] = jnp.zeros_like(crossing)

    for copy in gathering:
        copy.wait()
    total = slots[0].astype(F32)[short : short + 1, :LANES]
    for z in range(1, zeros):
        total = total + slots[z].astype(F32)[short : short + 1, :LANES]
    tally[...] = jnp.broadcast_to(total, (8, LANES))
    tallies[place] = jnp.broadcast_to(total, (8, LANES))
    counting = spread("dp", replicas, lambda peer: tally, tallies, tsend, trecv)
    for z in range(zeros):
        block = slots[z].astype(F32)
        filters[:, z * cw : z * cw + half] = block[0:8]
        filters[:, z * cw + half : (z + 1) * cw] = block[8:16]
    load_feats.wait()
    load_cot.wait()

    group = lax.broadcasted_iota(jnp.int32, (1, LANES), 1) // gsize
    picks = [(group == i).astype(BF16) for i in range(per)]

    def convolve(n, begin):
        where = pl.ds(pl.multiple_of(n * width + begin, LANES), WIDE)
        x = feats[:, where]
        taps7 = filters[:, where]
        narrow = taps7.astype(BF16)
        scaled = jnp.concatenate([x * narrow[j : j + 1] for j in range(1, short)], 0)
        return taps7[0:1] * x.astype(F32) + dot(down_cat[...], scaled)

    span = crossing.shape[0] * LANES

    def blocks(step, carry):
        halves = []
        for sub in range(span // WIDE):
            begin = step * span + sub * WIDE
            parts = [convolve(n, begin) for n in range(3)]
            for h in range(WIDE // LANES):
                halves.append([p[:, h * LANES : (h + 1) * LANES] for p in parts])
        products, longs, chosens = [], [], []
        for h, (q, k, v) in enumerate(halves):
            product = (k * v).astype(BF16)
            products.append(product)
            block = step * (span // LANES) + h
            longs.append(dot(forward[block], jnp.concatenate([product * m for m in picks], 0)))
        for h, (q, k, v) in enumerate(halves):
            grad_out = cot[:, here(step, h, 0)].astype(F32) * living[...]
            grad_long = (grad_out * q).astype(BF16)
            chosens.append(grad_long)
            turned = lax.dot_general(
                products[h], flip[...], (((0,), (0,)), ((), ())), preferred_element_type=F32
            ).astype(BF16)
            for i in range(per):
                at = slice(i * gsize, (i + 1) * gsize)
                crossing[h, at, i * length : (i + 1) * length] = turned[at]
        for h, (q, k, v) in enumerate(halves):
            block = step * (span // LANES) + h
            grad_product = dot(
                backward[block], jnp.concatenate([chosens[h] * m for m in picks], 0)
            )
            grad_short[:, here(step, h, 1)] = (grad_product * v).astype(BF16)
            grad_short[:, here(step, h, 2)] = (grad_product * k).astype(BF16)
        for h, (q, k, v) in enumerate(halves):
            alive = living[...]
            mixed[:, here(step, h, 0)] = (alive * q * longs[h]).astype(BF16)
            grad_out = cot[:, here(step, h, 0)].astype(F32) * alive
            grad_short[:, here(step, h, 0)] = (grad_out * longs[h]).astype(BF16)
        for h in range(len(halves)):
            block = step * (span // LANES) + h
            crossed = dot(chosens[h], crossing[h])
            for i in range(per):
                part = crossed[:, i * length : (i + 1) * length] * causal_r[...]
                summed = part[0:8]
                for at in range(8, length, 8):
                    summed = summed + pltpu.roll(part[at : at + 8], at, 1)
                med[pl.ds(pl.multiple_of((block * per + i) * 8, 8), 8), :] = summed
        return carry

    def here(step, h, n):
        return pl.ds(pl.multiple_of(n * width + step * span + h * LANES, LANES), LANES)

    lax.fori_loop(0, width // span, blocks, 0)
    save_mixed = pltpu.make_async_copy(mixed, mixed_hbm, loaded.at[2])
    save_mixed.start()

    for copy in counting:
        copy.wait()
    total = tallies[0]
    for p in range(1, replicas):
        total = total + tallies[p]
    lane8 = lax.broadcasted_iota(jnp.int32, (8, LANES), 1)
    own = jnp.sum(jnp.where(lane8 == plan[0], total, 0.0), 1, keepdims=True)
    weight = (scale / own)[0:1]

    depth = taps.shape[0] // zeros
    total = None
    for a in range(8):
        part = pltpu.roll(med[pl.ds(a, taps.shape[1], stride=8), :], a + 1, 1)
        total = part if total is None else total + part
    medium = total.T * weight
    for z in range(zeros):
        mpack[z] = medium[z * depth : (z + 1) * depth].astype(BF16)
    mslots[mine] = mpack[mine]
    medium_one = spread("zero", zeros, lambda peer: mpack.at[peer], mslots, m1s, m1r)

    def short_chunk(owner):
        sums = []
        for s in range(cw // WIDE):
            where = pl.ds(pl.multiple_of(owner * cw + s * WIDE, LANES), WIDE)
            x = feats[:, where]
            grad = grad_short[:, where].astype(F32)
            lines = [jnp.sum(grad * x.astype(F32), 0, keepdims=True)]
            for j in range(1, short):
                lines.append(jnp.sum(grad * dot(down[j], x), 0, keepdims=True))
            lines.append(jnp.zeros((8 - short, WIDE), F32))
            sums.append(jnp.concatenate(lines, 0))
        both = jnp.concatenate(sums, 1) * weight
        return jnp.concatenate([both[:, :half], both[:, half:]], 0).astype(BF16)

    def short_copy(step):
        peer = lax.rem(mine + step, zeros)
        return pltpu.make_async_remote_copy(
            src_ref=spack.at[peer],
            dst_ref=sslots.at[mine],
            send_sem=s1s.at[step],
            recv_sem=s1r.at[step],
            device_id={"zero": peer},
            device_id_type=MESH,
        )

    def send_short(step, carry):
        peer = lax.rem(mine + step, zeros)
        spack[peer] = short_chunk(peer)
        short_copy(step).start()
        return carry

    lax.fori_loop(1, zeros // 2 + 1, send_short, 0)
    for copy in medium_one:
        copy.wait()
    total = mslots[0].astype(F32)
    for z in range(1, zeros):
        total = total + mslots[z].astype(F32)
    mpart[...] = total
    mparts[place] = total
    medium_two = spread("dp", replicas, lambda peer: mpart, mparts, m2s, m2r)
    lax.fori_loop(zeros // 2 + 1, zeros, send_short, 0)
    sslots[mine] = short_chunk(mine)
    for copy in medium_two:
        copy.wait()
    total = mparts[0]
    for p in range(1, replicas):
        total = total + mparts[p]
    share[...] = total
    shares[mine] = total
    medium_three = spread("zero", zeros, lambda peer: share, shares, m3s, m3r)

    bundle = 12

    def feats_chunk(index, carry):
        for sub in range(bundle):
            where = pl.ds(pl.multiple_of((index * bundle + sub) * WIDE, LANES), WIDE)
            grad = grad_short[:, where]
            taps7 = filters[:, where]
            narrow = taps7.astype(BF16)
            scaled = jnp.concatenate([grad * narrow[j : j + 1] for j in range(1, short)], 0)
            total = taps7[0:1] * grad.astype(F32) + dot(up_cat[...], scaled)
            grads[:, where] = (total * weight).astype(BF16)
        return carry

    pieces = 3 * width // WIDE // bundle
    middle = pieces // 2 * bundle * WIDE
    lax.fori_loop(0, pieces // 2, feats_chunk, 0)
    cols = slice(0, middle)
    save_one = pltpu.make_async_copy(grads.at[:, cols], grads_hbm.at[:, cols], loaded.at[3])
    save_one.start()

    for step in range(1, zeros):
        short_copy(step).wait()
    total = sslots[0].astype(F32)
    for z in range(1, zeros):
        total = total + sslots[z].astype(F32)
    spart[...] = total
    sparts[place] = total
    short_two = spread("dp", replicas, lambda peer: spart, sparts, s2s, s2r)

    lax.fori_loop(pieces // 2, pieces, feats_chunk, 0)
    cols = slice(middle, 3 * width)
    save_two = pltpu.make_async_copy(grads.at[:, cols], grads_hbm.at[:, cols], loaded.at[4])
    save_two.start()

    for copy in short_two:
        copy.wait()
    total = sparts[0]
    for p in range(1, replicas):
        total = total + sparts[p]
    short_out[:, :half] = total[0:short]
    short_out[:, half:] = total[8 : 8 + short]
    for copy in medium_three:
        copy.wait()
    for z in range(zeros):
        medium_out[z * depth : (z + 1) * depth, :] = shares[z]
    save_mixed.wait()
    save_one.wait()
    save_two.wait()


def run_whole(feats, short_filter, medium_filter, doc_ids, counts, plan, cotangent, replicas, zeros, scale):
    length, width = cotangent.shape
    short, cw = short_filter.shape
    half = cw // 2
    taps_count, groups = medium_filter.shape
    depth = taps_count // zeros
    square = (length, length)
    gsize = width // groups
    in_vmem = pl.BlockSpec(memory_space=pltpu.VMEM)
    in_smem = pl.BlockSpec(memory_space=pltpu.SMEM)
    anywhere = pl.BlockSpec(memory_space=pl.ANY)
    stacked = (width // LANES, length, LANES // gsize * length)
    along_zero, along_dp = pltpu.SemaphoreType.DMA((zeros,)), pltpu.SemaphoreType.DMA((replicas,))
    return pl.pallas_call(
        functools.partial(whole_kernel, replicas, zeros, scale, short, gsize),
        in_specs=[in_smem, in_smem, in_vmem, in_vmem, in_vmem, anywhere, anywhere],
        out_specs=[anywhere, anywhere, in_vmem, in_vmem],
        out_shape=[
            jax.ShapeDtypeStruct((length, width), BF16),
            jax.ShapeDtypeStruct(feats.shape, BF16),
            jax.ShapeDtypeStruct((short, cw), F32),
            jax.ShapeDtypeStruct((taps_count, groups), F32),
        ],
        scratch_shapes=[
            pltpu.VMEM((length, width), BF16),
            pltpu.VMEM(feats.shape, BF16),
            pltpu.VMEM(feats.shape, BF16),
            pltpu.VMEM((length, width), BF16),
            pltpu.SemaphoreType.DMA((5,)),
            pltpu.VMEM((8, cw), F32),
            pltpu.VMEM((16, half), BF16),
            pltpu.VMEM((zeros, 16, half), BF16),
            pltpu.VMEM((8, LANES), F32),
            pltpu.VMEM((replicas, 8, LANES), F32),
            pltpu.VMEM((8, 3 * width), F32),
            pltpu.VMEM((short, length, length), BF16),
            pltpu.VMEM((length, (short - 1) * length), BF16),
            pltpu.VMEM((length, (short - 1) * length), BF16),
            pltpu.VMEM(square, BF16),
            pltpu.VMEM(square, BF16),
            pltpu.VMEM(square, F32),
            pltpu.VMEM(square, BF16),
            pltpu.VMEM((8 * groups, taps_count), F32),
            pltpu.VMEM((8 * groups, taps_count), F32),
            pltpu.VMEM((length, LANES), F32),
            pltpu.VMEM((8 * groups, taps_count), F32),
            pltpu.VMEM(stacked, BF16),
            pltpu.VMEM(stacked, BF16),
            pltpu.VMEM(feats.shape, BF16),
            pltpu.VMEM((4 * WIDE // LANES, LANES, LANES // gsize * length), BF16),
            pltpu.VMEM((zeros, depth, groups), BF16),
            pltpu.VMEM((zeros, depth, groups), BF16),
            pltpu.VMEM((depth, groups), F32),
            pltpu.VMEM((replicas, depth, groups), F32),
            pltpu.VMEM((depth, groups), F32),
            pltpu.VMEM((zeros, depth, groups), F32),
            pltpu.VMEM((zeros, 16, half), BF16),
            pltpu.VMEM((zeros, 16, half), BF16),
            pltpu.VMEM((16, half), F32),
            pltpu.VMEM((replicas, 16, half), F32),
            along_zero, along_zero, along_dp, along_dp,
            along_zero, along_zero, along_dp, along_dp, along_zero, along_zero,
            along_zero, along_zero, along_dp, along_dp,
        ],
        compiler_params=pltpu.CompilerParams(
            collective_id=0, has_side_effects=True, vmem_limit_bytes=56 * 1024 * 1024
        ),
        name="whole_block",
    )(counts, plan, doc_ids, medium_filter, short_filter, feats, cotangent)


def hand_kernel(count, *refs):
    sources, targets = refs[:count], refs[count : 2 * count]
    held, came, left = refs[2 * count : 3 * count], refs[3 * count], refs[3 * count + 1]
    arriving, leaving = [], []
    for n in range(count):
        rows = sources[n].shape[0]
        cuts = 4 if rows % 64 == 0 and n < 2 else 1
        for cut in range(cuts):
            part = pl.ds(cut * rows // cuts, rows // cuts)
            slot, at = held[n].at[part], len(arriving)
            arriving.append(pltpu.make_async_copy(sources[n].at[part], slot, came.at[at]))
            leaving.append(pltpu.make_async_copy(slot, targets[n].at[part], left.at[at]))
    for copy in arriving:
        copy.start()
    for copy, onward in zip(arriving, leaving):
        copy.wait()
        onward.start()
    for copy in leaving:
        copy.wait()


def hand_over(arrays):
    anywhere = pl.BlockSpec(memory_space=pl.ANY)
    return pl.pallas_call(
        functools.partial(hand_kernel, len(arrays)),
        in_specs=[anywhere] * len(arrays),
        out_specs=[anywhere] * len(arrays),
        out_shape=[jax.ShapeDtypeStruct(a.shape, a.dtype) for a in arrays],
        scratch_shapes=[pltpu.VMEM(a.shape, a.dtype) for a in arrays]
        + [pltpu.SemaphoreType.DMA((4 * len(arrays),))] * 2,
        compiler_params=pltpu.CompilerParams(vmem_limit_bytes=56 * 1024 * 1024),
        name="hand_over",
    )(*arrays)


def shards(feats, short_filter, medium_filter, doc_ids, counts, plan, cotangent):
    replicas = lax.axis_size("dp")
    zeros = lax.axis_size("zero")
    length = feats.shape[0]
    short, cw = short_filter.shape
    scale = float(length * replicas * zeros / replicas)
    packed = cw % WIDE == 0 and medium_filter.shape[0] == 16 * zeros
    if packed:
        return hand_over(run_whole(
            feats, short_filter, medium_filter, doc_ids, counts, plan, cotangent, replicas, zeros, scale
        ))
    member = (plan[0] == jnp.arange(replicas)).astype(F32)
    totals = lax.psum(member * counts[0].astype(F32), ("dp", "zero"))
    weight = jnp.broadcast_to(scale / jnp.sum(member * totals), (8, LANES))
    filters = lax.all_gather(short_filter, "zero", axis=1, tiled=True).astype(F32)
    filters = jnp.pad(filters, ((0, 8 - short), (0, 0)))
    mixed, grads, shorts, medium = run_block(
        feats, filters, medium_filter, doc_ids, counts, weight, cotangent, short
    )
    own = lax.psum(shorts[:short], "dp")
    own = own.reshape(short, zeros, cw).transpose(1, 0, 2)
    short_grad = lax.psum_scatter(own, "zero", scatter_dimension=0, tiled=True)[0]
    medium_grad = lax.psum(medium, ("dp", "zero"))
    return mixed, grads, short_grad, medium_grad


def solution(mesh):
    in_specs = (
        P(("dp", "zero"), None),
        P(None, "zero"),
        P(),
        P(("dp", "zero"), None),
        P(("dp", "zero")),
        P(("dp", "zero")),
        P(("dp", "zero"), None),
    )
    out_specs = (P(("dp", "zero"), None), P(("dp", "zero"), None), P(None, "zero"), P())
    return jax.shard_map(shards, mesh=mesh, in_specs=in_specs, out_specs=out_specs, check_vma=False)
```
